512 devices in a mesh: region: 64 (over y, z), season: 8 (over x, core).
Axes of the slice: x: 4, y: 4, z: 16, core: 2. Of those that a mesh axis runs over, the one named last changes fastest.
Arguments:
- demand: float32 [4096, 1024], P('region', 'season'), may hold values from 0.3 to 5.1, as said below
- avail: bfloat16 [16384, 1024], P('region', 'season'), may hold values from 0 to 1
- asset_bus: int32 [16384], P('region'), may hold values from 0 to 63
- run_cost: float32 [16384], P('region'), may hold values from 0.1 to 2
- build_cost: float32 [16384], P('region'), may hold values from 0.05 to 0.5
- line_from: int32 [16384], P('region'), may hold values from 0 to 63
- line_to: int32 [16384], P('region'), may hold values from 0 to 63
- link_count: int32 [64, 64], P('region'), may hold values from 0 to 4, as said below
- line_limit: float32 [16384], P('region'), may hold values from 0.5 to 2
- efficiency: float32 [4096], P('region'), may hold values from 0.6 to 1
- power_limit: float32 [4096], P('region'), may hold values from 0.5 to 2
- energy_limit: float32 [4096], P('region'), may hold values from 1 to 4
- season_link: int32 [4096, 8], P('region', 'season'), may hold values 0 or 1
- dispatch: float32 [16384, 1024], P('region', 'season'), may hold values from 0 to 1
- capacity: float32 [16384], P('region'), may hold values from 0.5 to 2
- flow: float32 [16384, 1024], P('region', 'season'), may hold values from -3 to 3
- charge: float32 [4096, 1024], P('region', 'season'), may hold values from -3 to 3
- soc: float32 [4096, 1024], P('region', 'season'), may hold values from 0 to 1
- price: float32 [4096, 1024], P('region', 'season'), may hold values from -5 to 5
- scarcity: float32 [16384, 1024], P('region', 'season'), may hold values from 0 to 1
- soc_dual: float32 [4096, 1024], P('region', 'season'), may hold values from -3 to 3
Outputs:
- next_dispatch: float32 [16384, 1024], P('region', 'season')
- next_capacity: float32 [16384], P('region')
- next_flow: float32 [16384, 1024], P('region', 'season')
- next_charge: float32 [4096, 1024], P('region', 'season')
- next_soc: float32 [4096, 1024], P('region', 'season')
- next_price: float32 [4096, 1024], P('region', 'season')
- next_scarcity: float32 [16384, 1024], P('region', 'season')
- next_soc_dual: float32 [4096, 1024], P('region', 'season')
The draws below stay inside these ranges and needn't reach their ends.
Inputs may be any that keep to these rules, and one draw needn't show every extreme that they name: `link_count`: each row has at least one entry equal to 4. `demand`: positive.
All inputs are finite; a program needn't handle non-finite values. No bound on the sum of `season_link` on one device may be relied on, other than what follows from the above.
Results may differ from the reference program's by a relative error of at most 0.002.
Values may be sent and summed in bfloat16 or wider, within the bound.
No kernel may reach another device: no remote copies, remote signals or barrier semaphores. Data moves between devices by JAX's collectives and lax.ppermute only.
A program may use at most 64 MiB of HBM per device.

```python
import math
import jax
import jax.numpy as jnp
from jax import lax

BUS_DEV = 64
ASSET_DEV = 256
HRS_DEV = 128
LINK_CAP = 4
BUSES = 4096
ASSETS = 16384
HOURS = 1024
LINE_DEV = 256
LINES = 16384
N_REGION = 64
N_SEASON = 8


def draw_demand(key, part):
    key = jax.random.fold_in(key, 11)
    base = jax.random.uniform(key, (BUSES, HOURS), jnp.float32)
    owners = (jnp.arange(BUSES) // BUS_DEV).astype(jnp.float32)
    rising = 1.0 + 2.0 * owners / (N_REGION - 1)
    shaped = 0.5 + base
    return shaped * rising[:, None]


def draw_avail(key, part):
    key = jax.random.fold_in(key, 12)
    base = jax.random.uniform(key, (ASSETS, HOURS), jnp.float32)
    seasons = (jnp.arange(HOURS) // HRS_DEV).astype(jnp.float32)
    rising = (1.0 + 2.0 * seasons / (N_SEASON - 1)) / 3.0
    shaped = base
    return (shaped * rising[None, :]).astype(jnp.bfloat16)


def draw_link_count(key, part):
    key = jax.random.fold_in(key, 13)
    counts = jax.random.randint(key, (N_REGION, N_REGION), 0, LINK_CAP + 1)
    rows = jnp.arange(N_REGION)
    filled = jnp.arange(N_REGION)[None, :] == ((rows + 1) % N_REGION)[:, None]
    return jnp.where(filled, LINK_CAP, counts).astype(jnp.int32)


def set_ends(result, stream_key, low, largest):
    longest = result.shape.index(max(result.shape))
    spots = []
    for shift in (0, 1):
        where = [jax.random.randint(jax.random.fold_in(stream_key, axis), (), 0, length) for axis, length in enumerate(result.shape)]
        where[longest] = (where[longest] + shift) % result.shape[longest]
        spots.append(tuple(where))
    return result.at[spots[0]].set(low).at[spots[1]].set(largest)


def shard_levels(stream_key, extent, cuts, low, high):
    level = 1.0
    for axis_at, shards_of in cuts:
        steps = jax.random.uniform(jax.random.fold_in(jax.random.fold_in(stream_key, 6), axis_at), (shards_of,), jnp.float32, low / len(cuts), high / len(cuts))
        level = level * jnp.repeat(jnp.exp(steps), extent[axis_at] // shards_of).reshape((-1,) + (1,) * (len(extent) - 1 - axis_at))
    return level


def gaussian(key, extent, scale, most, cuts=(), kind=jnp.bfloat16):
    drawn = jax.random.normal(key, extent, jnp.float32) * scale
    if len(cuts) > 0:
        drawn = shard_levels(key, extent, cuts, -0.22, 0.18) * drawn
    return jnp.clip(drawn, min=-most, max=most).astype(kind)


def setup_inputs(seed: int = 0) -> dict:
    key_of = jax.random.split(jax.random.key(seed), 22)
    return {
        "demand": draw_demand(jax.random.fold_in(key_of[21], 71), 0),
        "avail": draw_avail(jax.random.fold_in(key_of[21], 71), 0),
        "asset_bus": set_ends(jax.random.randint(key_of[2], (ASSETS,), 0, BUS_DEV), jax.random.fold_in(key_of[2], 1), 0, BUS_DEV - 1).astype(jnp.int32),
        "run_cost": jnp.clip(jnp.exp(math.log(2.0) - 2.9957323 * jax.random.uniform(key_of[3], (ASSETS,), jnp.float32) ** shard_levels(key_of[3], (ASSETS,), ((0, 64),), -0.2, 0.2)), 0.1, 2.0),
        "build_cost": jnp.clip(jnp.exp(math.log(0.5) - 2.3025851 * jax.random.uniform(key_of[4], (ASSETS,), jnp.float32) ** shard_levels(key_of[4], (ASSETS,), ((0, 64),), -0.2, 0.2)), 0.05, 0.5),
        "line_from": set_ends(jax.random.randint(key_of[5], (LINES,), 0, BUS_DEV), jax.random.fold_in(key_of[5], 1), 0, BUS_DEV - 1).astype(jnp.int32),
        "line_to": set_ends(jax.random.randint(key_of[6], (LINES,), 0, BUS_DEV), jax.random.fold_in(key_of[6], 1), 0, BUS_DEV - 1).astype(jnp.int32),
        "link_count": draw_link_count(jax.random.fold_in(key_of[21], 71), 0),
        "line_limit": jnp.clip(jnp.exp(math.log(2.0) - 1.3862944 * jax.random.uniform(key_of[8], (LINES,), jnp.float32) ** shard_levels(key_of[8], (LINES,), ((0, 64),), -0.2, 0.2)), 0.5, 2.0),
        "efficiency": jnp.clip(0.6 + 0.39999998 * jax.random.uniform(key_of[9], (BUSES,), jnp.float32) ** shard_levels(key_of[9], (BUSES,), ((0, 64),), -0.2, 0.2), 0.6, 1.0),
        "power_limit": jnp.clip(jnp.exp(math.log(2.0) - 1.3862944 * jax.random.uniform(key_of[10], (BUSES,), jnp.float32) ** shard_levels(key_of[10], (BUSES,), ((0, 64),), -0.2, 0.2)), 0.5, 2.0),
        "energy_limit": jnp.clip(jnp.exp(math.log(4.0) - 1.3862944 * jax.random.uniform(key_of[11], (BUSES,), jnp.float32) ** shard_levels(key_of[11], (BUSES,), ((0, 64),), -0.2, 0.2)), 1.0, 4.0),
        "season_link": set_ends((jax.random.randint(key_of[12], (BUSES, N_SEASON), 0, 2) < 1).astype(jnp.int32), jax.random.fold_in(key_of[12], 1), 0, 1),
        "dispatch": jnp.clip(1.0 * jax.random.uniform(key_of[13], (ASSETS, HOURS), jnp.float32) ** shard_levels(key_of[13], (ASSETS, HOURS), ((0, 64), (1, 8)), -0.2, 0.2), 0.0, 1.0),
        "capacity": jnp.clip(0.5 + 1.5 * jax.random.uniform(key_of[14], (ASSETS,), jnp.float32) ** shard_levels(key_of[14], (ASSETS,), ((0, 64),), -0.2, 0.2), 0.5, 2.0),
        "flow": gaussian(key_of[15], (LINES, HOURS), 0.5, 3.0, ((0, 64), (1, 8)), jnp.float32),
        "charge": gaussian(key_of[16], (BUSES, HOURS), 0.5, 3.0, ((0, 64), (1, 8)), jnp.float32),
        "soc": jnp.clip(1.0 * jax.random.uniform(key_of[17], (BUSES, HOURS), jnp.float32) ** shard_levels(key_of[17], (BUSES, HOURS), ((0, 64), (1, 8)), -0.2, 0.2), 0.0, 1.0),
        "price": gaussian(key_of[18], (BUSES, HOURS), 1.0, 5.0, ((0, 64), (1, 8)), jnp.float32),
        "scarcity": jnp.clip(1.0 * jax.random.uniform(key_of[19], (ASSETS, HOURS), jnp.float32) ** shard_levels(key_of[19], (ASSETS, HOURS), ((0, 64), (1, 8)), -0.2, 0.2), 0.0, 1.0),
        "soc_dual": gaussian(key_of[20], (BUSES, HOURS), 0.5, 3.0, ((0, 64), (1, 8)), jnp.float32),
    }


step_size = 0.2

def reference(demand, avail, asset_bus, run_cost, build_cost, line_from, line_to, link_count, line_limit, efficiency, power_limit, energy_limit, season_link, dispatch, capacity, flow, charge, soc, price, scarcity, soc_dual):
    asset_owner = jnp.arange(ASSETS, dtype=jnp.int32) // ASSET_DEV
    asset_global = asset_owner * BUS_DEV + asset_bus
    line_index = jnp.arange(LINES, dtype=jnp.int32)
    line_owner = line_index // LINE_DEV
    line_target = line_index % LINE_DEV // LINK_CAP
    line_live = (line_index % LINK_CAP < link_count[line_owner, line_target]).astype(jnp.float32)
    from_global = line_owner * BUS_DEV + line_from
    to_global = line_target * BUS_DEV + line_to
    limit_live = (line_limit * line_live)[:, None]
    avail_full = avail.astype(jnp.float32)
    link_float = season_link.astype(jnp.float32)
    decay = efficiency[:, None, None]

    def adjoint_apply(price_b, scarcity_b, dual_b):
        price_f = price_b.astype(jnp.float32)
        scarcity_f = scarcity_b.astype(jnp.float32)
        dual_f = dual_b.astype(jnp.float32)
        grad_dispatch = price_f[asset_global] - scarcity_f
        grad_build = lax.optimization_barrier(jnp.sum(avail_full * scarcity_f, axis=1)) / HOURS
        grad_flow = price_f[to_global] - price_f[from_global]
        grad_charge = price_f + dual_f
        dual_cube = dual_f.reshape(BUSES, N_SEASON, HRS_DEV)
        first_hour = dual_cube[:, :, 0]
        after_last = (1.0 - link_float) * first_hour + jnp.roll(link_float * first_hour, -1, axis=1)
        following = jnp.concatenate([dual_cube[:, :, 1:], after_last[:, :, None]], axis=2)
        grad_soc = (dual_cube - decay * following).reshape(BUSES, HOURS)
        return (grad_dispatch, grad_build, grad_flow, grad_charge, grad_soc)

    def forward_apply(dispatch_b, build_b, flow_b, charge_b, soc_b):
        dispatch_f = dispatch_b.astype(jnp.float32)
        flow_f = flow_b.astype(jnp.float32)
        charge_f = charge_b.astype(jnp.float32)
        soc_f = soc_b.astype(jnp.float32)
        generated = jax.ops.segment_sum(dispatch_f, asset_global, num_segments=BUSES)
        arriving = jax.ops.segment_sum(flow_f, to_global, num_segments=BUSES)
        leaving = jax.ops.segment_sum(flow_f, from_global, num_segments=BUSES)
        balance_rows = generated + charge_f + arriving - leaving
        avail_rows = avail_full * build_b.astype(jnp.float32)[:, None] - dispatch_f
        soc_cube = soc_f.reshape(BUSES, N_SEASON, HRS_DEV)
        last_hour = soc_cube[:, :, -1]
        carried = jnp.where(season_link == 1, jnp.roll(last_hour, 1, axis=1), last_hour)
        previous = jnp.concatenate([carried[:, :, None], soc_cube[:, :, :-1]], axis=2)
        soc_rows = (soc_cube - decay * previous).reshape(BUSES, HOURS) + charge_f
        return (balance_rows, avail_rows, soc_rows)

    def extrapolate(newer, older):
        return (2.0 * newer - older).astype(jnp.bfloat16)

    def primal_dual(state, tau, sigma):
        disp, build, flows, disch, level, duals, scarce, sdual = state
        grad_dispatch, grad_build, grad_flow, grad_charge, grad_soc = adjoint_apply(duals.astype(jnp.bfloat16), scarce.astype(jnp.bfloat16), sdual.astype(jnp.bfloat16))
        disp_new = jnp.maximum(disp - tau * (run_cost[:, None] - grad_dispatch), 0.0)
        build_new = jnp.maximum(build - tau * (build_cost - grad_build), 0.0)
        flows_new = jnp.clip(flows + tau * grad_flow, -limit_live, limit_live)
        disch_new = jnp.clip(disch + tau * grad_charge, -power_limit[:, None], power_limit[:, None])
        level_new = jnp.clip(level + tau * grad_soc, 0.0, energy_limit[:, None])
        balance_rows, avail_rows, soc_rows = forward_apply(extrapolate(disp_new, disp), extrapolate(build_new, build), extrapolate(flows_new, flows), extrapolate(disch_new, disch), extrapolate(level_new, level))
        duals_new = duals + sigma * (demand - balance_rows)
        scarce_new = jnp.maximum(scarce - sigma * avail_rows, 0.0)
        sdual_new = sdual - sigma * soc_rows
        return (disp_new, build_new, flows_new, disch_new, level_new, duals_new, scarce_new, sdual_new)

    def halpern(state, tau, sigma):
        mapped = primal_dual(state, tau, sigma)
        return tuple((0.5 * (newer + older) for newer, older in zip(mapped, state)))
    start = (dispatch, capacity, flow * line_live[:, None], charge, soc, price, scarcity, soc_dual)
    half = halpern(start, step_size, step_size)
    moves = [jnp.sum((newer - older) * (newer - older)) for newer, older in zip(half, start)]
    primal_move = moves[0] + moves[1] + moves[2] + moves[3] + moves[4]
    dual_move = moves[5] + moves[6] + moves[7]
    weight = jnp.sqrt(jnp.sqrt((dual_move + 1e-06) / (primal_move + 1e-06)))
    final = halpern(half, step_size / weight, step_size * weight)
    return (final[0], final[1], final[2], final[3], final[4], final[5], final[6], final[7])
```

```python
import jax
import jax.numpy as jnp
from jax import lax
from jax.experimental import pallas as pl
from jax.experimental.pallas import tpu as pltpu
from jax.sharding import PartitionSpec as P

LINK_CAP = 4
PACK = 3 * LINK_CAP
GROUP = 16
step_size = 0.2
F32 = jnp.float32
BF16 = jnp.bfloat16
I32 = jnp.int32
REGIONS, SEASONS = 64, 8
BUS, SLOT, HOUR = 64, 256, 128
PACKED = GROUP * PACK
UNPACKED = 2 * GROUP * LINK_CAP + GROUP


def iota(shape, axis):
    return lax.broadcasted_iota(I32, shape, axis)


def dot(a, b):
    return jnp.dot(a, b, preferred_element_type=F32)


def dot_t(a, b):
    return lax.dot_general(a, b, (((0,), (0,)), ((), ())), preferred_element_type=F32)


def as_bf(mask):
    return jnp.where(mask, 1.0, 0.0).astype(BF16)


def narrow(value):
    return value.astype(BF16)


def wide(value):
    return value.astype(F32)


def extrapolate(newer, older):
    return narrow(2.0 * newer - older)


def mean(newer, older):
    return 0.5 * (newer + older)


def total(value):
    return jnp.sum(jnp.sum(value, axis=1, keepdims=True), axis=0, keepdims=True)


def square(newer, older):
    moved = newer - older
    return total(moved * moved)


def row256(ref):
    return jnp.concatenate([ref[0:1, :], ref[1:2, :]], axis=1)


def pack_target(packed):
    q = lax.shift_right_logical(packed * 171, 11)
    j = packed - PACK * q
    first = LINK_CAP * q + j
    second = GROUP * LINK_CAP + LINK_CAP * q + j - LINK_CAP
    third = 2 * GROUP * LINK_CAP + q
    return jnp.where(
        j < LINK_CAP,
        first,
        jnp.where(j < 2 * LINK_CAP, second, jnp.where(j == 2 * LINK_CAP, third, -1)),
    )


def pack(first, second, third, out_ref):
    shape = (PACKED, UNPACKED)
    place = as_bf(pack_target(iota(shape, 0)) == iota(shape, 1))
    lines = GROUP * LINK_CAP
    for g in range(REGIONS // GROUP):
        rows = jnp.concatenate(
            [
                first[g * lines : (g + 1) * lines],
                second[g * lines : (g + 1) * lines],
                third[g * GROUP : (g + 1) * GROUP],
            ],
            axis=0,
        )
        out_ref[g * PACKED : (g + 1) * PACKED, :] = narrow(dot(place, rows))


def unpack(ref):
    shape = (UNPACKED, PACKED)
    place = as_bf(pack_target(iota(shape, 1)) == iota(shape, 0))
    parts = [
        dot(place, ref[g * PACKED : (g + 1) * PACKED, :]) for g in range(REGIONS // GROUP)
    ]
    lines = GROUP * LINK_CAP
    first = jnp.concatenate([p[:lines] for p in parts], axis=0)
    second = jnp.concatenate([p[lines : 2 * lines] for p in parts], axis=0)
    third = jnp.concatenate([p[2 * lines :] for p in parts], axis=0)
    return first, second, third


def columns(ref):
    return jnp.transpose(ref[...])


def long_column(turned, at):
    return jnp.concatenate([turned[:, at : at + 1], turned[:, at + 1 : at + 2]], axis=0)


def onehot_rows(column, count):
    return as_bf(column == wide(iota((SLOT, count), 1)))


def lines_out(
    flow, price, line_from, line_to, line_limit, link_count,
    sent, flow0, near0, cap, leave, turn,
):
    lane = iota((1, SLOT), 1)
    spread = as_bf(iota((REGIONS, SLOT), 0) == lax.shift_right_logical(iota((REGIONS, SLOT), 1), 2))
    counts = jnp.broadcast_to(narrow(wide(link_count[...])), (8, REGIONS))
    counts = dot(counts, spread)[0:1]
    live = jnp.where(wide(lane & (LINK_CAP - 1)) < counts, 1.0, 0.0)
    limit = row256(line_limit) * live
    turn[0:2, :] = wide(line_from[...])
    turn[2:3, :] = live[:, :128]
    turn[3:4, :] = live[:, 128:]
    turn[4:5, :] = limit[:, :128]
    turn[5:6, :] = limit[:, 128:]
    turned = columns(turn)
    leave_t = onehot_rows(long_column(turned, 0), BUS)
    f0 = flow[...] * long_column(turned, 2)
    near = narrow(dot(leave_t, narrow(price[...])))
    flow0[...] = f0
    near0[...] = near
    cap[...] = jnp.broadcast_to(long_column(turned, 4), (SLOT, HOUR))
    leave[...] = leave_t
    high = wide(narrow(limit))
    low = limit - high
    held = jnp.zeros((REGIONS, 128), F32)
    slot_kind = iota((SLOT, 128), 0) & (LINK_CAP - 1)
    for at, value in enumerate((wide(row256(line_to)), high, low)):
        spots = as_bf(iota((SLOT, 128), 1) == slot_kind + LINK_CAP * at)
        held = held + dot(spread * narrow(value), spots)
    pack(narrow(f0), near, narrow(held), sent)


def season_block(sums, level, dual_f, link_column, sent, move_row=None):
    lane = iota((128, 128), 1)
    tail = jnp.concatenate([level[:, HOUR - 1 : HOUR], dual_f[:, HOUR - 1 : HOUR]], axis=0)
    head = jnp.concatenate([dual_f[:, 0:1], link_column], axis=0)
    held = jnp.where(
        lane == 0,
        sums[:128],
        jnp.where(lane == 1, sums[128:], jnp.where(lane == 2, tail, jnp.where(lane == 3, head, 0.0))),
    )
    return jnp.transpose(held)[0:8]


def season_out(avail, scarcity, soc, soc_dual, link, sent, turn):
    turn[0:1, 0:BUS] = wide(link[...])
    turned = columns(turn)
    sums = jnp.sum(wide(avail[...]) * wide(narrow(scarcity[...])), axis=1, keepdims=True)
    rows = season_block(sums, soc[...], wide(narrow(soc_dual[...])), turned[:BUS, 0:1], sent)
    for s in range(SEASONS):
        sent[s] = rows


def ends_in(got, price, sent, arrive, cap):
    _, _, held = unpack(got)
    shape = (SLOT, REGIONS)
    spread = as_bf(iota(shape, 1) == lax.shift_right_logical(iota(shape, 0), 2))
    lines = dot(spread, narrow(held))
    lane = iota((SLOT, 128), 1)
    kind = iota((SLOT, 128), 0) & (LINK_CAP - 1)
    ends = jnp.sum(jnp.where(lane == kind, lines, 0.0), axis=1, keepdims=True)
    limits = (lane == kind + LINK_CAP) | (lane == kind + 2 * LINK_CAP)
    limit = jnp.sum(jnp.where(limits, lines, 0.0), axis=1, keepdims=True)
    arrive_t = onehot_rows(ends, BUS)
    sent[...] = narrow(dot(arrive_t, narrow(price[...])))
    arrive[...] = arrive_t
    cap[...] = jnp.broadcast_to(limit, (SLOT, HOUR))


def line_step(flows, near, far, cap, tau):
    moved = jnp.clip(flows + tau * (far - near), -cap, cap)
    return moved, extrapolate(moved, flows)


def local_step(season, consts, state, price_v, got, turn, tau, sigma):
    avail, asset_bus, run_cost, build_cost, efficiency, power, energy, link = consts
    disp, build, disch, level, scarce, sdual = state
    before_at = (season + SEASONS - 1) & (SEASONS - 1)
    after_at = (season + 1) & (SEASONS - 1)
    sums = got[0, 0:2]
    for s in range(1, SEASONS):
        sums = sums + got[s, 0:2]
    grad_build = sums * (1.0 / (HOUR * SEASONS))
    build_new = jnp.maximum(build - tau * (build_cost[...] - grad_build), 0.0)
    turn[0:8, :] = got[before_at]
    turn[8:16, :] = got[after_at]
    turn[16:18, :] = wide(extrapolate(build_new, build))
    turn[18:20, :] = run_cost[...]
    turn[20:22, :] = wide(asset_bus[...])
    turn[22:23, 0:BUS] = efficiency[...]
    turn[23:24, 0:BUS] = power[...]
    turn[24:25, 0:BUS] = energy[...]
    turn[25:26, 0:BUS] = wide(link[...])
    turned = columns(turn)
    build_x = long_column(turned, 16)
    cost = long_column(turned, 18)
    asset_t = onehot_rows(long_column(turned, 20), BUS)
    asset_row = row256(asset_bus)
    asset_onehot = as_bf(iota((BUS, SLOT), 0) == asset_row)
    decay = turned[:BUS, 22:23]
    power_c = turned[:BUS, 23:24]
    energy_c = turned[:BUS, 24:25]
    link_c = turned[:BUS, 25:26]
    before_level, before_dual = turned[:BUS, 2:3], turned[BUS:, 2:3]
    before_first, before_link = turned[:BUS, 3:4], turned[BUS:, 3:4]
    after_first, after_link = turned[:BUS, 11:12], turned[BUS:, 11:12]
    price_b = narrow(price_v)
    dual_f = wide(narrow(sdual))
    grad_dispatch = dot(asset_t, price_b) - wide(narrow(scarce))
    grad_charge = wide(price_b) + dual_f
    first = dual_f[:, 0:1]
    after_last = (1.0 - link_c) * first + after_link * after_first
    following = jnp.concatenate([dual_f[:, 1:], after_last], axis=1)
    grad_soc = dual_f - decay * following
    before_grad = before_dual - decay * ((1.0 - before_link) * before_first + link_c * first)
    disp_new = jnp.maximum(disp - tau * (cost - grad_dispatch), 0.0)
    disch_new = jnp.clip(disch + tau * grad_charge, -power_c, power_c)
    level_new = jnp.clip(level + tau * grad_soc, 0.0, energy_c)
    before_new = jnp.clip(before_level + tau * before_grad, 0.0, energy_c)
    disp_x = extrapolate(disp_new, disp)
    charge_f = wide(extrapolate(disch_new, disch))
    soc_f = wide(extrapolate(level_new, level))
    before_x = wide(extrapolate(before_new, before_level))
    balance = dot(asset_onehot, disp_x) + charge_f
    avail_rows = wide(avail[...]) * build_x - wide(disp_x)
    carried = jnp.where(link_c == 1.0, before_x, soc_f[:, HOUR - 1 : HOUR])
    previous = jnp.concatenate([carried, soc_f[:, : HOUR - 1]], axis=1)
    soc_rows = soc_f - decay * previous + charge_f
    scarce_new = jnp.maximum(scarce - sigma * avail_rows, 0.0)
    sdual_new = sdual - sigma * soc_rows
    halves = (
        mean(disp_new, disp),
        mean(build_new, build),
        mean(disch_new, disch),
        mean(level_new, level),
        mean(scarce_new, scarce),
        mean(sdual_new, sdual),
    )
    return balance, halves, link_c


def first_local(
    season, avail, asset_bus, run_cost, build_cost, efficiency, power, energy, link,
    disp, build, disch, level, scarce, sdual, price, got, lines_got, arrive, cap, far,
    disp1, build1, disch1, level1, scarce1, sdual1, came1, balance, rows, moves, turn,
):
    consts = (avail, asset_bus, run_cost, build_cost, efficiency, power, energy, link)
    state = (disp[...], build[...], disch[...], level[...], scarce[...], sdual[...])
    came0, near, _ = unpack(lines_got)
    moved, came_x = line_step(came0, near, wide(far[...]), cap[...], step_size)
    came1[...] = mean(moved, came0)
    local, halves, link_c = local_step(
        season[0], consts, state, price[...], got, turn, step_size, step_size
    )
    balance[...] = local + dot_t(arrive[...], came_x)
    for ref, value in zip((disp1, build1, disch1, level1, scarce1, sdual1), halves):
        ref[...] = value
    sums = jnp.sum(wide(avail[...]) * wide(narrow(halves[4])), axis=1, keepdims=True)
    rows[...] = season_block(sums, halves[3], wide(narrow(halves[5])), link_c, None)
    primal = (
        square(halves[0], state[0])
        + square(halves[1], state[1]) * (1.0 / SEASONS)
        + square(halves[2], state[2])
        + square(halves[3], state[3])
    )
    dual = square(halves[4], state[4]) + square(halves[5], state[5])
    lane = iota((8, 128), 1)
    moves[...] = jnp.where(lane == 0, primal, dual)


def price_step(
    flow0, near0, cap, leave, arrive, got, demand, price, balance, moves,
    price1, flow1, far0, sent,
):
    f0 = flow0[...]
    leave_t = leave[...]
    moved, flow_x = line_step(f0, wide(near0[...]), wide(got[...]), cap[...], step_size)
    f1 = mean(moved, f0)
    flow1[...] = f1
    p0 = price[...]
    whole = balance[...] - dot_t(leave_t, flow_x)
    p1 = mean(p0 + step_size * (demand[...] - whole), p0)
    price1[...] = p1
    primal = moves[0:1, 0:1] + square(f1, f0)
    dual = moves[0:1, 1:2] + square(p1, p0)
    lane = iota((GROUP, 128), 1)
    held = jnp.zeros((GROUP, 128), F32)
    for at, value in ((0, primal), (3, dual)):
        for step in range(3):
            piece = wide(narrow(value))
            held = jnp.where(lane == at + step, piece, held)
            value = value - piece
    held = narrow(held)
    price_b = narrow(p1)
    near = narrow(dot(leave_t, price_b))
    far = narrow(dot(arrive[...], price_b))
    far0[...] = far
    pack(near, far, jnp.concatenate([held] * (REGIONS // GROUP), axis=0), sent)


def moves_out(got, rows, sent):
    shape = (8, REGIONS * PACK)
    at = iota(shape, 1)
    q = lax.shift_right_logical(at * 21846, 18)
    mask = as_bf(at - PACK * q == 2 * LINK_CAP)
    moves = dot(mask, got[...])
    held = jnp.where(iota((8, 128), 0) == 4, moves, rows[...])
    for s in range(SEASONS):
        sent[s] = held


def second_step(
    season, avail, asset_bus, run_cost, build_cost, efficiency, power, energy, link,
    disp, build, disch, level, scarce, sdual, price, got, lines_got, arrive, came_cap,
    came_far, came, demand, flow, cap, leave,
    disp2, build2, flow2, disch2, level2, price2, scarce2, sdual2, turn,
):
    moves = got[0, 4:5]
    for s in range(1, SEASONS):
        moves = moves + got[s, 4:5]
    primal = moves[:, 0:1] + moves[:, 1:2] + moves[:, 2:3]
    dual = moves[:, 3:4] + moves[:, 4:5] + moves[:, 5:6]
    weight = jnp.sqrt(jnp.sqrt((dual + 1e-06) / (primal + 1e-06)))
    tau = step_size / weight
    sigma = step_size * weight
    consts = (avail, asset_bus, run_cost, build_cost, efficiency, power, energy, link)
    state = (disp[...], build[...], disch[...], level[...], scarce[...], sdual[...])
    came_near, far, _ = unpack(lines_got)
    _, came_x = line_step(came[...], came_near, wide(came_far[...]), came_cap[...], tau)
    f1 = flow[...]
    p1 = price[...]
    leave_t = leave[...]
    near = dot(leave_t, narrow(p1))
    moved, flow_x = line_step(f1, near, far, cap[...], tau)
    flow2[...] = mean(moved, f1)
    local, halves, _ = local_step(season[0], consts, state, p1, got, turn, tau, sigma)
    whole = local + dot_t(arrive[...], came_x) - dot_t(leave_t, flow_x)
    price2[...] = mean(p1 + sigma * (demand[...] - whole), p1)
    for ref, value in zip((disp2, build2, disch2, level2, scarce2, sdual2), halves):
        ref[...] = value


def call(body, outs, *operands, scalar=False, turn=False):
    in_specs = [pl.BlockSpec(memory_space=pltpu.VMEM)] * len(operands)
    if scalar:
        in_specs[0] = pl.BlockSpec(memory_space=pltpu.SMEM)
    return pl.pallas_call(
        body,
        out_shape=[jax.ShapeDtypeStruct(shape, kind) for shape, kind in outs],
        in_specs=in_specs,
        out_specs=[pl.BlockSpec(memory_space=pltpu.VMEM)] * len(outs),
        scratch_shapes=[pltpu.VMEM((128, 128), F32)] if turn else [],
        compiler_params=pltpu.CompilerParams(vmem_limit_bytes=32 * 1024 * 1024),
    )(*operands)


def region_exchange(value, per_pair):
    cut = value.reshape(REGIONS, per_pair, LINK_CAP, HOUR)
    got = lax.all_to_all(cut, "region", split_axis=0, concat_axis=0, tiled=True)
    return got.reshape(value.shape)


def season_exchange(value):
    return lax.all_to_all(value, "season", split_axis=0, concat_axis=0, tiled=True)


def on_device(
    demand,
    avail,
    asset_bus,
    run_cost,
    build_cost,
    line_from,
    line_to,
    link_count,
    line_limit,
    efficiency,
    power_limit,
    energy_limit,
    season_link,
    dispatch,
    capacity,
    flow,
    charge,
    soc,
    price,
    scarcity,
    soc_dual,
):
    season = lax.axis_index("season").astype(I32).reshape(1)
    pair = lambda v: v.reshape(2, 128)
    short = lambda v: v.reshape(1, BUS)
    link = short(season_link)
    lines = ((SLOT, HOUR), F32)
    lines_b = ((SLOT, HOUR), BF16)
    buses = ((BUS, HOUR), F32)
    picks = ((SLOT, BUS), BF16)
    packed = ((REGIONS * PACK, HOUR), BF16)
    seasons = ((SEASONS, 8, 128), F32)
    consts = (
        avail,
        pair(asset_bus),
        pair(run_cost),
        pair(build_cost),
        short(efficiency),
        short(power_limit),
        short(energy_limit),
        link,
    )
    sent1, flow0, near0, cap, leave = call(
        lines_out,
        [packed, lines, lines_b, lines, picks],
        flow,
        price,
        pair(line_from),
        pair(line_to),
        pair(line_limit),
        link_count,
        turn=True,
    )
    got1 = region_exchange(sent1, 3)
    (rows1,) = call(season_out, [seasons], avail, scarcity, soc, soc_dual, link, turn=True)
    season1 = season_exchange(rows1)
    sent2, arrive, came_cap = call(ends_in, [lines_b, picks, lines], got1, price)
    got2 = region_exchange(sent2, 1)
    disp1, build1, disch1, level1, scarce1, sdual1, came1, balance, rows2, moves = call(
        first_local,
        [lines, ((2, 128), F32), buses, buses, lines, buses, lines, buses, ((8, 128), F32), ((8, 128), F32)],
        season,
        *consts,
        dispatch,
        pair(capacity),
        charge,
        soc,
        scarcity,
        soc_dual,
        price,
        season1,
        got1,
        arrive,
        came_cap,
        sent2,
        scalar=True,
        turn=True,
    )
    price1, flow1, came_far1, sent3 = call(
        price_step,
        [buses, lines, lines_b, packed],
        flow0,
        near0,
        cap,
        leave,
        arrive,
        got2,
        demand,
        price,
        balance,
        moves,
    )
    got3 = region_exchange(sent3, 3)
    (rows3,) = call(moves_out, [seasons], got3, rows2)
    season2 = season_exchange(rows3)
    disp2, build2, flow2, disch2, level2, price2, scarce2, sdual2 = call(
        second_step,
        [lines, ((2, 128), F32), lines, buses, buses, buses, lines, buses],
        season,
        *consts,
        disp1,
        build1,
        disch1,
        level1,
        scarce1,
        sdual1,
        price1,
        season2,
        got3,
        arrive,
        came_cap,
        came_far1,
        came1,
        demand,
        flow1,
        cap,
        leave,
        scalar=True,
        turn=True,
    )
    return (disp2, build2.reshape(capacity.shape), flow2, disch2, level2, price2, scarce2, sdual2)


def solution(mesh):
    both = P("region", "season")
    rows = P("region")
    in_specs = (
        both,
        both,
        rows,
        rows,
        rows,
        rows,
        rows,
        P("region", None),
        rows,
        rows,
        rows,
        rows,
        both,
        both,
        rows,
        both,
        both,
        both,
        both,
        both,
        both,
    )
    out_specs = (both, rows, both, both, both, both, both, both)
    return jax.shard_map(
        on_device, mesh=mesh, in_specs=in_specs, out_specs=out_specs, check_vma=False
    )
```

```python
import jax
import jax.numpy as jnp
from jax import lax
from jax.experimental import pallas as pl
from jax.experimental.pallas import tpu as pltpu
from jax.sharding import PartitionSpec as P

LINK_CAP = 4
PACK = 3 * LINK_CAP
GROUP = 16
step_size = 0.2
F32 = jnp.float32
BF16 = jnp.bfloat16
I32 = jnp.int32
REGIONS, SEASONS = 64, 8
SIDE_Y, SIDE_Z = 4, 16
Z_GROUPS = [[SIDE_Z * y + z for z in range(SIDE_Z)] for y in range(SIDE_Y)]
Y_GROUPS = [[SIDE_Z * y + z for y in range(SIDE_Y)] for z in range(SIDE_Z)]
BUS, SLOT, HOUR = 64, 256, 128
PACKED = GROUP * PACK
UNPACKED = 2 * GROUP * LINK_CAP + GROUP


def iota(shape, axis):
    return lax.broadcasted_iota(I32, shape, axis)


def dot(a, b):
    return jnp.dot(a, b, preferred_element_type=F32)


def dot_t(a, b):
    return lax.dot_general(a, b, (((0,), (0,)), ((), ())), preferred_element_type=F32)


def as_bf(mask):
    return jnp.where(mask, 1.0, 0.0).astype(BF16)


def narrow(value):
    return value.astype(BF16)


def wide(value):
    return value.astype(F32)


def extrapolate(newer, older):
    return narrow(2.0 * newer - older)


def mean(newer, older):
    return 0.5 * (newer + older)


def total(value):
    return jnp.sum(jnp.sum(value, axis=1, keepdims=True), axis=0, keepdims=True)


def square(newer, older):
    moved = newer - older
    return total(moved * moved)


def row256(ref):
    return jnp.concatenate([ref[0:1, :], ref[1:2, :]], axis=1)


def pack_target(packed):
    q = lax.shift_right_logical(packed * 171, 11)
    j = packed - PACK * q
    first = LINK_CAP * q + j
    second = GROUP * LINK_CAP + LINK_CAP * q + j - LINK_CAP
    third = 2 * GROUP * LINK_CAP + q
    return jnp.where(
        j < LINK_CAP,
        first,
        jnp.where(j < 2 * LINK_CAP, second, jnp.where(j == 2 * LINK_CAP, third, -1)),
    )


def send_target(packed):
    q = lax.shift_right_logical(packed * 171, 11)
    j = packed - PACK * q
    place = GROUP * (q & 3) + (q & -4)
    first = place + j
    second = GROUP * LINK_CAP + place + j - LINK_CAP
    third = 2 * GROUP * LINK_CAP + q
    return jnp.where(
        j < LINK_CAP,
        first,
        jnp.where(j < 2 * LINK_CAP, second, jnp.where(j == 2 * LINK_CAP, third, -1)),
    )


def across(value, g):
    lines = GROUP * LINK_CAP
    return [value[y * lines + g * GROUP : y * lines + (g + 1) * GROUP] for y in range(SIDE_Y)]


def pack(first, second, third, out_ref):
    shape = (PACKED, UNPACKED)
    place = as_bf(send_target(iota(shape, 0)) == iota(shape, 1))
    for g in range(REGIONS // GROUP):
        rows = jnp.concatenate(
            across(first, g) + across(second, g) + [third[g * GROUP : (g + 1) * GROUP]], axis=0
        )
        out_ref[g * PACKED : (g + 1) * PACKED, :] = narrow(dot(place, rows))


def unpack(ref):
    shape = (UNPACKED, PACKED)
    place = as_bf(pack_target(iota(shape, 1)) == iota(shape, 0))
    parts = [
        dot(place, ref[g * PACKED : (g + 1) * PACKED, :]) for g in range(REGIONS // GROUP)
    ]
    lines = GROUP * LINK_CAP
    first = jnp.concatenate([p[:lines] for p in parts], axis=0)
    second = jnp.concatenate([p[lines : 2 * lines] for p in parts], axis=0)
    third = jnp.concatenate([p[2 * lines :] for p in parts], axis=0)
    return first, second, third


def columns(ref):
    return jnp.transpose(ref[...])


def long_column(turned, at):
    return jnp.concatenate([turned[:, at : at + 1], turned[:, at + 1 : at + 2]], axis=0)


def onehot_rows(column, count):
    return as_bf(column == wide(iota((SLOT, count), 1)))


def lines_out(
    flow, price, line_from, line_to, line_limit, link_count,
    sent, flow0, near0, cap, leave, turn,
):
    lane = iota((1, SLOT), 1)
    target = iota((REGIONS, SLOT), 0)
    spread = as_bf(target == lax.shift_right_logical(iota((REGIONS, SLOT), 1), 2))
    reorder = SIDE_Z * (target & 3) + lax.shift_right_logical(target, 2)
    sending = as_bf(reorder == lax.shift_right_logical(iota((REGIONS, SLOT), 1), 2))
    counts = jnp.broadcast_to(narrow(wide(link_count[...])), (8, REGIONS))
    counts = dot(counts, spread)[0:1]
    live = jnp.where(wide(lane & (LINK_CAP - 1)) < counts, 1.0, 0.0)
    limit = row256(line_limit) * live
    turn[0:2, :] = wide(line_from[...])
    turn[2:3, :] = live[:, :128]
    turn[3:4, :] = live[:, 128:]
    turn[4:5, :] = limit[:, :128]
    turn[5:6, :] = limit[:, 128:]
    turned = columns(turn)
    leave_t = onehot_rows(long_column(turned, 0), BUS)
    f0 = flow[...] * long_column(turned, 2)
    near = narrow(dot(leave_t, narrow(price[...])))
    flow0[...] = f0
    near0[...] = near
    cap[...] = jnp.broadcast_to(long_column(turned, 4), (SLOT, HOUR))
    leave[...] = leave_t
    high = wide(narrow(limit))
    low = limit - high
    held = jnp.zeros((REGIONS, 128), F32)
    slot_kind = iota((SLOT, 128), 0) & (LINK_CAP - 1)
    for at, value in enumerate((wide(row256(line_to)), high, low)):
        spots = as_bf(iota((SLOT, 128), 1) == slot_kind + LINK_CAP * at)
        held = held + dot(sending * narrow(value), spots)
    pack(narrow(f0), near, narrow(held), sent)


def season_block(sums, level, dual_f, link_column):
    lane = iota((128, 128), 1)
    tail = jnp.concatenate([level[:, HOUR - 1 : HOUR], dual_f[:, HOUR - 1 : HOUR]], axis=0)
    head = jnp.concatenate([dual_f[:, 0:1], link_column], axis=0)
    held = jnp.where(
        lane == 0,
        sums[:128],
        jnp.where(lane == 1, sums[128:], jnp.where(lane == 2, tail, jnp.where(lane == 3, head, 0.0))),
    )
    return jnp.transpose(held)[0:8]


def season_out(avail, scarcity, soc, soc_dual, link, sent, turn):
    turn[0:1, 0:BUS] = wide(link[...])
    turned = columns(turn)
    sums = jnp.sum(wide(avail[...]) * wide(narrow(scarcity[...])), axis=1, keepdims=True)
    rows = season_block(sums, soc[...], wide(narrow(soc_dual[...])), turned[:BUS, 0:1])
    for s in range(SEASONS):
        sent[s] = rows


def ends_in(got, price, sent, far, arrive, cap):
    _, _, held = unpack(got)
    shape = (SLOT, REGIONS)
    spread = as_bf(iota(shape, 1) == lax.shift_right_logical(iota(shape, 0), 2))
    lines = dot(spread, narrow(held))
    lane = iota((SLOT, 128), 1)
    kind = iota((SLOT, 128), 0) & (LINK_CAP - 1)
    ends = jnp.sum(jnp.where(lane == kind, lines, 0.0), axis=1, keepdims=True)
    limits = (lane == kind + LINK_CAP) | (lane == kind + 2 * LINK_CAP)
    limit = jnp.sum(jnp.where(limits, lines, 0.0), axis=1, keepdims=True)
    arrive_t = onehot_rows(ends, BUS)
    values = narrow(dot(arrive_t, narrow(price[...])))
    far[...] = values
    row = iota((SLOT, SLOT), 0)
    z = lax.shift_right_logical(row, 4)
    source = GROUP * LINK_CAP * (lax.shift_right_logical(row, 2) & 3) + LINK_CAP * z + (row & 3)
    sent[...] = narrow(dot(as_bf(source == iota((SLOT, SLOT), 1)), values))
    arrive[...] = arrive_t
    cap[...] = jnp.broadcast_to(limit, (SLOT, HOUR))


def line_step(flows, near, far, cap, tau):
    moved = jnp.clip(flows + tau * (far - near), -cap, cap)
    return moved, extrapolate(moved, flows)


def local_step(season, consts, state, price_v, got, turn, tau, sigma):
    avail, asset_bus, run_cost, build_cost, efficiency, power, energy, link = consts
    disp, build, disch, level, scarce, sdual = state
    before_at = (season + SEASONS - 1) & (SEASONS - 1)
    after_at = (season + 1) & (SEASONS - 1)
    sums = got[0, 0:2]
    for s in range(1, SEASONS):
        sums = sums + got[s, 0:2]
    grad_build = sums * (1.0 / (HOUR * SEASONS))
    build_new = jnp.maximum(build - tau * (build_cost[...] - grad_build), 0.0)
    turn[0:8, :] = got[before_at]
    turn[8:16, :] = got[after_at]
    turn[16:18, :] = wide(extrapolate(build_new, build))
    turn[18:20, :] = run_cost[...]
    turn[20:22, :] = wide(asset_bus[...])
    turn[22:23, 0:BUS] = efficiency[...]
    turn[23:24, 0:BUS] = power[...]
    turn[24:25, 0:BUS] = energy[...]
    turn[25:26, 0:BUS] = wide(link[...])
    turned = columns(turn)
    build_x = long_column(turned, 16)
    cost = long_column(turned, 18)
    asset_t = onehot_rows(long_column(turned, 20), BUS)
    asset_row = row256(asset_bus)
    asset_onehot = as_bf(iota((BUS, SLOT), 0) == asset_row)
    decay = turned[:BUS, 22:23]
    power_c = turned[:BUS, 23:24]
    energy_c = turned[:BUS, 24:25]
    link_c = turned[:BUS, 25:26]
    before_level, before_dual = turned[:BUS, 2:3], turned[BUS:, 2:3]
    before_first, before_link = turned[:BUS, 3:4], turned[BUS:, 3:4]
    after_first, after_link = turned[:BUS, 11:12], turned[BUS:, 11:12]
    price_b = narrow(price_v)
    dual_f = wide(narrow(sdual))
    grad_dispatch = dot(asset_t, price_b) - wide(narrow(scarce))
    grad_charge = wide(price_b) + dual_f
    first = dual_f[:, 0:1]
    after_last = (1.0 - link_c) * first + after_link * after_first
    following = jnp.concatenate([dual_f[:, 1:], after_last], axis=1)
    grad_soc = dual_f - decay * following
    before_grad = before_dual - decay * ((1.0 - before_link) * before_first + link_c * first)
    disp_new = jnp.maximum(disp - tau * (cost - grad_dispatch), 0.0)
    disch_new = jnp.clip(disch + tau * grad_charge, -power_c, power_c)
    level_new = jnp.clip(level + tau * grad_soc, 0.0, energy_c)
    before_new = jnp.clip(before_level + tau * before_grad, 0.0, energy_c)
    disp_x = extrapolate(disp_new, disp)
    charge_f = wide(extrapolate(disch_new, disch))
    soc_f = wide(extrapolate(level_new, level))
    before_x = wide(extrapolate(before_new, before_level))
    balance = dot(asset_onehot, disp_x) + charge_f
    avail_rows = wide(avail[...]) * build_x - wide(disp_x)
    carried = jnp.where(link_c == 1.0, before_x, soc_f[:, HOUR - 1 : HOUR])
    previous = jnp.concatenate([carried, soc_f[:, : HOUR - 1]], axis=1)
    soc_rows = soc_f - decay * previous + charge_f
    scarce_new = jnp.maximum(scarce - sigma * avail_rows, 0.0)
    sdual_new = sdual - sigma * soc_rows
    halves = (
        mean(disp_new, disp),
        mean(build_new, build),
        mean(disch_new, disch),
        mean(level_new, level),
        mean(scarce_new, scarce),
        mean(sdual_new, sdual),
    )
    return balance, halves, link_c


def first_local(
    season, avail, asset_bus, run_cost, build_cost, efficiency, power, energy, link,
    disp, build, disch, level, scarce, sdual, price, got, lines_got, arrive, cap, far,
    disp1, build1, disch1, level1, scarce1, sdual1, came1, balance, rows, moves, turn,
):
    consts = (avail, asset_bus, run_cost, build_cost, efficiency, power, energy, link)
    state = (disp[...], build[...], disch[...], level[...], scarce[...], sdual[...])
    came0, near, _ = unpack(lines_got)
    moved, came_x = line_step(came0, near, wide(far[...]), cap[...], step_size)
    came1[...] = mean(moved, came0)
    local, halves, link_c = local_step(
        season[0], consts, state, price[...], got, turn, step_size, step_size
    )
    balance[...] = local + dot_t(arrive[...], came_x)
    for ref, value in zip((disp1, build1, disch1, level1, scarce1, sdual1), halves):
        ref[...] = value
    sums = jnp.sum(wide(avail[...]) * wide(narrow(halves[4])), axis=1, keepdims=True)
    rows[...] = season_block(sums, halves[3], wide(narrow(halves[5])), link_c)
    primal = (
        square(halves[0], state[0])
        + square(halves[1], state[1]) * (1.0 / SEASONS)
        + square(halves[2], state[2])
        + square(halves[3], state[3])
    )
    dual = square(halves[4], state[4]) + square(halves[5], state[5])
    lane = iota((8, 128), 1)
    moves[...] = jnp.where(lane == 0, primal, dual)


def price_step(
    flow0, near0, cap, leave, arrive, got, demand, price, balance, moves,
    price1, flow1, far0, sent,
):
    f0 = flow0[...]
    leave_t = leave[...]
    moved, flow_x = line_step(f0, wide(near0[...]), wide(got[...]), cap[...], step_size)
    f1 = mean(moved, f0)
    flow1[...] = f1
    p0 = price[...]
    whole = balance[...] - dot_t(leave_t, flow_x)
    p1 = mean(p0 + step_size * (demand[...] - whole), p0)
    price1[...] = p1
    primal = moves[0:1, 0:1] + square(f1, f0)
    dual = moves[0:1, 1:2] + square(p1, p0)
    lane = iota((GROUP, 128), 1)
    held = jnp.zeros((GROUP, 128), F32)
    for at, value in ((0, primal), (3, dual)):
        for step in range(3):
            piece = wide(narrow(value))
            held = jnp.where(lane == at + step, piece, held)
            value = value - piece
    held = narrow(held)
    price_b = narrow(p1)
    near = narrow(dot(leave_t, price_b))
    far = narrow(dot(arrive[...], price_b))
    far0[...] = far
    pack(near, far, jnp.concatenate([held] * (REGIONS // GROUP), axis=0), sent)


def moves_out(got, rows, sent):
    shape = (8, REGIONS * PACK)
    at = iota(shape, 1)
    q = lax.shift_right_logical(at * 21846, 18)
    mask = as_bf(at - PACK * q == 2 * LINK_CAP)
    moves = dot(mask, got[...])
    held = jnp.where(iota((8, 128), 0) == 4, moves, rows[...])
    for s in range(SEASONS):
        sent[s] = held


def second_step(
    season, avail, asset_bus, run_cost, build_cost, efficiency, power, energy, link,
    disp, build, disch, level, scarce, sdual, price, got, lines_got, arrive, came_cap,
    came_far, came, demand, flow, cap, leave,
    disp2, build2, flow2, disch2, level2, price2, scarce2, sdual2, turn,
):
    moves = got[0, 4:5]
    for s in range(1, SEASONS):
        moves = moves + got[s, 4:5]
    primal = moves[:, 0:1] + moves[:, 1:2] + moves[:, 2:3]
    dual = moves[:, 3:4] + moves[:, 4:5] + moves[:, 5:6]
    weight = jnp.sqrt(jnp.sqrt((dual + 1e-06) / (primal + 1e-06)))
    tau = step_size / weight
    sigma = step_size * weight
    consts = (avail, asset_bus, run_cost, build_cost, efficiency, power, energy, link)
    state = (disp[...], build[...], disch[...], level[...], scarce[...], sdual[...])
    came_near, far, _ = unpack(lines_got)
    _, came_x = line_step(came[...], came_near, wide(came_far[...]), came_cap[...], tau)
    f1 = flow[...]
    p1 = price[...]
    leave_t = leave[...]
    near = dot(leave_t, narrow(p1))
    moved, flow_x = line_step(f1, near, far, cap[...], tau)
    flow2[...] = mean(moved, f1)
    local, halves, _ = local_step(season[0], consts, state, p1, got, turn, tau, sigma)
    whole = local + dot_t(arrive[...], came_x) - dot_t(leave_t, flow_x)
    price2[...] = mean(p1 + sigma * (demand[...] - whole), p1)
    for ref, value in zip((disp2, build2, disch2, level2, scarce2, sdual2), halves):
        ref[...] = value


def call(body, outs, *operands, scalar=False, turn=False):
    in_specs = [pl.BlockSpec(memory_space=pltpu.VMEM)] * len(operands)
    if scalar:
        in_specs[0] = pl.BlockSpec(memory_space=pltpu.SMEM)
    return pl.pallas_call(
        body,
        out_shape=[jax.ShapeDtypeStruct(shape, kind) for shape, kind in outs],
        in_specs=in_specs,
        out_specs=[pl.BlockSpec(memory_space=pltpu.VMEM)] * len(outs),
        scratch_shapes=[pltpu.VMEM((128, 128), F32)] if turn else [],
        compiler_params=pltpu.CompilerParams(vmem_limit_bytes=32 * 1024 * 1024),
    )(*operands)


def region_exchange(value, per_pair):
    cut = value.reshape(SIDE_Z, SIDE_Y * per_pair, LINK_CAP, HOUR)
    came = lax.all_to_all(cut, "region", 0, 0, axis_index_groups=Z_GROUPS, tiled=True)
    came = came.reshape(SIDE_Z, SIDE_Y, per_pair, LINK_CAP, HOUR).transpose(1, 0, 2, 3, 4)
    came = came.reshape(SIDE_Y, SIDE_Z * per_pair, LINK_CAP, HOUR)
    got = lax.all_to_all(came, "region", 0, 0, axis_index_groups=Y_GROUPS, tiled=True)
    return got.reshape(value.shape)


def season_exchange(value):
    return lax.all_to_all(value, "season", split_axis=0, concat_axis=0, tiled=True)


def on_device(
    demand,
    avail,
    asset_bus,
    run_cost,
    build_cost,
    line_from,
    line_to,
    link_count,
    line_limit,
    efficiency,
    power_limit,
    energy_limit,
    season_link,
    dispatch,
    capacity,
    flow,
    charge,
    soc,
    price,
    scarcity,
    soc_dual,
):
    season = lax.axis_index("season").astype(I32).reshape(1)
    pair = lambda v: v.reshape(2, 128)
    short = lambda v: v.reshape(1, BUS)
    link = short(season_link)
    lines = ((SLOT, HOUR), F32)
    lines_b = ((SLOT, HOUR), BF16)
    buses = ((BUS, HOUR), F32)
    picks = ((SLOT, BUS), BF16)
    packed = ((REGIONS * PACK, HOUR), BF16)
    seasons = ((SEASONS, 8, 128), F32)
    consts = (
        avail,
        pair(asset_bus),
        pair(run_cost),
        pair(build_cost),
        short(efficiency),
        short(power_limit),
        short(energy_limit),
        link,
    )
    sent1, flow0, near0, cap, leave = call(
        lines_out,
        [packed, lines, lines_b, lines, picks],
        flow,
        price,
        pair(line_from),
        pair(line_to),
        pair(line_limit),
        link_count,
        turn=True,
    )
    got1 = region_exchange(sent1, 3)
    (rows1,) = call(season_out, [seasons], avail, scarcity, soc, soc_dual, link, turn=True)
    season1 = season_exchange(rows1)
    sent2, came_far0, arrive, came_cap = call(
        ends_in, [lines_b, lines_b, picks, lines], got1, price
    )
    got2 = region_exchange(sent2, 1)
    disp1, build1, disch1, level1, scarce1, sdual1, came1, balance, rows2, moves = call(
        first_local,
        [lines, ((2, 128), F32), buses, buses, lines, buses, lines, buses, ((8, 128), F32), ((8, 128), F32)],
        season,
        *consts,
        dispatch,
        pair(capacity),
        charge,
        soc,
        scarcity,
        soc_dual,
        price,
        season1,
        got1,
        arrive,
        came_cap,
        came_far0,
        scalar=True,
        turn=True,
    )
    price1, flow1, came_far1, sent3 = call(
        price_step,
        [buses, lines, lines_b, packed],
        flow0,
        near0,
        cap,
        leave,
        arrive,
        got2,
        demand,
        price,
        balance,
        moves,
    )
    got3 = region_exchange(sent3, 3)
    (rows3,) = call(moves_out, [seasons], got3, rows2)
    season2 = season_exchange(rows3)
    disp2, build2, flow2, disch2, level2, price2, scarce2, sdual2 = call(
        second_step,
        [lines, ((2, 128), F32), lines, buses, buses, buses, lines, buses],
        season,
        *consts,
        disp1,
        build1,
        disch1,
        level1,
        scarce1,
        sdual1,
        price1,
        season2,
        got3,
        arrive,
        came_cap,
        came_far1,
        came1,
        demand,
        flow1,
        cap,
        leave,
        scalar=True,
        turn=True,
    )
    return (disp2, build2.reshape(capacity.shape), flow2, disch2, level2, price2, scarce2, sdual2)


def solution(mesh):
    both = P("region", "season")
    rows = P("region")
    in_specs = (
        both,
        both,
        rows,
        rows,
        rows,
        rows,
        rows,
        P("region", None),
        rows,
        rows,
        rows,
        rows,
        both,
        both,
        rows,
        both,
        both,
        both,
        both,
        both,
        both,
    )
    out_specs = (both, rows, both, both, both, both, both, both)
    return jax.shard_map(
        on_device, mesh=mesh, in_specs=in_specs, out_specs=out_specs, check_vma=False
    )
```

```python
import jax
import jax.numpy as jnp
from jax import lax
from jax.experimental import pallas as pl
from jax.experimental.pallas import tpu as pltpu
from jax.sharding import PartitionSpec as P

LINK_CAP = 4
GROUP = 16
step_size = 0.2
F32 = jnp.float32
BF16 = jnp.bfloat16
I32 = jnp.int32
REGIONS, SEASONS = 64, 8
BUS, SLOT, HOUR = 64, 256, 128
LINES = GROUP * LINK_CAP
WITH_FLOWS = (LINK_CAP, LINK_CAP, LINK_CAP)
WITH_MOVES = (LINK_CAP, LINK_CAP, 2)


def iota(shape, axis):
    return lax.broadcasted_iota(I32, shape, axis)


def dot(a, b):
    return jnp.dot(a, b, preferred_element_type=F32)


def dot_t(a, b):
    return lax.dot_general(a, b, (((0,), (0,)), ((), ())), preferred_element_type=F32)


def as_bf(mask):
    return jnp.where(mask, 1.0, 0.0).astype(BF16)


def narrow(value):
    return value.astype(BF16)


def wide(value):
    return value.astype(F32)


def extrapolate(newer, older):
    return narrow(2.0 * newer - older)


def mean(newer, older):
    return 0.5 * (newer + older)


def total(value):
    return jnp.sum(jnp.sum(value, axis=1, keepdims=True), axis=0, keepdims=True)


def square(newer, older):
    moved = newer - older
    return total(moved * moved)


def row256(ref):
    return jnp.concatenate([ref[0:1, :], ref[1:2, :]], axis=1)


def sizes(kinds):
    return GROUP * sum(kinds), 2 * LINES + GROUP * (LINK_CAP if kinds[2] == LINK_CAP else 1)


def pack_target(packed, kinds):
    rows = sum(kinds)
    q = lax.shift_right_logical(packed * (21846 * 12 // rows + 1), 18)
    j = packed - rows * q
    first = LINK_CAP * q + j
    second = LINES + first - LINK_CAP
    if kinds[2] == LINK_CAP:
        third = 2 * LINES + first - 2 * LINK_CAP
    else:
        third = jnp.where(j == 2 * LINK_CAP, 2 * LINES + q, -1)
    return jnp.where(j < LINK_CAP, first, jnp.where(j < 2 * LINK_CAP, second, third))


def pack(first, second, third, out_ref, kinds):
    shape = sizes(kinds)
    place = as_bf(pack_target(iota(shape, 0), kinds) == iota(shape, 1))
    thirds = shape[1] - 2 * LINES
    for g in range(REGIONS // GROUP):
        rows = jnp.concatenate(
            [
                first[g * LINES : (g + 1) * LINES],
                second[g * LINES : (g + 1) * LINES],
                third[g * thirds : (g + 1) * thirds],
            ],
            axis=0,
        )
        out_ref[g * shape[0] : (g + 1) * shape[0], :] = narrow(dot(place, rows))


def unpack(ref, kinds):
    packed, unpacked = sizes(kinds)
    shape = (unpacked, packed)
    place = as_bf(pack_target(iota(shape, 1), kinds) == iota(shape, 0))
    parts = [dot(place, ref[g * packed : (g + 1) * packed, :]) for g in range(REGIONS // GROUP)]
    first = jnp.concatenate([p[:LINES] for p in parts], axis=0)
    second = jnp.concatenate([p[LINES : 2 * LINES] for p in parts], axis=0)
    third = jnp.concatenate([p[2 * LINES :] for p in parts], axis=0)
    return first, second, third


def pieces(value):
    parts = []
    for _ in range(3):
        part = narrow(value)
        parts.append(part)
        value = value - wide(part)
    return parts


def columns(ref):
    return jnp.transpose(ref[...])


def long_column(turned, at):
    return jnp.concatenate([turned[:, at : at + 1], turned[:, at + 1 : at + 2]], axis=0)


def onehot_rows(column, count):
    return as_bf(column == wide(iota((SLOT, count), 1)))


def live_limit(line_limit, link_count):
    shape = (REGIONS, SLOT)
    spread = as_bf(iota(shape, 0) == lax.shift_right_logical(iota(shape, 1), 2))
    counts = jnp.broadcast_to(narrow(wide(link_count[...])), (8, REGIONS))
    counts = dot(counts, spread)[0:1]
    kind = iota((1, SLOT), 1) & (LINK_CAP - 1)
    live = jnp.where(wide(kind) < counts, 1.0, 0.0)
    return spread, live, row256(line_limit) * live


def ends_out(line_to, line_limit, link_count, sent):
    spread, _, limit = live_limit(line_limit, link_count)
    lane = iota((SLOT, 128), 1)
    kind = iota((SLOT, 128), 0) & (LINK_CAP - 1)
    held = dot(spread * narrow(wide(row256(line_to))), as_bf(lane == kind))
    spots = as_bf(lane == kind + LINK_CAP)
    for part in pieces(limit):
        held = held + dot(spread * part, spots)
    sent[...] = held


def lines_near(
    flow, price, line_from, line_limit, link_count, flow0, near0, cap, leave, turn
):
    _, live, limit = live_limit(line_limit, link_count)
    turn[0:2, :] = wide(line_from[...])
    turn[2:3, :] = live[:, :128]
    turn[3:4, :] = live[:, 128:]
    turn[4:5, :] = limit[:, :128]
    turn[5:6, :] = limit[:, 128:]
    turned = columns(turn)
    leave_t = onehot_rows(long_column(turned, 0), BUS)
    flow0[...] = flow[...] * long_column(turned, 2)
    near0[...] = narrow(dot(leave_t, narrow(price[...])))
    cap[...] = jnp.broadcast_to(long_column(turned, 4), (SLOT, HOUR))
    leave[...] = leave_t


def season_block(sums, level, dual_f, link_column):
    lane = iota((128, 128), 1)
    tail = jnp.concatenate([level[:, HOUR - 1 : HOUR], dual_f[:, HOUR - 1 : HOUR]], axis=0)
    head = jnp.concatenate([dual_f[:, 0:1], link_column], axis=0)
    held = jnp.where(
        lane == 0,
        sums[:128],
        jnp.where(lane == 1, sums[128:], jnp.where(lane == 2, tail, jnp.where(lane == 3, head, 0.0))),
    )
    return jnp.transpose(held)[0:8]


def season_out(avail, scarcity, soc, soc_dual, link, sent, turn):
    turn[0:1, 0:BUS] = wide(link[...])
    turned = columns(turn)
    sums = jnp.sum(wide(avail[...]) * wide(narrow(scarcity[...])), axis=1, keepdims=True)
    sent[0] = season_block(sums, soc[...], wide(narrow(soc_dual[...])), turned[:BUS, 0:1])


def ends_in(got, price, flow0, near0, sent, arrive, cap):
    shape = (SLOT, REGIONS)
    spread = as_bf(iota(shape, 1) == lax.shift_right_logical(iota(shape, 0), 2))
    high, middle, low = pieces(got[...])
    lines = dot(spread, high) + dot(spread, middle) + dot(spread, low)
    lane = iota((SLOT, 128), 1)
    kind = iota((SLOT, 128), 0) & (LINK_CAP - 1)
    ends = jnp.sum(jnp.where(lane == kind, lines, 0.0), axis=1, keepdims=True)
    limit = jnp.sum(jnp.where(lane == kind + LINK_CAP, lines, 0.0), axis=1, keepdims=True)
    arrive_t = onehot_rows(ends, BUS)
    far = narrow(dot(arrive_t, narrow(price[...])))
    arrive[...] = arrive_t
    cap[...] = jnp.broadcast_to(limit, (SLOT, HOUR))
    pack(narrow(flow0[...]), near0[...], far, sent, WITH_FLOWS)


def line_step(flows, near, far, cap, tau):
    moved = jnp.clip(flows + tau * (far - near), -cap, cap)
    return moved, extrapolate(moved, flows)


def tree(values):
    while len(values) > 1:
        values = [values[i] + values[i + 1] for i in range(0, len(values), 2)]
    return values[0]


def local_step(season, consts, state, price_v, got, turn, tau, sigma, paired):
    avail, asset_bus, run_cost, build_cost, efficiency, power, energy, link = consts
    disp, build, disch, level, scarce, sdual = state
    before_at = (season + SEASONS - 1) & (SEASONS - 1)
    after_at = (season + 1) & (SEASONS - 1)
    if paired:
        before_at, after_at = before_at ^ season, after_at ^ season
    sums = tree([got[s, 0:2] for s in range(SEASONS)])
    grad_build = sums * (1.0 / (HOUR * SEASONS))
    build_new = jnp.maximum(build - tau * (build_cost[...] - grad_build), 0.0)
    turn[0:8, :] = got[before_at]
    turn[8:16, :] = got[after_at]
    turn[16:18, :] = wide(extrapolate(build_new, build))
    turn[18:20, :] = run_cost[...]
    turn[20:22, :] = wide(asset_bus[...])
    turn[22:23, 0:BUS] = efficiency[...]
    turn[23:24, 0:BUS] = power[...]
    turn[24:25, 0:BUS] = energy[...]
    turn[25:26, 0:BUS] = wide(link[...])
    turned = columns(turn)
    build_x = long_column(turned, 16)
    cost = long_column(turned, 18)
    asset_t = onehot_rows(long_column(turned, 20), BUS)
    asset_row = row256(asset_bus)
    asset_onehot = as_bf(iota((BUS, SLOT), 0) == asset_row)
    decay = turned[:BUS, 22:23]
    power_c = turned[:BUS, 23:24]
    energy_c = turned[:BUS, 24:25]
    link_c = turned[:BUS, 25:26]
    before_level, before_dual = turned[:BUS, 2:3], turned[BUS:, 2:3]
    before_first, before_link = turned[:BUS, 3:4], turned[BUS:, 3:4]
    after_first, after_link = turned[:BUS, 11:12], turned[BUS:, 11:12]
    price_b = narrow(price_v)
    dual_f = wide(narrow(sdual))
    grad_dispatch = dot(asset_t, price_b) - wide(narrow(scarce))
    grad_charge = wide(price_b) + dual_f
    first = dual_f[:, 0:1]
    after_last = (1.0 - link_c) * first + after_link * after_first
    following = jnp.concatenate([dual_f[:, 1:], after_last], axis=1)
    grad_soc = dual_f - decay * following
    before_grad = before_dual - decay * ((1.0 - before_link) * before_first + link_c * first)
    disp_new = jnp.maximum(disp - tau * (cost - grad_dispatch), 0.0)
    disch_new = jnp.clip(disch + tau * grad_charge, -power_c, power_c)
    level_new = jnp.clip(level + tau * grad_soc, 0.0, energy_c)
    before_new = jnp.clip(before_level + tau * before_grad, 0.0, energy_c)
    disp_x = extrapolate(disp_new, disp)
    charge_f = wide(extrapolate(disch_new, disch))
    soc_f = wide(extrapolate(level_new, level))
    before_x = wide(extrapolate(before_new, before_level))
    balance = dot(asset_onehot, disp_x) + charge_f
    avail_rows = wide(avail[...]) * build_x - wide(disp_x)
    carried = jnp.where(link_c == 1.0, before_x, soc_f[:, HOUR - 1 : HOUR])
    previous = jnp.concatenate([carried, soc_f[:, : HOUR - 1]], axis=1)
    soc_rows = soc_f - decay * previous + charge_f
    scarce_new = jnp.maximum(scarce - sigma * avail_rows, 0.0)
    sdual_new = sdual - sigma * soc_rows
    halves = (
        mean(disp_new, disp),
        mean(build_new, build),
        mean(disch_new, disch),
        mean(level_new, level),
        mean(scarce_new, scarce),
        mean(sdual_new, sdual),
    )
    return balance, halves, link_c


def first_local(
    season, avail, asset_bus, run_cost, build_cost, efficiency, power, energy, link,
    disp, build, disch, level, scarce, sdual, price, got,
    disp1, build1, disch1, level1, scarce1, sdual1, balance, rows, moves, turn,
):
    consts = (avail, asset_bus, run_cost, build_cost, efficiency, power, energy, link)
    state = (disp[...], build[...], disch[...], level[...], scarce[...], sdual[...])
    local, halves, link_c = local_step(
        season[0], consts, state, price[...], got, turn, step_size, step_size, True
    )
    balance[...] = local
    for ref, value in zip((disp1, build1, disch1, level1, scarce1, sdual1), halves):
        ref[...] = value
    sums = jnp.sum(wide(avail[...]) * wide(narrow(halves[4])), axis=1, keepdims=True)
    rows[...] = season_block(sums, halves[3], wide(narrow(halves[5])), link_c)
    primal = (
        square(halves[0], state[0])
        + square(halves[1], state[1]) * (1.0 / SEASONS)
        + square(halves[2], state[2])
        + square(halves[3], state[3])
    )
    dual = square(halves[4], state[4]) + square(halves[5], state[5])
    lane = iota((8, 128), 1)
    moves[...] = jnp.where(lane == 0, primal, dual)


def price_step(
    flow0, near0, cap, leave, arrive, came_cap, got, demand, price, balance, moves,
    price1, flow1, came1, far1, sent,
):
    f0 = flow0[...]
    p0 = price[...]
    leave_t = leave[...]
    arrive_t = arrive[...]
    came0, came_near, far = unpack(got, WITH_FLOWS)
    came_far = dot(arrive_t, narrow(p0))
    came_moved, came_x = line_step(came0, came_near, came_far, came_cap[...], step_size)
    came1[...] = mean(came_moved, came0)
    moved, flow_x = line_step(f0, wide(near0[...]), far, cap[...], step_size)
    f1 = mean(moved, f0)
    flow1[...] = f1
    whole = balance[...] + dot_t(arrive_t, came_x) - dot_t(leave_t, flow_x)
    p1 = mean(p0 + step_size * (demand[...] - whole), p0)
    price1[...] = p1
    primal = moves[0:1, 0:1] + square(f1, f0)
    dual = moves[0:1, 1:2] + square(p1, p0)
    lane = iota((GROUP, 128), 1)
    held = jnp.zeros((GROUP, 128), F32)
    for at, value in ((0, primal), (3, dual)):
        for step, piece in enumerate(pieces(value)):
            held = jnp.where(lane == at + step, wide(piece), held)
    held = narrow(held)
    price_b = narrow(p1)
    near = narrow(dot(leave_t, price_b))
    far = narrow(dot(arrive_t, price_b))
    far1[...] = far
    pack(near, far, jnp.concatenate([held] * (REGIONS // GROUP), axis=0), sent, WITH_MOVES)


def moves_out(got, rows, sent):
    rows_each = sum(WITH_MOVES)
    shape = (8, REGIONS * rows_each)
    at = iota(shape, 1)
    q = lax.shift_right_logical(at * (262144 // rows_each + 1), 18)
    mask = as_bf(at - rows_each * q == 2 * LINK_CAP)
    moves = dot(mask, got[...])
    held = jnp.where(iota((8, 128), 0) == 4, moves, rows[...])
    for s in range(SEASONS):
        sent[s] = held


def second_step(
    season, avail, asset_bus, run_cost, build_cost, efficiency, power, energy, link,
    disp, build, disch, level, scarce, sdual, price, got, lines_got, arrive, came_cap,
    came_far, came, demand, flow, cap, leave,
    disp2, build2, flow2, disch2, level2, price2, scarce2, sdual2, turn,
):
    moves = tree([got[s, 4:5] for s in range(SEASONS)])
    primal = moves[:, 0:1] + moves[:, 1:2] + moves[:, 2:3]
    dual = moves[:, 3:4] + moves[:, 4:5] + moves[:, 5:6]
    weight = jnp.sqrt(jnp.sqrt((dual + 1e-06) / (primal + 1e-06)))
    tau = step_size / weight
    sigma = step_size * weight
    consts = (avail, asset_bus, run_cost, build_cost, efficiency, power, energy, link)
    state = (disp[...], build[...], disch[...], level[...], scarce[...], sdual[...])
    came_near, far, _ = unpack(lines_got, WITH_MOVES)
    _, came_x = line_step(came[...], came_near, wide(came_far[...]), came_cap[...], tau)
    f1 = flow[...]
    p1 = price[...]
    leave_t = leave[...]
    near = dot(leave_t, narrow(p1))
    moved, flow_x = line_step(f1, near, far, cap[...], tau)
    flow2[...] = mean(moved, f1)
    local, halves, _ = local_step(season[0], consts, state, p1, got, turn, tau, sigma, False)
    whole = local + dot_t(arrive[...], came_x) - dot_t(leave_t, flow_x)
    price2[...] = mean(p1 + sigma * (demand[...] - whole), p1)
    for ref, value in zip((disp2, build2, disch2, level2, scarce2, sdual2), halves):
        ref[...] = value


def call(body, outs, *operands, scalar=False, turn=False):
    in_specs = [pl.BlockSpec(memory_space=pltpu.VMEM)] * len(operands)
    if scalar:
        in_specs[0] = pl.BlockSpec(memory_space=pltpu.SMEM)
    return pl.pallas_call(
        body,
        out_shape=[jax.ShapeDtypeStruct(shape, kind) for shape, kind in outs],
        in_specs=in_specs,
        out_specs=[pl.BlockSpec(memory_space=pltpu.VMEM)] * len(outs),
        scratch_shapes=[pltpu.VMEM((128, 128), F32)] if turn else [],
        compiler_params=pltpu.CompilerParams(vmem_limit_bytes=32 * 1024 * 1024),
    )(*operands)


def region_exchange(value, rows, per_pair):
    cut = value.reshape(REGIONS, per_pair, rows, HOUR)
    got = lax.all_to_all(cut, "region", split_axis=0, concat_axis=0, tiled=True)
    return got.reshape(value.shape)


def season_exchange(value):
    return lax.all_to_all(value, "season", split_axis=0, concat_axis=0, tiled=True)


def season_gather(value):
    apart = 1
    while apart < SEASONS:
        pairs = [(s, s ^ apart) for s in range(SEASONS)]
        value = jnp.concatenate([value, lax.ppermute(value, "season", pairs)], axis=0)
        apart *= 2
    return value


def on_device(
    demand,
    avail,
    asset_bus,
    run_cost,
    build_cost,
    line_from,
    line_to,
    link_count,
    line_limit,
    efficiency,
    power_limit,
    energy_limit,
    season_link,
    dispatch,
    capacity,
    flow,
    charge,
    soc,
    price,
    scarcity,
    soc_dual,
):
    season = lax.axis_index("season").astype(I32).reshape(1)
    pair = lambda v: v.reshape(2, 128)
    short = lambda v: v.reshape(1, BUS)
    link = short(season_link)
    lines = ((SLOT, HOUR), F32)
    lines_b = ((SLOT, HOUR), BF16)
    buses = ((BUS, HOUR), F32)
    picks = ((SLOT, BUS), BF16)
    rows_of = lambda kinds: ((REGIONS * sum(kinds), HOUR), BF16)
    seasons = ((SEASONS, 8, 128), F32)
    pack_row = ((8, 128), F32)
    consts = (
        avail,
        pair(asset_bus),
        pair(run_cost),
        pair(build_cost),
        short(efficiency),
        short(power_limit),
        short(energy_limit),
        link,
    )
    limit = pair(line_limit)
    (sent1,) = call(ends_out, [((REGIONS, 128), F32)], pair(line_to), limit, link_count)
    got1 = region_exchange(sent1, 1, 1)
    (rows1,) = call(
        season_out, [((1, 8, 128), F32)], avail, scarcity, soc, soc_dual, link, turn=True
    )
    season1 = season_gather(rows1)
    flow0, near0, cap, leave = call(
        lines_near,
        [lines, lines_b, lines, picks],
        flow,
        price,
        pair(line_from),
        limit,
        link_count,
        turn=True,
    )
    got1, season1 = lax.optimization_barrier((got1, season1))
    sent2, arrive, came_cap = call(
        ends_in, [rows_of(WITH_FLOWS), picks, lines], got1, price, flow0, near0
    )
    got2 = region_exchange(sent2, LINK_CAP, 3)
    disp1, build1, disch1, level1, scarce1, sdual1, balance, rows2, moves = call(
        first_local,
        [lines, ((2, 128), F32), buses, buses, lines, buses, buses, pack_row, pack_row],
        season,
        *consts,
        dispatch,
        pair(capacity),
        charge,
        soc,
        scarcity,
        soc_dual,
        price,
        season1,
        scalar=True,
        turn=True,
    )
    price1, flow1, came1, came_far1, sent3 = call(
        price_step,
        [buses, lines, lines, lines_b, rows_of(WITH_MOVES)],
        flow0,
        near0,
        cap,
        leave,
        arrive,
        came_cap,
        got2,
        demand,
        price,
        balance,
        moves,
    )
    got3 = region_exchange(sent3, 2, 5)
    (rows3,) = call(moves_out, [seasons], got3, rows2)
    season2 = season_exchange(rows3)
    disp2, build2, flow2, disch2, level2, price2, scarce2, sdual2 = call(
        second_step,
        [lines, ((2, 128), F32), lines, buses, buses, buses, lines, buses],
        season,
        *consts,
        disp1,
        build1,
        disch1,
        level1,
        scarce1,
        sdual1,
        price1,
        season2,
        got3,
        arrive,
        came_cap,
        came_far1,
        came1,
        demand,
        flow1,
        cap,
        leave,
        scalar=True,
        turn=True,
    )
    return (disp2, build2.reshape(capacity.shape), flow2, disch2, level2, price2, scarce2, sdual2)


def solution(mesh):
    both = P("region", "season")
    rows = P("region")
    in_specs = (
        both,
        both,
        rows,
        rows,
        rows,
        rows,
        rows,
        P("region", None),
        rows,
        rows,
        rows,
        rows,
        both,
        both,
        rows,
        both,
        both,
        both,
        both,
        both,
        both,
    )
    out_specs = (both, rows, both, both, both, both, both, both)
    return jax.shard_map(
        on_device, mesh=mesh, in_specs=in_specs, out_specs=out_specs, check_vma=False
    )
```

```python
import jax
import jax.numpy as jnp
from jax import lax
from jax.experimental import pallas as pl
from jax.experimental.pallas import tpu as pltpu
from jax.sharding import PartitionSpec as P

LINK_CAP = 4
GROUP = 16
step_size = 0.2
F32 = jnp.float32
BF16 = jnp.bfloat16
I32 = jnp.int32
REGIONS, SEASONS = 64, 8
BUS, SLOT, HOUR = 64, 256, 128
LINES = GROUP * LINK_CAP
WITH_FLOWS = (LINK_CAP, LINK_CAP, LINK_CAP)
WITH_MOVES = (LINK_CAP, LINK_CAP, 2)


def iota(shape, axis):
    return lax.broadcasted_iota(I32, shape, axis)


def dot(a, b):
    return jnp.dot(a, b, preferred_element_type=F32)


def dot_t(a, b):
    return lax.dot_general(a, b, (((0,), (0,)), ((), ())), preferred_element_type=F32)


def as_bf(mask):
    return jnp.where(mask, 1.0, 0.0).astype(BF16)


def narrow(value):
    return value.astype(BF16)


def wide(value):
    return value.astype(F32)


def extrapolate(newer, older):
    return narrow(2.0 * newer - older)


def mean(newer, older):
    return 0.5 * (newer + older)


def total(value):
    return jnp.sum(jnp.sum(value, axis=1, keepdims=True), axis=0, keepdims=True)


def square(newer, older):
    moved = newer - older
    return total(moved * moved)


def row256(ref):
    return jnp.concatenate([ref[0:1, :], ref[1:2, :]], axis=1)


def sizes(kinds):
    return GROUP * sum(kinds), 2 * LINES + GROUP * (LINK_CAP if kinds[2] == LINK_CAP else 1)


def pack_target(packed, kinds):
    rows = sum(kinds)
    q = lax.shift_right_logical(packed * (21846 * 12 // rows + 1), 18)
    j = packed - rows * q
    first = LINK_CAP * q + j
    second = LINES + first - LINK_CAP
    if kinds[2] == LINK_CAP:
        third = 2 * LINES + first - 2 * LINK_CAP
    else:
        third = jnp.where(j == 2 * LINK_CAP, 2 * LINES + q, -1)
    return jnp.where(j < LINK_CAP, first, jnp.where(j < 2 * LINK_CAP, second, third))


def pack(first, second, third, out_ref, kinds):
    shape = sizes(kinds)
    place = as_bf(pack_target(iota(shape, 0), kinds) == iota(shape, 1))
    thirds = shape[1] - 2 * LINES
    for g in range(REGIONS // GROUP):
        rows = jnp.concatenate(
            [
                first[g * LINES : (g + 1) * LINES],
                second[g * LINES : (g + 1) * LINES],
                third[g * thirds : (g + 1) * thirds],
            ],
            axis=0,
        )
        out_ref[g * shape[0] : (g + 1) * shape[0], :] = narrow(dot(place, rows))


def unpack(ref, kinds):
    packed, unpacked = sizes(kinds)
    shape = (unpacked, packed)
    place = as_bf(pack_target(iota(shape, 1), kinds) == iota(shape, 0))
    parts = [dot(place, ref[g * packed : (g + 1) * packed, :]) for g in range(REGIONS // GROUP)]
    first = jnp.concatenate([p[:LINES] for p in parts], axis=0)
    second = jnp.concatenate([p[LINES : 2 * LINES] for p in parts], axis=0)
    third = jnp.concatenate([p[2 * LINES :] for p in parts], axis=0)
    return first, second, third


def pieces(value):
    parts = []
    for _ in range(3):
        part = narrow(value)
        parts.append(part)
        value = value - wide(part)
    return parts


def columns(ref):
    return jnp.transpose(ref[...])


def long_column(turned, at):
    return jnp.concatenate([turned[:, at : at + 1], turned[:, at + 1 : at + 2]], axis=0)


def onehot_rows(column, count):
    return as_bf(column == wide(iota((SLOT, count), 1)))


def live_limit(line_limit, link_count):
    shape = (REGIONS, SLOT)
    spread = as_bf(iota(shape, 0) == lax.shift_right_logical(iota(shape, 1), 2))
    counts = jnp.broadcast_to(narrow(wide(link_count[...])), (8, REGIONS))
    counts = dot(counts, spread)[0:1]
    kind = iota((1, SLOT), 1) & (LINK_CAP - 1)
    live = jnp.where(wide(kind) < counts, 1.0, 0.0)
    return spread, live, row256(line_limit) * live


def field_times(season, value):
    product = (
        (season & 1) * value
        ^ (lax.shift_right_logical(season, 1) & 1) * (value << 1)
        ^ (lax.shift_right_logical(season, 2) & 1) * (value << 2)
    )
    product = product ^ ((lax.shift_right_logical(product, 4) & 1) * 22)
    return product ^ ((lax.shift_right_logical(product, 3) & 1) * 11)


def step_of(season):
    return jnp.where(season == SEASONS - 1, 1, season + 1)


def coset_of(season, region):
    high, low = lax.shift_right_logical(region, 3), region & 7
    offset = low ^ field_times(season, high)
    return high, offset, jnp.minimum(offset, offset ^ step_of(season))


def coset_groups():
    def times(a, b):
        product = 0
        for bit in range(3):
            product ^= (b << bit) * ((a >> bit) & 1)
        for bit in (4, 3):
            product ^= (0b1011 << (bit - 3)) * ((product >> bit) & 1)
        return product

    groups = []
    for s in range(SEASONS):
        step = 1 if s == SEASONS - 1 else s + 1
        for base in range(8):
            if base < base ^ step:
                groups.append(
                    [
                        (8 * a + (times(s, a) ^ base ^ (step * side))) * SEASONS + s
                        for side in range(2)
                        for a in range(8)
                    ]
                )
    return groups


def ends_out(region, season, line_to, line_limit, link_count, sent):
    _, _, limit = live_limit(line_limit, link_count)
    mine, offset, base = coset_of(season[0], region[0])
    position = mine + 8 * jnp.where(offset == base, 0, 1)
    shape = (GROUP, SLOT)
    member = iota(shape, 0)
    high = member & 7
    side = lax.shift_right_logical(member, 3)
    low = field_times(season[0], high) ^ base ^ (side * step_of(season[0]))
    chosen = as_bf(8 * high + low == lax.shift_right_logical(iota(shape, 1), 2))
    lane = iota((SLOT, 128), 1)
    kind = (iota((SLOT, 128), 0) & (LINK_CAP - 1)) + 2 * LINK_CAP * position
    held = dot(chosen * narrow(wide(row256(line_to))), as_bf(lane == kind))
    spots = as_bf(lane == kind + LINK_CAP)
    for part in pieces(limit):
        held = held + dot(chosen * part, spots)
    sent[...] = held


def lines_near(
    region, flow, price, line_from, line_limit, link_count,
    flow0, near0, cap, leave, source, turn,
):
    shape = (SEASONS, SLOT)
    season = iota(shape, 0)
    slot = iota(shape, 1)
    high, offset, base = coset_of(season, lax.shift_right_logical(slot, 2))
    _, _, own = coset_of(season, jnp.broadcast_to(region[0], shape))
    position = high + 8 * jnp.where(offset == base, 0, 1)
    spot = 128 * season + 2 * LINK_CAP * position + (slot & (LINK_CAP - 1))
    spot = jnp.min(wide(jnp.where(base == own, spot, 1 << 20)), axis=0, keepdims=True)
    _, live, limit = live_limit(line_limit, link_count)
    turn[0:2, :] = wide(line_from[...])
    turn[2:3, :] = live[:, :128]
    turn[3:4, :] = live[:, 128:]
    turn[4:5, :] = limit[:, :128]
    turn[5:6, :] = limit[:, 128:]
    turn[6:7, :] = spot[:, :128]
    turn[7:8, :] = spot[:, 128:]
    turned = columns(turn)
    source[...] = jnp.broadcast_to(long_column(turned, 6), (SLOT, 128))
    leave_t = onehot_rows(long_column(turned, 0), BUS)
    flow0[...] = flow[...] * long_column(turned, 2)
    near0[...] = narrow(dot(leave_t, narrow(price[...])))
    cap[...] = jnp.broadcast_to(long_column(turned, 4), (SLOT, HOUR))
    leave[...] = leave_t


def season_block(sums, level, dual_f, link_column):
    lane = iota((128, 128), 1)
    tail = jnp.concatenate([level[:, HOUR - 1 : HOUR], dual_f[:, HOUR - 1 : HOUR]], axis=0)
    head = jnp.concatenate([dual_f[:, 0:1], link_column], axis=0)
    held = jnp.where(
        lane == 0,
        sums[:128],
        jnp.where(lane == 1, sums[128:], jnp.where(lane == 2, tail, jnp.where(lane == 3, head, 0.0))),
    )
    return jnp.transpose(held)[0:8]


def season_out(avail, scarcity, soc, soc_dual, link, sent, turn):
    turn[0:1, 0:BUS] = wide(link[...])
    turned = columns(turn)
    sums = jnp.sum(wide(avail[...]) * wide(narrow(scarcity[...])), axis=1, keepdims=True)
    sent[...] = season_block(sums, soc[...], wide(narrow(soc_dual[...])), turned[:BUS, 0:1])


def season_with_ends(rows, ends, sent):
    gathered = jnp.sum(ends[...], axis=0, keepdims=True)
    held = jnp.where(iota((8, 128), 0) == 4, gathered, rows[...])
    for s in range(SEASONS):
        sent[s] = held


def ends_in(got, source, price, flow0, near0, sent, arrive, cap):
    lane = wide(iota((SLOT, 128), 1))
    spot = source[...]
    ends = jnp.zeros((SLOT, 128), F32)
    limit = jnp.zeros((SLOT, 128), F32)
    for s in range(SEASONS):
        row = got[s, 4:5]
        ends = jnp.where(lane + 128 * s == spot, row, ends)
        limit = jnp.where(lane + (128 * s - LINK_CAP) == spot, row, limit)
    ends = jnp.sum(ends, axis=1, keepdims=True)
    limit = jnp.sum(limit, axis=1, keepdims=True)
    arrive_t = onehot_rows(ends, BUS)
    far = narrow(dot(arrive_t, narrow(price[...])))
    arrive[...] = arrive_t
    cap[...] = jnp.broadcast_to(limit, (SLOT, HOUR))
    pack(narrow(flow0[...]), near0[...], far, sent, WITH_FLOWS)


def line_step(flows, near, far, cap, tau):
    moved = jnp.clip(flows + tau * (far - near), -cap, cap)
    return moved, extrapolate(moved, flows)


def tree(values):
    while len(values) > 1:
        values = [values[i] + values[i + 1] for i in range(0, len(values), 2)]
    return values[0]


def local_step(season, consts, state, price_v, got, turn, tau, sigma):
    avail, asset_bus, run_cost, build_cost, efficiency, power, energy, link = consts
    disp, build, disch, level, scarce, sdual = state
    before_at = (season + SEASONS - 1) & (SEASONS - 1)
    after_at = (season + 1) & (SEASONS - 1)
    sums = tree([got[s, 0:2] for s in range(SEASONS)])
    grad_build = sums * (1.0 / (HOUR * SEASONS))
    build_new = jnp.maximum(build - tau * (build_cost[...] - grad_build), 0.0)
    turn[0:8, :] = got[before_at]
    turn[8:16, :] = got[after_at]
    turn[16:18, :] = wide(extrapolate(build_new, build))
    turn[18:20, :] = run_cost[...]
    turn[20:22, :] = wide(asset_bus[...])
    turn[22:23, 0:BUS] = efficiency[...]
    turn[23:24, 0:BUS] = power[...]
    turn[24:25, 0:BUS] = energy[...]
    turn[25:26, 0:BUS] = wide(link[...])
    turned = columns(turn)
    build_x = long_column(turned, 16)
    cost = long_column(turned, 18)
    asset_t = onehot_rows(long_column(turned, 20), BUS)
    asset_row = row256(asset_bus)
    asset_onehot = as_bf(iota((BUS, SLOT), 0) == asset_row)
    decay = turned[:BUS, 22:23]
    power_c = turned[:BUS, 23:24]
    energy_c = turned[:BUS, 24:25]
    link_c = turned[:BUS, 25:26]
    before_level, before_dual = turned[:BUS, 2:3], turned[BUS:, 2:3]
    before_first, before_link = turned[:BUS, 3:4], turned[BUS:, 3:4]
    after_first, after_link = turned[:BUS, 11:12], turned[BUS:, 11:12]
    price_b = narrow(price_v)
    dual_f = wide(narrow(sdual))
    grad_dispatch = dot(asset_t, price_b) - wide(narrow(scarce))
    grad_charge = wide(price_b) + dual_f
    first = dual_f[:, 0:1]
    after_last = (1.0 - link_c) * first + after_link * after_first
    following = jnp.concatenate([dual_f[:, 1:], after_last], axis=1)
    grad_soc = dual_f - decay * following
    before_grad = before_dual - decay * ((1.0 - before_link) * before_first + link_c * first)
    disp_new = jnp.maximum(disp - tau * (cost - grad_dispatch), 0.0)
    disch_new = jnp.clip(disch + tau * grad_charge, -power_c, power_c)
    level_new = jnp.clip(level + tau * grad_soc, 0.0, energy_c)
    before_new = jnp.clip(before_level + tau * before_grad, 0.0, energy_c)
    disp_x = extrapolate(disp_new, disp)
    charge_f = wide(extrapolate(disch_new, disch))
    soc_f = wide(extrapolate(level_new, level))
    before_x = wide(extrapolate(before_new, before_level))
    balance = dot(asset_onehot, disp_x) + charge_f
    avail_rows = wide(avail[...]) * build_x - wide(disp_x)
    carried = jnp.where(link_c == 1.0, before_x, soc_f[:, HOUR - 1 : HOUR])
    previous = jnp.concatenate([carried, soc_f[:, : HOUR - 1]], axis=1)
    soc_rows = soc_f - decay * previous + charge_f
    scarce_new = jnp.maximum(scarce - sigma * avail_rows, 0.0)
    sdual_new = sdual - sigma * soc_rows
    halves = (
        mean(disp_new, disp),
        mean(build_new, build),
        mean(disch_new, disch),
        mean(level_new, level),
        mean(scarce_new, scarce),
        mean(sdual_new, sdual),
    )
    return balance, halves, link_c


def first_local(
    season, avail, asset_bus, run_cost, build_cost, efficiency, power, energy, link,
    disp, build, disch, level, scarce, sdual, price, got,
    disp1, build1, disch1, level1, scarce1, sdual1, balance, rows, moves, turn,
):
    consts = (avail, asset_bus, run_cost, build_cost, efficiency, power, energy, link)
    state = (disp[...], build[...], disch[...], level[...], scarce[...], sdual[...])
    local, halves, link_c = local_step(
        season[0], consts, state, price[...], got, turn, step_size, step_size
    )
    balance[...] = local
    for ref, value in zip((disp1, build1, disch1, level1, scarce1, sdual1), halves):
        ref[...] = value
    sums = jnp.sum(wide(avail[...]) * wide(narrow(halves[4])), axis=1, keepdims=True)
    rows[...] = season_block(sums, halves[3], wide(narrow(halves[5])), link_c)
    primal = (
        square(halves[0], state[0])
        + square(halves[1], state[1]) * (1.0 / SEASONS)
        + square(halves[2], state[2])
        + square(halves[3], state[3])
    )
    dual = square(halves[4], state[4]) + square(halves[5], state[5])
    lane = iota((8, 128), 1)
    moves[...] = jnp.where(lane == 0, primal, dual)


def price_step(
    flow0, near0, cap, leave, arrive, came_cap, got, demand, price, balance, moves,
    price1, flow1, came1, far1, sent,
):
    f0 = flow0[...]
    p0 = price[...]
    leave_t = leave[...]
    arrive_t = arrive[...]
    came0, came_near, far = unpack(got, WITH_FLOWS)
    came_far = dot(arrive_t, narrow(p0))
    came_moved, came_x = line_step(came0, came_near, came_far, came_cap[...], step_size)
    came1[...] = mean(came_moved, came0)
    moved, flow_x = line_step(f0, wide(near0[...]), far, cap[...], step_size)
    f1 = mean(moved, f0)
    flow1[...] = f1
    whole = balance[...] + dot_t(arrive_t, came_x) - dot_t(leave_t, flow_x)
    p1 = mean(p0 + step_size * (demand[...] - whole), p0)
    price1[...] = p1
    primal = moves[0:1, 0:1] + square(f1, f0)
    dual = moves[0:1, 1:2] + square(p1, p0)
    lane = iota((GROUP, 128), 1)
    held = jnp.zeros((GROUP, 128), F32)
    for at, value in ((0, primal), (3, dual)):
        for step, piece in enumerate(pieces(value)):
            held = jnp.where(lane == at + step, wide(piece), held)
    held = narrow(held)
    price_b = narrow(p1)
    near = narrow(dot(leave_t, price_b))
    far = narrow(dot(arrive_t, price_b))
    far1[...] = far
    pack(near, far, jnp.concatenate([held] * (REGIONS // GROUP), axis=0), sent, WITH_MOVES)


def moves_out(got, rows, sent):
    rows_each = sum(WITH_MOVES)
    shape = (8, REGIONS * rows_each)
    at = iota(shape, 1)
    q = lax.shift_right_logical(at * (262144 // rows_each + 1), 18)
    mask = as_bf(at - rows_each * q == 2 * LINK_CAP)
    moves = dot(mask, got[...])
    held = jnp.where(iota((8, 128), 0) == 4, moves, rows[...])
    for s in range(SEASONS):
        sent[s] = held


def second_step(
    season, avail, asset_bus, run_cost, build_cost, efficiency, power, energy, link,
    disp, build, disch, level, scarce, sdual, price, got, lines_got, arrive, came_cap,
    came_far, came, demand, flow, cap, leave,
    disp2, build2, flow2, disch2, level2, price2, scarce2, sdual2, turn,
):
    moves = tree([got[s, 4:5] for s in range(SEASONS)])
    primal = moves[:, 0:1] + moves[:, 1:2] + moves[:, 2:3]
    dual = moves[:, 3:4] + moves[:, 4:5] + moves[:, 5:6]
    weight = jnp.sqrt(jnp.sqrt((dual + 1e-06) / (primal + 1e-06)))
    tau = step_size / weight
    sigma = step_size * weight
    consts = (avail, asset_bus, run_cost, build_cost, efficiency, power, energy, link)
    state = (disp[...], build[...], disch[...], level[...], scarce[...], sdual[...])
    came_near, far, _ = unpack(lines_got, WITH_MOVES)
    _, came_x = line_step(came[...], came_near, wide(came_far[...]), came_cap[...], tau)
    f1 = flow[...]
    p1 = price[...]
    leave_t = leave[...]
    near = dot(leave_t, narrow(p1))
    moved, flow_x = line_step(f1, near, far, cap[...], tau)
    flow2[...] = mean(moved, f1)
    local, halves, _ = local_step(season[0], consts, state, p1, got, turn, tau, sigma)
    whole = local + dot_t(arrive[...], came_x) - dot_t(leave_t, flow_x)
    price2[...] = mean(p1 + sigma * (demand[...] - whole), p1)
    for ref, value in zip((disp2, build2, disch2, level2, scarce2, sdual2), halves):
        ref[...] = value


def call(body, outs, *operands, scalars=0, turn=False):
    in_specs = [pl.BlockSpec(memory_space=pltpu.SMEM)] * scalars
    in_specs += [pl.BlockSpec(memory_space=pltpu.VMEM)] * (len(operands) - scalars)
    return pl.pallas_call(
        body,
        out_shape=[jax.ShapeDtypeStruct(shape, kind) for shape, kind in outs],
        in_specs=in_specs,
        out_specs=[pl.BlockSpec(memory_space=pltpu.VMEM)] * len(outs),
        scratch_shapes=[pltpu.VMEM((128, 128), F32)] if turn else [],
        compiler_params=pltpu.CompilerParams(vmem_limit_bytes=32 * 1024 * 1024),
    )(*operands)


def region_exchange(value, rows, per_pair):
    cut = value.reshape(REGIONS, per_pair, rows, HOUR)
    got = lax.all_to_all(cut, "region", split_axis=0, concat_axis=0, tiled=True)
    return got.reshape(value.shape)


def season_exchange(value):
    return lax.all_to_all(value, "season", split_axis=0, concat_axis=0, tiled=True)


def on_device(
    demand,
    avail,
    asset_bus,
    run_cost,
    build_cost,
    line_from,
    line_to,
    link_count,
    line_limit,
    efficiency,
    power_limit,
    energy_limit,
    season_link,
    dispatch,
    capacity,
    flow,
    charge,
    soc,
    price,
    scarcity,
    soc_dual,
):
    season = lax.axis_index("season").astype(I32).reshape(1)
    region = lax.axis_index("region").astype(I32).reshape(1)
    pair = lambda v: v.reshape(2, 128)
    short = lambda v: v.reshape(1, BUS)
    link = short(season_link)
    lines = ((SLOT, HOUR), F32)
    lines_b = ((SLOT, HOUR), BF16)
    buses = ((BUS, HOUR), F32)
    picks = ((SLOT, BUS), BF16)
    rows_of = lambda kinds: ((REGIONS * sum(kinds), HOUR), BF16)
    seasons = ((SEASONS, 8, 128), F32)
    pack_row = ((8, 128), F32)
    consts = (
        avail,
        pair(asset_bus),
        pair(run_cost),
        pair(build_cost),
        short(efficiency),
        short(power_limit),
        short(energy_limit),
        link,
    )
    limit = pair(line_limit)
    (sent1,) = call(
        ends_out,
        [((GROUP, 128), F32)],
        region,
        season,
        pair(line_to),
        limit,
        link_count,
        scalars=2,
    )
    got1 = lax.all_to_all(
        sent1.reshape(GROUP, 1, 128),
        ("region", "season"),
        0,
        0,
        axis_index_groups=coset_groups(),
        tiled=True,
    ).reshape(GROUP, 128)
    (rows1,) = call(season_out, [pack_row], avail, scarcity, soc, soc_dual, link, turn=True)
    flow0, near0, cap, leave, source = call(
        lines_near,
        [lines, lines_b, lines, picks, lines],
        region,
        flow,
        price,
        pair(line_from),
        limit,
        link_count,
        scalars=1,
        turn=True,
    )
    (sent_s,) = call(season_with_ends, [seasons], rows1, got1)
    season1 = season_exchange(sent_s)
    sent2, arrive, came_cap = call(
        ends_in, [rows_of(WITH_FLOWS), picks, lines], season1, source, price, flow0, near0
    )
    got2 = region_exchange(sent2, LINK_CAP, 3)
    disp1, build1, disch1, level1, scarce1, sdual1, balance, rows2, moves = call(
        first_local,
        [lines, ((2, 128), F32), buses, buses, lines, buses, buses, pack_row, pack_row],
        season,
        *consts,
        dispatch,
        pair(capacity),
        charge,
        soc,
        scarcity,
        soc_dual,
        price,
        season1,
        scalars=1,
        turn=True,
    )
    price1, flow1, came1, came_far1, sent3 = call(
        price_step,
        [buses, lines, lines, lines_b, rows_of(WITH_MOVES)],
        flow0,
        near0,
        cap,
        leave,
        arrive,
        came_cap,
        got2,
        demand,
        price,
        balance,
        moves,
    )
    got3 = region_exchange(sent3, 2, 5)
    (rows3,) = call(moves_out, [seasons], got3, rows2)
    season2 = season_exchange(rows3)
    disp2, build2, flow2, disch2, level2, price2, scarce2, sdual2 = call(
        second_step,
        [lines, ((2, 128), F32), lines, buses, buses, buses, lines, buses],
        season,
        *consts,
        disp1,
        build1,
        disch1,
        level1,
        scarce1,
        sdual1,
        price1,
        season2,
        got3,
        arrive,
        came_cap,
        came_far1,
        came1,
        demand,
        flow1,
        cap,
        leave,
        scalars=1,
        turn=True,
    )
    return (disp2, build2.reshape(capacity.shape), flow2, disch2, level2, price2, scarce2, sdual2)


def solution(mesh):
    both = P("region", "season")
    rows = P("region")
    in_specs = (
        both,
        both,
        rows,
        rows,
        rows,
        rows,
        rows,
        P("region", None),
        rows,
        rows,
        rows,
        rows,
        both,
        both,
        rows,
        both,
        both,
        both,
        both,
        both,
        both,
    )
    out_specs = (both, rows, both, both, both, both, both, both)
    return jax.shard_map(
        on_device, mesh=mesh, in_specs=in_specs, out_specs=out_specs, check_vma=False
    )
```

```python
import jax
import jax.numpy as jnp
from jax import lax
from jax.experimental import pallas as pl
from jax.experimental.pallas import tpu as pltpu
from jax.sharding import PartitionSpec as P

LINK_CAP = 4
GROUP = 16
step_size = 0.2
F32 = jnp.float32
BF16 = jnp.bfloat16
I32 = jnp.int32
REGIONS, SEASONS = 64, 8
BUS, SLOT, HOUR = 64, 256, 128
LINES = GROUP * LINK_CAP
WITH_FLOWS = (LINK_CAP, LINK_CAP, LINK_CAP)
WITH_MOVES = (LINK_CAP, LINK_CAP, 2)


def iota(shape, axis):
    return lax.broadcasted_iota(I32, shape, axis)


def dot(a, b):
    return jnp.dot(a, b, preferred_element_type=F32)


def dot_t(a, b):
    return lax.dot_general(a, b, (((0,), (0,)), ((), ())), preferred_element_type=F32)


def as_bf(mask):
    return jnp.where(mask, 1.0, 0.0).astype(BF16)


def narrow(value):
    return value.astype(BF16)


def wide(value):
    return value.astype(F32)


def extrapolate(newer, older):
    return narrow(2.0 * newer - older)


def mean(newer, older):
    return 0.5 * (newer + older)


def total(value):
    return jnp.sum(jnp.sum(value, axis=1, keepdims=True), axis=0, keepdims=True)


def square(newer, older):
    moved = newer - older
    return total(moved * moved)


def row256(ref):
    return jnp.concatenate([ref[0:1, :], ref[1:2, :]], axis=1)


def sizes(kinds):
    return GROUP * sum(kinds), 2 * LINES + GROUP * (LINK_CAP if kinds[2] == LINK_CAP else 1)


def pack_target(packed, kinds):
    rows = sum(kinds)
    q = lax.shift_right_logical(packed * (21846 * 12 // rows + 1), 18)
    j = packed - rows * q
    first = LINK_CAP * q + j
    second = LINES + first - LINK_CAP
    if kinds[2] == LINK_CAP:
        third = 2 * LINES + first - 2 * LINK_CAP
    else:
        third = jnp.where(j == 2 * LINK_CAP, 2 * LINES + q, -1)
    return jnp.where(j < LINK_CAP, first, jnp.where(j < 2 * LINK_CAP, second, third))


def pack(first, second, third, out_ref, kinds):
    shape = sizes(kinds)
    place = as_bf(pack_target(iota(shape, 0), kinds) == iota(shape, 1))
    thirds = shape[1] - 2 * LINES
    for g in range(REGIONS // GROUP):
        rows = jnp.concatenate(
            [
                first[g * LINES : (g + 1) * LINES],
                second[g * LINES : (g + 1) * LINES],
                third[g * thirds : (g + 1) * thirds],
            ],
            axis=0,
        )
        out_ref[g * shape[0] : (g + 1) * shape[0], :] = narrow(dot(place, rows))


def unpack(ref, kinds):
    packed, unpacked = sizes(kinds)
    shape = (unpacked, packed)
    place = as_bf(pack_target(iota(shape, 1), kinds) == iota(shape, 0))
    parts = [dot(place, ref[g * packed : (g + 1) * packed, :]) for g in range(REGIONS // GROUP)]
    first = jnp.concatenate([p[:LINES] for p in parts], axis=0)
    second = jnp.concatenate([p[LINES : 2 * LINES] for p in parts], axis=0)
    third = jnp.concatenate([p[2 * LINES :] for p in parts], axis=0)
    return first, second, third


def pieces(value):
    parts = []
    for _ in range(3):
        part = narrow(value)
        parts.append(part)
        value = value - wide(part)
    return parts


def columns(ref):
    return jnp.transpose(ref[...])


def long_column(turned, at):
    return jnp.concatenate([turned[:, at : at + 1], turned[:, at + 1 : at + 2]], axis=0)


def onehot_rows(column, count):
    return as_bf(column == wide(iota((SLOT, count), 1)))


def live_limit(line_limit, link_count):
    shape = (REGIONS, SLOT)
    spread = as_bf(iota(shape, 0) == lax.shift_right_logical(iota(shape, 1), 2))
    counts = jnp.broadcast_to(narrow(wide(link_count[...])), (8, REGIONS))
    counts = dot(counts, spread)[0:1]
    kind = iota((1, SLOT), 1) & (LINK_CAP - 1)
    live = jnp.where(wide(kind) < counts, 1.0, 0.0)
    return spread, live, row256(line_limit) * live


def field_times(season, value):
    product = (
        (season & 1) * value
        ^ (lax.shift_right_logical(season, 1) & 1) * (value << 1)
        ^ (lax.shift_right_logical(season, 2) & 1) * (value << 2)
    )
    product = product ^ ((lax.shift_right_logical(product, 4) & 1) * 22)
    return product ^ ((lax.shift_right_logical(product, 3) & 1) * 11)


def step_of(season):
    return jnp.where(season == SEASONS - 1, 1, season + 1)


def coset_of(season, region):
    high, low = lax.shift_right_logical(region, 3), region & 7
    offset = low ^ field_times(season, high)
    return high, offset, jnp.minimum(offset, offset ^ step_of(season))


def fetch(sources, held, sems):
    copies = [
        pltpu.make_async_copy(source, target, sems.at[at])
        for at, (source, target) in enumerate(zip(sources, held))
    ]
    for copy in copies:
        copy.start()
    for copy in copies:
        copy.wait()


def coset_groups():
    def times(a, b):
        product = 0
        for bit in range(3):
            product ^= (b << bit) * ((a >> bit) & 1)
        for bit in (4, 3):
            product ^= (0b1011 << (bit - 3)) * ((product >> bit) & 1)
        return product

    groups = []
    for s in range(SEASONS):
        step = 1 if s == SEASONS - 1 else s + 1
        for base in range(8):
            if base < base ^ step:
                groups.append(
                    [
                        (8 * a + (times(s, a) ^ base ^ (step * side))) * SEASONS + s
                        for side in range(2)
                        for a in range(8)
                    ]
                )
    return groups


def ends_out(region, season, *refs):
    sources, (sent, line_to, line_limit, link_count, sems) = refs[:3], refs[3:]
    fetch(sources, (line_to, line_limit, link_count), sems)
    _, _, limit = live_limit(line_limit, link_count)
    mine, offset, base = coset_of(season[0], region[0])
    position = mine + 8 * jnp.where(offset == base, 0, 1)
    shape = (GROUP, SLOT)
    member = iota(shape, 0)
    high = member & 7
    side = lax.shift_right_logical(member, 3)
    low = field_times(season[0], high) ^ base ^ (side * step_of(season[0]))
    chosen = as_bf(8 * high + low == lax.shift_right_logical(iota(shape, 1), 2))
    lane = iota((SLOT, 128), 1)
    kind = (iota((SLOT, 128), 0) & (LINK_CAP - 1)) + 2 * LINK_CAP * position
    held = dot(chosen * narrow(wide(row256(line_to))), as_bf(lane == kind))
    spots = as_bf(lane == kind + LINK_CAP)
    for part in pieces(limit):
        held = held + dot(chosen * part, spots)
    sent[...] = held


def lines_near(
    region, flow, price, line_from, line_limit, link_count,
    flow0, near0, cap, leave, source, turn,
):
    shape = (SEASONS, SLOT)
    season = iota(shape, 0)
    slot = iota(shape, 1)
    high, offset, base = coset_of(season, lax.shift_right_logical(slot, 2))
    _, _, own = coset_of(season, jnp.broadcast_to(region[0], shape))
    position = high + 8 * jnp.where(offset == base, 0, 1)
    spot = 128 * season + 2 * LINK_CAP * position + (slot & (LINK_CAP - 1))
    spot = jnp.min(wide(jnp.where(base == own, spot, 1 << 20)), axis=0, keepdims=True)
    _, live, limit = live_limit(line_limit, link_count)
    turn[0:2, :] = wide(line_from[...])
    turn[2:3, :] = live[:, :128]
    turn[3:4, :] = live[:, 128:]
    turn[4:5, :] = limit[:, :128]
    turn[5:6, :] = limit[:, 128:]
    turn[6:7, :] = spot[:, :128]
    turn[7:8, :] = spot[:, 128:]
    turned = columns(turn)
    source[...] = jnp.broadcast_to(long_column(turned, 6), (SLOT, 128))
    leave_t = onehot_rows(long_column(turned, 0), BUS)
    flow0[...] = flow[...] * long_column(turned, 2)
    near0[...] = narrow(dot(leave_t, narrow(price[...])))
    cap[...] = jnp.broadcast_to(long_column(turned, 4), (SLOT, HOUR))
    leave[...] = leave_t


def season_block(sums, level, dual_f, link_column):
    lane = iota((128, 128), 1)
    tail = jnp.concatenate([level[:, HOUR - 1 : HOUR], dual_f[:, HOUR - 1 : HOUR]], axis=0)
    head = jnp.concatenate([dual_f[:, 0:1], link_column], axis=0)
    held = jnp.where(
        lane == 0,
        sums[:128],
        jnp.where(lane == 1, sums[128:], jnp.where(lane == 2, tail, jnp.where(lane == 3, head, 0.0))),
    )
    return jnp.transpose(held)[0:8]


def season_out(*refs):
    sources, (sent, turn, avail, scarcity, soc, soc_dual, link, sems) = refs[:5], refs[5:]
    fetch(sources, (avail, scarcity, soc, soc_dual, link), sems)
    turn[0:1, 0:BUS] = wide(link[...])
    turned = columns(turn)
    sums = jnp.sum(wide(avail[...]) * wide(narrow(scarcity[...])), axis=1, keepdims=True)
    sent[...] = season_block(sums, soc[...], wide(narrow(soc_dual[...])), turned[:BUS, 0:1])


def season_with_ends(rows, ends, sent):
    gathered = jnp.sum(ends[...], axis=0, keepdims=True)
    held = jnp.where(iota((8, 128), 0) == 4, gathered, rows[...])
    for s in range(SEASONS):
        sent[s] = held


def ends_in(got, source, price, flow0, near0, sent, arrive, cap):
    lane = wide(iota((SLOT, 128), 1))
    spot = source[...]
    ends = jnp.zeros((SLOT, 128), F32)
    limit = jnp.zeros((SLOT, 128), F32)
    for s in range(SEASONS):
        row = got[s, 4:5]
        ends = jnp.where(lane + 128 * s == spot, row, ends)
        limit = jnp.where(lane + (128 * s - LINK_CAP) == spot, row, limit)
    ends = jnp.sum(ends, axis=1, keepdims=True)
    limit = jnp.sum(limit, axis=1, keepdims=True)
    arrive_t = onehot_rows(ends, BUS)
    far = narrow(dot(arrive_t, narrow(price[...])))
    arrive[...] = arrive_t
    cap[...] = jnp.broadcast_to(limit, (SLOT, HOUR))
    pack(narrow(flow0[...]), near0[...], far, sent, WITH_FLOWS)


def line_step(flows, push, cap, tau):
    moved = jnp.clip(flows + tau * push, -cap, cap)
    return moved, extrapolate(moved, flows)


def tree(values):
    while len(values) > 1:
        values = [values[i] + values[i + 1] for i in range(0, len(values), 2)]
    return values[0]


def local_step(season, consts, state, price_v, got, turn, tau, sigma, disp_push=None):
    avail, asset_bus, run_cost, build_cost, efficiency, power, energy, link = consts
    disp, build, disch, level, scarce, sdual = state
    before_at = (season + SEASONS - 1) & (SEASONS - 1)
    after_at = (season + 1) & (SEASONS - 1)
    sums = tree([got[s, 0:2] for s in range(SEASONS)])
    grad_build = sums * (1.0 / (HOUR * SEASONS))
    build_new = jnp.maximum(build - tau * (build_cost[...] - grad_build), 0.0)
    turn[0:8, :] = got[before_at]
    turn[8:16, :] = got[after_at]
    turn[16:18, :] = wide(extrapolate(build_new, build))
    turn[18:20, :] = run_cost[...]
    turn[20:22, :] = wide(asset_bus[...])
    turn[22:23, 0:BUS] = efficiency[...]
    turn[23:24, 0:BUS] = power[...]
    turn[24:25, 0:BUS] = energy[...]
    turn[25:26, 0:BUS] = wide(link[...])
    turned = columns(turn)
    build_x = long_column(turned, 16)
    cost = long_column(turned, 18)
    asset_row = row256(asset_bus)
    asset_onehot = as_bf(iota((BUS, SLOT), 0) == asset_row)
    decay = turned[:BUS, 22:23]
    power_c = turned[:BUS, 23:24]
    energy_c = turned[:BUS, 24:25]
    link_c = turned[:BUS, 25:26]
    before_level, before_dual = turned[:BUS, 2:3], turned[BUS:, 2:3]
    before_first, before_link = turned[:BUS, 3:4], turned[BUS:, 3:4]
    after_first, after_link = turned[:BUS, 11:12], turned[BUS:, 11:12]
    price_b = narrow(price_v)
    dual_f = wide(narrow(sdual))
    if disp_push is None:
        asset_t = onehot_rows(long_column(turned, 20), BUS)
        disp_push = cost - (dot(asset_t, price_b) - wide(narrow(scarce)))
    grad_charge = wide(price_b) + dual_f
    first = dual_f[:, 0:1]
    after_last = (1.0 - link_c) * first + after_link * after_first
    following = jnp.concatenate([dual_f[:, 1:], after_last], axis=1)
    grad_soc = dual_f - decay * following
    before_grad = before_dual - decay * ((1.0 - before_link) * before_first + link_c * first)
    disp_new = jnp.maximum(disp - tau * disp_push, 0.0)
    disch_new = jnp.clip(disch + tau * grad_charge, -power_c, power_c)
    level_new = jnp.clip(level + tau * grad_soc, 0.0, energy_c)
    before_new = jnp.clip(before_level + tau * before_grad, 0.0, energy_c)
    disp_x = extrapolate(disp_new, disp)
    charge_f = wide(extrapolate(disch_new, disch))
    soc_f = wide(extrapolate(level_new, level))
    before_x = wide(extrapolate(before_new, before_level))
    balance = dot(asset_onehot, disp_x) + charge_f
    avail_rows = wide(avail[...]) * build_x - wide(disp_x)
    carried = jnp.where(link_c == 1.0, before_x, soc_f[:, HOUR - 1 : HOUR])
    previous = jnp.concatenate([carried, soc_f[:, : HOUR - 1]], axis=1)
    soc_rows = soc_f - decay * previous + charge_f
    scarce_new = jnp.maximum(scarce - sigma * avail_rows, 0.0)
    sdual_new = sdual - sigma * soc_rows
    halves = (
        mean(disp_new, disp),
        mean(build_new, build),
        mean(disch_new, disch),
        mean(level_new, level),
        mean(scarce_new, scarce),
        mean(sdual_new, sdual),
    )
    return balance, halves, link_c


def first_local(
    season, avail, asset_bus, run_cost, build_cost, efficiency, power, energy, link,
    disp, build, disch, level, scarce, sdual, price, got,
    disp1, build1, disch1, level1, scarce1, sdual1, balance, rows, moves, turn,
):
    consts = (avail, asset_bus, run_cost, build_cost, efficiency, power, energy, link)
    state = (disp[...], build[...], disch[...], level[...], scarce[...], sdual[...])
    local, halves, link_c = local_step(
        season[0], consts, state, price[...], got, turn, step_size, step_size
    )
    balance[...] = local
    for ref, value in zip((disp1, build1, disch1, level1, scarce1, sdual1), halves):
        ref[...] = value
    sums = jnp.sum(wide(avail[...]) * wide(narrow(halves[4])), axis=1, keepdims=True)
    rows[...] = season_block(sums, halves[3], wide(narrow(halves[5])), link_c)
    primal = (
        square(halves[0], state[0])
        + square(halves[1], state[1]) * (1.0 / SEASONS)
        + square(halves[2], state[2])
        + square(halves[3], state[3])
    )
    dual = square(halves[4], state[4]) + square(halves[5], state[5])
    lane = iota((8, 128), 1)
    moves[...] = jnp.where(lane == 0, primal, dual)


def price_step(
    flow0, near0, cap, leave, arrive, came_cap, got, demand, price, balance, moves,
    price1, flow1, came1, far1, sent,
):
    f0 = flow0[...]
    p0 = price[...]
    leave_t = leave[...]
    arrive_t = arrive[...]
    came0, came_near, far = unpack(got, WITH_FLOWS)
    came_far = dot(arrive_t, narrow(p0))
    came_moved, came_x = line_step(came0, came_far - came_near, came_cap[...], step_size)
    came1[...] = mean(came_moved, came0)
    moved, flow_x = line_step(f0, far - wide(near0[...]), cap[...], step_size)
    f1 = mean(moved, f0)
    flow1[...] = f1
    whole = balance[...] + dot_t(arrive_t, came_x) - dot_t(leave_t, flow_x)
    p1 = mean(p0 + step_size * (demand[...] - whole), p0)
    price1[...] = p1
    primal = moves[0:1, 0:1] + square(f1, f0)
    dual = moves[0:1, 1:2] + square(p1, p0)
    lane = iota((GROUP, 128), 1)
    held = jnp.zeros((GROUP, 128), F32)
    for at, value in ((0, primal), (3, dual)):
        for step, piece in enumerate(pieces(value)):
            held = jnp.where(lane == at + step, wide(piece), held)
    held = narrow(held)
    price_b = narrow(p1)
    near = narrow(dot(leave_t, price_b))
    far = narrow(dot(arrive_t, price_b))
    far1[...] = far
    pack(near, far, jnp.concatenate([held] * (REGIONS // GROUP), axis=0), sent, WITH_MOVES)


def moves_out(got, rows, sent):
    rows_each = sum(WITH_MOVES)
    shape = (8, REGIONS * rows_each)
    at = iota(shape, 1)
    q = lax.shift_right_logical(at * (262144 // rows_each + 1), 18)
    mask = as_bf(at - rows_each * q == 2 * LINK_CAP)
    moves = dot(mask, got[...])
    held = jnp.where(iota((8, 128), 0) == 4, moves, rows[...])
    for s in range(SEASONS):
        sent[s] = held


def pushes(
    lines_got, price, came_far, leave, asset_bus, run_cost, scarce,
    push, came_push, disp_push, turn,
):
    price_b = narrow(price[...])
    came_near, far, _ = unpack(lines_got, WITH_MOVES)
    push[...] = far - dot(leave[...], price_b)
    came_push[...] = wide(came_far[...]) - came_near
    turn[0:2, :] = run_cost[...]
    turn[2:4, :] = wide(asset_bus[...])
    turned = columns(turn)
    asset_t = onehot_rows(long_column(turned, 2), BUS)
    grad = dot(asset_t, price_b) - wide(narrow(scarce[...]))
    disp_push[...] = long_column(turned, 0) - grad


def second_step(
    season, avail, asset_bus, run_cost, build_cost, efficiency, power, energy, link,
    disp, build, disch, level, scarce, sdual, price, got, push, came_push, disp_push,
    arrive, came_cap, came, demand, flow, cap, leave,
    disp2, build2, flow2, disch2, level2, price2, scarce2, sdual2, turn,
):
    moves = tree([got[s, 4:5] for s in range(SEASONS)])
    primal = moves[:, 0:1] + moves[:, 1:2] + moves[:, 2:3]
    dual = moves[:, 3:4] + moves[:, 4:5] + moves[:, 5:6]
    weight = jnp.sqrt(jnp.sqrt((dual + 1e-06) / (primal + 1e-06)))
    tau = step_size / weight
    sigma = step_size * weight
    consts = (avail, asset_bus, run_cost, build_cost, efficiency, power, energy, link)
    state = (disp[...], build[...], disch[...], level[...], scarce[...], sdual[...])
    _, came_x = line_step(came[...], came_push[...], came_cap[...], tau)
    f1 = flow[...]
    p1 = price[...]
    leave_t = leave[...]
    moved, flow_x = line_step(f1, push[...], cap[...], tau)
    flow2[...] = mean(moved, f1)
    local, halves, _ = local_step(season[0], consts, state, p1, got, turn, tau, sigma, disp_push[...])
    whole = local + dot_t(arrive[...], came_x) - dot_t(leave_t, flow_x)
    price2[...] = mean(p1 + sigma * (demand[...] - whole), p1)
    for ref, value in zip((disp2, build2, disch2, level2, scarce2, sdual2), halves):
        ref[...] = value


def call(body, outs, *operands, scalars=0, turn=False, fetched=False):
    in_specs = [pl.BlockSpec(memory_space=pltpu.SMEM)] * scalars
    space = pltpu.HBM if fetched else pltpu.VMEM
    in_specs += [pl.BlockSpec(memory_space=space)] * (len(operands) - scalars)
    scratch = [pltpu.VMEM((128, 128), F32)] if turn else []
    if fetched:
        scratch += [pltpu.VMEM(v.shape, v.dtype) for v in operands[scalars:]]
        scratch += [pltpu.SemaphoreType.DMA((len(operands) - scalars,))]
    return pl.pallas_call(
        body,
        out_shape=[jax.ShapeDtypeStruct(shape, kind) for shape, kind in outs],
        in_specs=in_specs,
        out_specs=[pl.BlockSpec(memory_space=pltpu.VMEM)] * len(outs),
        scratch_shapes=scratch,
        compiler_params=pltpu.CompilerParams(vmem_limit_bytes=32 * 1024 * 1024),
    )(*operands)


def region_exchange(value, rows, per_pair):
    cut = value.reshape(REGIONS, per_pair, rows, HOUR)
    got = lax.all_to_all(cut, "region", split_axis=0, concat_axis=0, tiled=True)
    return got.reshape(value.shape)


def season_exchange(value):
    return lax.all_to_all(value, "season", split_axis=0, concat_axis=0, tiled=True)


def on_device(
    demand,
    avail,
    asset_bus,
    run_cost,
    build_cost,
    line_from,
    line_to,
    link_count,
    line_limit,
    efficiency,
    power_limit,
    energy_limit,
    season_link,
    dispatch,
    capacity,
    flow,
    charge,
    soc,
    price,
    scarcity,
    soc_dual,
):
    season = lax.axis_index("season").astype(I32).reshape(1)
    region = lax.axis_index("region").astype(I32).reshape(1)
    pair = lambda v: v.reshape(2, 128)
    short = lambda v: v.reshape(1, BUS)
    link = short(season_link)
    lines = ((SLOT, HOUR), F32)
    lines_b = ((SLOT, HOUR), BF16)
    buses = ((BUS, HOUR), F32)
    picks = ((SLOT, BUS), BF16)
    rows_of = lambda kinds: ((REGIONS * sum(kinds), HOUR), BF16)
    seasons = ((SEASONS, 8, 128), F32)
    pack_row = ((8, 128), F32)
    consts = (
        avail,
        pair(asset_bus),
        pair(run_cost),
        pair(build_cost),
        short(efficiency),
        short(power_limit),
        short(energy_limit),
        link,
    )
    limit = pair(line_limit)
    (sent1,) = call(
        ends_out,
        [((GROUP, 128), F32)],
        region,
        season,
        pair(line_to),
        limit,
        link_count,
        scalars=2,
        fetched=True,
    )
    got1 = lax.all_to_all(
        sent1.reshape(GROUP, 1, 128),
        ("region", "season"),
        0,
        0,
        axis_index_groups=coset_groups(),
        tiled=True,
    ).reshape(GROUP, 128)
    (rows1,) = call(season_out, [pack_row], avail, scarcity, soc, soc_dual, link, turn=True, fetched=True)
    flow0, near0, cap, leave, source = call(
        lines_near,
        [lines, lines_b, lines, picks, lines],
        region,
        flow,
        price,
        pair(line_from),
        limit,
        link_count,
        scalars=1,
        turn=True,
    )
    (sent_s,) = call(season_with_ends, [seasons], rows1, got1)
    season1 = season_exchange(sent_s)
    sent2, arrive, came_cap = call(
        ends_in, [rows_of(WITH_FLOWS), picks, lines], season1, source, price, flow0, near0
    )
    got2 = region_exchange(sent2, LINK_CAP, 3)
    disp1, build1, disch1, level1, scarce1, sdual1, balance, rows2, moves = call(
        first_local,
        [lines, ((2, 128), F32), buses, buses, lines, buses, buses, pack_row, pack_row],
        season,
        *consts,
        dispatch,
        pair(capacity),
        charge,
        soc,
        scarcity,
        soc_dual,
        price,
        season1,
        scalars=1,
        turn=True,
    )
    price1, flow1, came1, came_far1, sent3 = call(
        price_step,
        [buses, lines, lines, lines_b, rows_of(WITH_MOVES)],
        flow0,
        near0,
        cap,
        leave,
        arrive,
        came_cap,
        got2,
        demand,
        price,
        balance,
        moves,
    )
    got3 = region_exchange(sent3, 2, 5)
    (rows3,) = call(moves_out, [seasons], got3, rows2)
    season2 = season_exchange(rows3)
    push, came_push, disp_push = call(
        pushes,
        [lines, lines, lines],
        got3,
        price1,
        came_far1,
        leave,
        pair(asset_bus),
        pair(run_cost),
        scarce1,
        turn=True,
    )
    disp2, build2, flow2, disch2, level2, price2, scarce2, sdual2 = call(
        second_step,
        [lines, ((2, 128), F32), lines, buses, buses, buses, lines, buses],
        season,
        *consts,
        disp1,
        build1,
        disch1,
        level1,
        scarce1,
        sdual1,
        price1,
        season2,
        push,
        came_push,
        disp_push,
        arrive,
        came_cap,
        came1,
        demand,
        flow1,
        cap,
        leave,
        scalars=1,
        turn=True,
    )
    return (disp2, build2.reshape(capacity.shape), flow2, disch2, level2, price2, scarce2, sdual2)


def solution(mesh):
    both = P("region", "season")
    rows = P("region")
    in_specs = (
        both,
        both,
        rows,
        rows,
        rows,
        rows,
        rows,
        P("region", None),
        rows,
        rows,
        rows,
        rows,
        both,
        both,
        rows,
        both,
        both,
        both,
        both,
        both,
        both,
    )
    out_specs = (both, rows, both, both, both, both, both, both)
    return jax.shard_map(
        on_device, mesh=mesh, in_specs=in_specs, out_specs=out_specs, check_vma=False
    )
```

```python
import jax
import jax.numpy as jnp
from jax import lax
from jax.experimental import pallas as pl
from jax.experimental.pallas import tpu as pltpu
from jax.sharding import PartitionSpec as P

LINK_CAP = 4
GROUP = 16
step_size = 0.2
F32 = jnp.float32
BF16 = jnp.bfloat16
I32 = jnp.int32
REGIONS, SEASONS = 64, 8
BUS, SLOT, HOUR = 64, 256, 128
LINES = GROUP * LINK_CAP
ROWS_EACH = 2 * LINK_CAP + 2
PACKED = GROUP * ROWS_EACH
UNPACKED = 2 * LINES + GROUP


def iota(shape, axis):
    return lax.broadcasted_iota(I32, shape, axis)


def dot(a, b):
    return jnp.dot(a, b, preferred_element_type=F32)


def dot_t(a, b):
    return lax.dot_general(a, b, (((0,), (0,)), ((), ())), preferred_element_type=F32)


def as_bf(mask):
    return jnp.where(mask, 1.0, 0.0).astype(BF16)


def narrow(value):
    return value.astype(BF16)


def wide(value):
    return value.astype(F32)


def extrapolate(newer, older):
    return narrow(2.0 * newer - older)


def mean(newer, older):
    return 0.5 * (newer + older)


def total(value):
    return jnp.sum(jnp.sum(value, axis=1, keepdims=True), axis=0, keepdims=True)


def square(newer, older):
    moved = newer - older
    return total(moved * moved)


def row256(ref):
    return jnp.concatenate([ref[0:1, :], ref[1:2, :]], axis=1)


def flip_bits(value):
    flipped = value & 0
    for bit in range(6):
        flipped = flipped | (((value >> bit) & 1) << (5 - bit))
    return flipped


def region_at(place):
    return flip_bits(place ^ (place >> 1))


def place_of(region):
    place = flip_bits(region)
    for shift in (1, 2, 4):
        place = place ^ (place >> shift)
    return place


def order_out():
    shape = (SLOT, SLOT)
    slot = iota((1, SLOT), 1)
    return as_bf(iota(shape, 0) == LINK_CAP * place_of(slot >> 2) + (slot & 3))


def order_in():
    shape = (SLOT, SLOT)
    at = iota((1, SLOT), 1)
    return as_bf(iota(shape, 0) == LINK_CAP * region_at(at >> 2) + (at & 3))


def pack_target(packed):
    q = (packed * (262144 // ROWS_EACH + 1)) >> 18
    j = packed - ROWS_EACH * q
    first = LINK_CAP * q + j
    second = LINES + first - LINK_CAP
    third = jnp.where(j == 2 * LINK_CAP, 2 * LINES + q, -1)
    return jnp.where(j < LINK_CAP, first, jnp.where(j < 2 * LINK_CAP, second, third))


def pack(first, second, third, out_ref):
    order = order_out()
    first = narrow(dot(order, first))
    second = narrow(dot(order, second))
    shape = (PACKED, UNPACKED)
    place = as_bf(pack_target(iota(shape, 0)) == iota(shape, 1))
    for g in range(REGIONS // GROUP):
        rows = jnp.concatenate(
            [
                first[g * LINES : (g + 1) * LINES],
                second[g * LINES : (g + 1) * LINES],
                third[g * GROUP : (g + 1) * GROUP],
            ],
            axis=0,
        )
        out_ref[g * PACKED : (g + 1) * PACKED, :] = narrow(dot(place, rows))


def unpack(ref):
    shape = (UNPACKED, PACKED)
    place = as_bf(pack_target(iota(shape, 1)) == iota(shape, 0))
    parts = [
        narrow(dot(place, ref[g * PACKED : (g + 1) * PACKED, :])) for g in range(REGIONS // GROUP)
    ]
    order = order_in()
    first = jnp.concatenate([p[:LINES] for p in parts], axis=0)
    second = jnp.concatenate([p[LINES : 2 * LINES] for p in parts], axis=0)
    third = jnp.concatenate([p[2 * LINES :] for p in parts], axis=0)
    return dot(order, first), dot(order, second), third


def columns(ref):
    return jnp.transpose(ref[...])


def long_column(turned, at):
    return jnp.concatenate([turned[:, at : at + 1], turned[:, at + 1 : at + 2]], axis=0)


def onehot_rows(column, count):
    return as_bf(column == wide(iota((SLOT, count), 1)))


def lines_out(
    flow, price, line_from, line_to, line_limit, link_count,
    sent, flow0, near0, cap, leave, turn,
):
    lane = iota((1, SLOT), 1)
    spread = as_bf(iota((REGIONS, SLOT), 0) == lax.shift_right_logical(iota((REGIONS, SLOT), 1), 2))
    counts = jnp.broadcast_to(narrow(wide(link_count[...])), (8, REGIONS))
    counts = dot(counts, spread)[0:1]
    live = jnp.where(wide(lane & (LINK_CAP - 1)) < counts, 1.0, 0.0)
    limit = row256(line_limit) * live
    turn[0:2, :] = wide(line_from[...])
    turn[2:3, :] = live[:, :128]
    turn[3:4, :] = live[:, 128:]
    turn[4:5, :] = limit[:, :128]
    turn[5:6, :] = limit[:, 128:]
    turned = columns(turn)
    leave_t = onehot_rows(long_column(turned, 0), BUS)
    f0 = flow[...] * long_column(turned, 2)
    near = narrow(dot(leave_t, narrow(price[...])))
    flow0[...] = f0
    near0[...] = near
    cap[...] = jnp.broadcast_to(long_column(turned, 4), (SLOT, HOUR))
    leave[...] = leave_t
    high = wide(narrow(limit))
    low = limit - high
    sending = as_bf(
        iota((REGIONS, SLOT), 0) == place_of(iota((1, SLOT), 1) >> 2)
    )
    held = jnp.zeros((REGIONS, 128), F32)
    slot_kind = iota((SLOT, 128), 0) & (LINK_CAP - 1)
    for at, value in enumerate((wide(row256(line_to)), high, low)):
        spots = as_bf(iota((SLOT, 128), 1) == slot_kind + LINK_CAP * at)
        held = held + dot(sending * narrow(value), spots)
    pack(narrow(f0), near, narrow(held), sent)


def season_block(sums, level, dual_f, link_column):
    lane = iota((128, 128), 1)
    tail = jnp.concatenate([level[:, HOUR - 1 : HOUR], dual_f[:, HOUR - 1 : HOUR]], axis=0)
    head = jnp.concatenate([dual_f[:, 0:1], link_column], axis=0)
    held = jnp.where(
        lane == 0,
        sums[:128],
        jnp.where(lane == 1, sums[128:], jnp.where(lane == 2, tail, jnp.where(lane == 3, head, 0.0))),
    )
    return jnp.transpose(held)[0:8]


def season_out(avail, scarcity, soc, soc_dual, link, sent, turn):
    turn[0:1, 0:BUS] = wide(link[...])
    turned = columns(turn)
    sums = jnp.sum(wide(avail[...]) * wide(narrow(scarcity[...])), axis=1, keepdims=True)
    rows = season_block(sums, soc[...], wide(narrow(soc_dual[...])), turned[:BUS, 0:1])
    for s in range(SEASONS):
        sent[s] = rows


def ends_in(got, price, sent, far, arrive, cap):
    _, _, held = unpack(got)
    shape = (SLOT, REGIONS)
    spread = as_bf(region_at(iota((1, REGIONS), 1)) == iota(shape, 0) >> 2)
    lines = dot(spread, held)
    lane = iota((SLOT, 128), 1)
    kind = iota((SLOT, 128), 0) & (LINK_CAP - 1)
    ends = jnp.sum(jnp.where(lane == kind, lines, 0.0), axis=1, keepdims=True)
    limits = (lane == kind + LINK_CAP) | (lane == kind + 2 * LINK_CAP)
    limit = jnp.sum(jnp.where(limits, lines, 0.0), axis=1, keepdims=True)
    arrive_t = onehot_rows(ends, BUS)
    values = narrow(dot(arrive_t, narrow(price[...])))
    far[...] = values
    sent[...] = narrow(dot(order_out(), values))
    arrive[...] = arrive_t
    cap[...] = jnp.broadcast_to(limit, (SLOT, HOUR))


def line_step(flows, near, far, cap, tau):
    moved = jnp.clip(flows + tau * (far - near), -cap, cap)
    return moved, extrapolate(moved, flows)


def local_step(season, consts, state, price_v, got, turn, tau, sigma):
    avail, asset_bus, run_cost, build_cost, efficiency, power, energy, link = consts
    disp, build, disch, level, scarce, sdual = state
    before_at = (season + SEASONS - 1) & (SEASONS - 1)
    after_at = (season + 1) & (SEASONS - 1)
    sums = got[0, 0:2]
    for s in range(1, SEASONS):
        sums = sums + got[s, 0:2]
    grad_build = sums * (1.0 / (HOUR * SEASONS))
    build_new = jnp.maximum(build - tau * (build_cost[...] - grad_build), 0.0)
    turn[0:8, :] = got[before_at]
    turn[8:16, :] = got[after_at]
    turn[16:18, :] = wide(extrapolate(build_new, build))
    turn[18:20, :] = run_cost[...]
    turn[20:22, :] = wide(asset_bus[...])
    turn[22:23, 0:BUS] = efficiency[...]
    turn[23:24, 0:BUS] = power[...]
    turn[24:25, 0:BUS] = energy[...]
    turn[25:26, 0:BUS] = wide(link[...])
    turned = columns(turn)
    build_x = long_column(turned, 16)
    cost = long_column(turned, 18)
    asset_t = onehot_rows(long_column(turned, 20), BUS)
    asset_row = row256(asset_bus)
    asset_onehot = as_bf(iota((BUS, SLOT), 0) == asset_row)
    decay = turned[:BUS, 22:23]
    power_c = turned[:BUS, 23:24]
    energy_c = turned[:BUS, 24:25]
    link_c = turned[:BUS, 25:26]
    before_level, before_dual = turned[:BUS, 2:3], turned[BUS:, 2:3]
    before_first, before_link = turned[:BUS, 3:4], turned[BUS:, 3:4]
    after_first, after_link = turned[:BUS, 11:12], turned[BUS:, 11:12]
    price_b = narrow(price_v)
    dual_f = wide(narrow(sdual))
    grad_dispatch = dot(asset_t, price_b) - wide(narrow(scarce))
    grad_charge = wide(price_b) + dual_f
    first = dual_f[:, 0:1]
    after_last = (1.0 - link_c) * first + after_link * after_first
    following = jnp.concatenate([dual_f[:, 1:], after_last], axis=1)
    grad_soc = dual_f - decay * following
    before_grad = before_dual - decay * ((1.0 - before_link) * before_first + link_c * first)
    disp_new = jnp.maximum(disp - tau * (cost - grad_dispatch), 0.0)
    disch_new = jnp.clip(disch + tau * grad_charge, -power_c, power_c)
    level_new = jnp.clip(level + tau * grad_soc, 0.0, energy_c)
    before_new = jnp.clip(before_level + tau * before_grad, 0.0, energy_c)
    disp_x = extrapolate(disp_new, disp)
    charge_f = wide(extrapolate(disch_new, disch))
    soc_f = wide(extrapolate(level_new, level))
    before_x = wide(extrapolate(before_new, before_level))
    balance = dot(asset_onehot, disp_x) + charge_f
    avail_rows = wide(avail[...]) * build_x - wide(disp_x)
    carried = jnp.where(link_c == 1.0, before_x, soc_f[:, HOUR - 1 : HOUR])
    previous = jnp.concatenate([carried, soc_f[:, : HOUR - 1]], axis=1)
    soc_rows = soc_f - decay * previous + charge_f
    scarce_new = jnp.maximum(scarce - sigma * avail_rows, 0.0)
    sdual_new = sdual - sigma * soc_rows
    halves = (
        mean(disp_new, disp),
        mean(build_new, build),
        mean(disch_new, disch),
        mean(level_new, level),
        mean(scarce_new, scarce),
        mean(sdual_new, sdual),
    )
    return balance, halves, link_c


def first_local(
    season, avail, asset_bus, run_cost, build_cost, efficiency, power, energy, link,
    disp, build, disch, level, scarce, sdual, price, got, lines_got, arrive, cap, far,
    disp1, build1, disch1, level1, scarce1, sdual1, came1, balance, rows, moves, turn,
):
    consts = (avail, asset_bus, run_cost, build_cost, efficiency, power, energy, link)
    state = (disp[...], build[...], disch[...], level[...], scarce[...], sdual[...])
    came0, near, _ = unpack(lines_got)
    moved, came_x = line_step(came0, near, wide(far[...]), cap[...], step_size)
    came1[...] = mean(moved, came0)
    local, halves, link_c = local_step(
        season[0], consts, state, price[...], got, turn, step_size, step_size
    )
    balance[...] = local + dot_t(arrive[...], came_x)
    for ref, value in zip((disp1, build1, disch1, level1, scarce1, sdual1), halves):
        ref[...] = value
    sums = jnp.sum(wide(avail[...]) * wide(narrow(halves[4])), axis=1, keepdims=True)
    rows[...] = season_block(sums, halves[3], wide(narrow(halves[5])), link_c)
    primal = (
        square(halves[0], state[0])
        + square(halves[1], state[1]) * (1.0 / SEASONS)
        + square(halves[2], state[2])
        + square(halves[3], state[3])
    )
    dual = square(halves[4], state[4]) + square(halves[5], state[5])
    lane = iota((8, 128), 1)
    moves[...] = jnp.where(lane == 0, primal, dual)


def price_step(
    flow0, near0, cap, leave, arrive, got, demand, price, balance, moves,
    price1, flow1, far0, sent,
):
    f0 = flow0[...]
    leave_t = leave[...]
    far = dot(order_in(), got[...])
    moved, flow_x = line_step(f0, wide(near0[...]), far, cap[...], step_size)
    f1 = mean(moved, f0)
    flow1[...] = f1
    p0 = price[...]
    whole = balance[...] - dot_t(leave_t, flow_x)
    p1 = mean(p0 + step_size * (demand[...] - whole), p0)
    price1[...] = p1
    primal = moves[0:1, 0:1] + square(f1, f0)
    dual = moves[0:1, 1:2] + square(p1, p0)
    lane = iota((GROUP, 128), 1)
    held = jnp.zeros((GROUP, 128), F32)
    for at, value in ((0, primal), (3, dual)):
        for step in range(3):
            piece = wide(narrow(value))
            held = jnp.where(lane == at + step, piece, held)
            value = value - piece
    held = narrow(held)
    price_b = narrow(p1)
    near = narrow(dot(leave_t, price_b))
    far = narrow(dot(arrive[...], price_b))
    far0[...] = far
    pack(near, far, jnp.concatenate([held] * (REGIONS // GROUP), axis=0), sent)


def moves_out(got, rows, sent):
    at = iota((8, REGIONS * ROWS_EACH), 1)
    q = (at * (262144 // ROWS_EACH + 1)) >> 18
    mask = as_bf(at - ROWS_EACH * q == 2 * LINK_CAP)
    moves = dot(mask, got[...])
    held = jnp.where(iota((8, 128), 0) == 4, moves, rows[...])
    for s in range(SEASONS):
        sent[s] = held


def second_step(
    season, avail, asset_bus, run_cost, build_cost, efficiency, power, energy, link,
    disp, build, disch, level, scarce, sdual, price, got, lines_got, arrive, came_cap,
    came_far, came, demand, flow, cap, leave,
    disp2, build2, flow2, disch2, level2, price2, scarce2, sdual2, turn,
):
    moves = got[0, 4:5]
    for s in range(1, SEASONS):
        moves = moves + got[s, 4:5]
    primal = moves[:, 0:1] + moves[:, 1:2] + moves[:, 2:3]
    dual = moves[:, 3:4] + moves[:, 4:5] + moves[:, 5:6]
    weight = jnp.sqrt(jnp.sqrt((dual + 1e-06) / (primal + 1e-06)))
    tau = step_size / weight
    sigma = step_size * weight
    consts = (avail, asset_bus, run_cost, build_cost, efficiency, power, energy, link)
    state = (disp[...], build[...], disch[...], level[...], scarce[...], sdual[...])
    came_near, far, _ = unpack(lines_got)
    _, came_x = line_step(came[...], came_near, wide(came_far[...]), came_cap[...], tau)
    f1 = flow[...]
    p1 = price[...]
    leave_t = leave[...]
    near = dot(leave_t, narrow(p1))
    moved, flow_x = line_step(f1, near, far, cap[...], tau)
    flow2[...] = mean(moved, f1)
    local, halves, _ = local_step(season[0], consts, state, p1, got, turn, tau, sigma)
    whole = local + dot_t(arrive[...], came_x) - dot_t(leave_t, flow_x)
    price2[...] = mean(p1 + sigma * (demand[...] - whole), p1)
    for ref, value in zip((disp2, build2, disch2, level2, scarce2, sdual2), halves):
        ref[...] = value


def call(body, outs, *operands, scalar=False, turn=False):
    in_specs = [pl.BlockSpec(memory_space=pltpu.VMEM)] * len(operands)
    if scalar:
        in_specs[0] = pl.BlockSpec(memory_space=pltpu.SMEM)
    return pl.pallas_call(
        body,
        out_shape=[jax.ShapeDtypeStruct(shape, kind) for shape, kind in outs],
        in_specs=in_specs,
        out_specs=[pl.BlockSpec(memory_space=pltpu.VMEM)] * len(outs),
        scratch_shapes=[pltpu.VMEM((128, 128), F32)] if turn else [],
        compiler_params=pltpu.CompilerParams(vmem_limit_bytes=32 * 1024 * 1024),
    )(*operands)


def region_exchange(value, rows, per_pair):
    cut = value.reshape(REGIONS, per_pair, rows, HOUR)
    members = [[region_at(place) for place in range(REGIONS)]]
    got = lax.all_to_all(cut, "region", 0, 0, axis_index_groups=members, tiled=True)
    return got.reshape(value.shape)


def season_exchange(value):
    return lax.all_to_all(value, "season", split_axis=0, concat_axis=0, tiled=True)


def on_device(
    demand,
    avail,
    asset_bus,
    run_cost,
    build_cost,
    line_from,
    line_to,
    link_count,
    line_limit,
    efficiency,
    power_limit,
    energy_limit,
    season_link,
    dispatch,
    capacity,
    flow,
    charge,
    soc,
    price,
    scarcity,
    soc_dual,
):
    season = lax.axis_index("season").astype(I32).reshape(1)
    pair = lambda v: v.reshape(2, 128)
    short = lambda v: v.reshape(1, BUS)
    link = short(season_link)
    lines = ((SLOT, HOUR), F32)
    lines_b = ((SLOT, HOUR), BF16)
    buses = ((BUS, HOUR), F32)
    picks = ((SLOT, BUS), BF16)
    packed = ((REGIONS * ROWS_EACH, HOUR), BF16)
    seasons = ((SEASONS, 8, 128), F32)
    consts = (
        avail,
        pair(asset_bus),
        pair(run_cost),
        pair(build_cost),
        short(efficiency),
        short(power_limit),
        short(energy_limit),
        link,
    )
    sent1, flow0, near0, cap, leave = call(
        lines_out,
        [packed, lines, lines_b, lines, picks],
        flow,
        price,
        pair(line_from),
        pair(line_to),
        pair(line_limit),
        link_count,
        turn=True,
    )
    got1 = region_exchange(sent1, 2, 5)
    (rows1,) = call(season_out, [seasons], avail, scarcity, soc, soc_dual, link, turn=True)
    season1 = season_exchange(rows1)
    sent2, came_far0, arrive, came_cap = call(
        ends_in, [lines_b, lines_b, picks, lines], got1, price
    )
    got2 = region_exchange(sent2, LINK_CAP, 1)
    disp1, build1, disch1, level1, scarce1, sdual1, came1, balance, rows2, moves = call(
        first_local,
        [lines, ((2, 128), F32), buses, buses, lines, buses, lines, buses, ((8, 128), F32), ((8, 128), F32)],
        season,
        *consts,
        dispatch,
        pair(capacity),
        charge,
        soc,
        scarcity,
        soc_dual,
        price,
        season1,
        got1,
        arrive,
        came_cap,
        came_far0,
        scalar=True,
        turn=True,
    )
    price1, flow1, came_far1, sent3 = call(
        price_step,
        [buses, lines, lines_b, packed],
        flow0,
        near0,
        cap,
        leave,
        arrive,
        got2,
        demand,
        price,
        balance,
        moves,
    )
    got3 = region_exchange(sent3, 2, 5)
    (rows3,) = call(moves_out, [seasons], got3, rows2)
    season2 = season_exchange(rows3)
    disp2, build2, flow2, disch2, level2, price2, scarce2, sdual2 = call(
        second_step,
        [lines, ((2, 128), F32), lines, buses, buses, buses, lines, buses],
        season,
        *consts,
        disp1,
        build1,
        disch1,
        level1,
        scarce1,
        sdual1,
        price1,
        season2,
        got3,
        arrive,
        came_cap,
        came_far1,
        came1,
        demand,
        flow1,
        cap,
        leave,
        scalar=True,
        turn=True,
    )
    return (disp2, build2.reshape(capacity.shape), flow2, disch2, level2, price2, scarce2, sdual2)


def solution(mesh):
    both = P("region", "season")
    rows = P("region")
    in_specs = (
        both,
        both,
        rows,
        rows,
        rows,
        rows,
        rows,
        P("region", None),
        rows,
        rows,
        rows,
        rows,
        both,
        both,
        rows,
        both,
        both,
        both,
        both,
        both,
        both,
    )
    out_specs = (both, rows, both, both, both, both, both, both)
    return jax.shard_map(
        on_device, mesh=mesh, in_specs=in_specs, out_specs=out_specs, check_vma=False
    )
```

```python
import jax
import jax.numpy as jnp
from jax import lax
from jax.experimental import pallas as pl
from jax.experimental.pallas import tpu as pltpu
from jax.sharding import PartitionSpec as P

LINK_CAP = 4
GROUP = 16
step_size = 0.2
F32 = jnp.float32
BF16 = jnp.bfloat16
I32 = jnp.int32
REGIONS, SEASONS = 64, 8
BUS, SLOT, HOUR = 64, 256, 128
LINES = GROUP * LINK_CAP
HALF = 64
WITH_FLOWS = (LINK_CAP, LINK_CAP, LINK_CAP, 1, 1)
WITH_MOVES = (LINK_CAP, LINK_CAP, 1, 1)


def iota(shape, axis):
    return lax.broadcasted_iota(I32, shape, axis)


def dot(a, b):
    return jnp.dot(a, b, preferred_element_type=F32)


def dot_t(a, b):
    return lax.dot_general(a, b, (((0,), (0,)), ((), ())), preferred_element_type=F32)


def as_bf(mask):
    return jnp.where(mask, 1.0, 0.0).astype(BF16)


def narrow(value):
    return value.astype(BF16)


def wide(value):
    return value.astype(F32)


def extrapolate(newer, older):
    return narrow(2.0 * newer - older)


def mean(newer, older):
    return 0.5 * (newer + older)


def total(value):
    return jnp.sum(jnp.sum(value, axis=1, keepdims=True), axis=0, keepdims=True)


def square(newer, older):
    moved = newer - older
    return total(moved * moved)


def row256(ref):
    return jnp.concatenate([ref[0:1, :], ref[1:2, :]], axis=1)


def pack_target(packed, kinds):
    rows = sum(kinds)
    q = (packed * (262144 // rows + 1)) >> 18
    j = packed - rows * q
    target = packed * 0 - 1
    row, held = 0, 0
    for count in kinds:
        inside = (j >= row) & (j < row + count)
        target = jnp.where(inside, held + count * q + j - row, target)
        row += count
        held += count * GROUP
    return target


def pack(parts, out_ref, kinds):
    size = GROUP * sum(kinds)
    place = as_bf(pack_target(iota((size, size), 0), kinds) == iota((size, size), 1))
    for g in range(REGIONS // GROUP):
        rows = jnp.concatenate(
            [part[g * n * GROUP : (g + 1) * n * GROUP] for part, n in zip(parts, kinds)], axis=0
        )
        out_ref[g * size : (g + 1) * size, :] = narrow(dot(place, rows))


def unpack(ref, kinds):
    size = GROUP * sum(kinds)
    place = as_bf(pack_target(iota((size, size), 1), kinds) == iota((size, size), 0))
    groups = [dot(place, ref[g * size : (g + 1) * size, :]) for g in range(REGIONS // GROUP)]
    parts = []
    held = 0
    for n in kinds:
        parts.append(jnp.concatenate([p[held : held + n * GROUP] for p in groups], axis=0))
        held += n * GROUP
    return parts


def pieces(value):
    parts = []
    for _ in range(3):
        part = narrow(value)
        parts.append(part)
        value = value - wide(part)
    return parts


def columns(ref):
    return jnp.transpose(ref[...])


def long_column(turned, at):
    return jnp.concatenate([turned[:, at : at + 1], turned[:, at + 1 : at + 2]], axis=0)


def onehot_rows(column, count):
    return as_bf(column == wide(iota((SLOT, count), 1)))


def live_limit(line_limit, link_count):
    shape = (REGIONS, SLOT)
    spread = as_bf(iota(shape, 0) == lax.shift_right_logical(iota(shape, 1), 2))
    counts = jnp.broadcast_to(narrow(wide(link_count[...])), (8, REGIONS))
    counts = dot(counts, spread)[0:1]
    kind = iota((1, SLOT), 1) & (LINK_CAP - 1)
    live = jnp.where(wide(kind) < counts, 1.0, 0.0)
    return spread, live, row256(line_limit) * live


def season_block(sums, level, dual_f, link_column):
    lane = iota((HALF, 128), 1)
    held = jnp.zeros((HALF, 128), F32)
    eighths = [sums[HALF * n : HALF * (n + 1)] for n in range(4)]
    eighths += [level[:, HOUR - 1 : HOUR], dual_f[:, HOUR - 1 : HOUR], dual_f[:, 0:1], link_column]
    for at, eighth in enumerate(eighths):
        held = jnp.where(lane == at, eighth, held)
    return jnp.transpose(jnp.concatenate([jnp.zeros((HALF, 128), F32), held], axis=0))[0:8]


def ends_out(
    line_to, line_limit, link_count, avail, scarcity, soc, soc_dual, link, sent, turn
):
    spread, _, limit = live_limit(line_limit, link_count)
    lane = iota((SLOT, 128), 1)
    kind = iota((SLOT, 128), 0) & (LINK_CAP - 1)
    held = dot(spread * narrow(wide(row256(line_to))), as_bf(lane == kind))
    spots = as_bf(lane == kind + LINK_CAP)
    for part in pieces(limit):
        held = held + dot(spread * part, spots)
    turn[0:1, 0:BUS] = wide(link[...])
    turned = columns(turn)
    sums = jnp.sum(wide(avail[...]) * wide(narrow(scarcity[...])), axis=1, keepdims=True)
    block = season_block(sums, soc[...], wide(narrow(soc_dual[...])), turned[:BUS, 0:1])
    eighth = iota((REGIONS, 128), 0) >> 3
    handed = jnp.zeros((REGIONS, 128), F32)
    for at in range(8):
        handed = jnp.where(eighth == at, block[at : at + 1], handed)
    sent[...] = jnp.where(iota((REGIONS, 128), 1) < HALF, held, handed)


def lines_near(
    flow, price, line_from, line_limit, link_count, flow0, near0, cap, leave, turn
):
    _, live, limit = live_limit(line_limit, link_count)
    turn[0:2, :] = wide(line_from[...])
    turn[2:3, :] = live[:, :128]
    turn[3:4, :] = live[:, 128:]
    turn[4:5, :] = limit[:, :128]
    turn[5:6, :] = limit[:, 128:]
    turned = columns(turn)
    leave_t = onehot_rows(long_column(turned, 0), BUS)
    flow0[...] = flow[...] * long_column(turned, 2)
    near0[...] = narrow(dot(leave_t, narrow(price[...])))
    cap[...] = jnp.broadcast_to(long_column(turned, 4), (SLOT, HOUR))
    leave[...] = leave_t


def ends_in(got, price, flow0, near0, sent, arrive, cap):
    shape = (SLOT, REGIONS)
    spread = as_bf(iota(shape, 1) == lax.shift_right_logical(iota(shape, 0), 2))
    high, middle, low = pieces(got[...])
    lines = dot(spread, high) + dot(spread, middle) + dot(spread, low)
    lane = iota((SLOT, 128), 1)
    kind = iota((SLOT, 128), 0) & (LINK_CAP - 1)
    ends = jnp.sum(jnp.where(lane == kind, lines, 0.0), axis=1, keepdims=True)
    limit = jnp.sum(jnp.where(lane == kind + LINK_CAP, lines, 0.0), axis=1, keepdims=True)
    arrive_t = onehot_rows(ends, BUS)
    far = narrow(dot(arrive_t, narrow(price[...])))
    arrive[...] = arrive_t
    cap[...] = jnp.broadcast_to(limit, (SLOT, HOUR))
    turned = jnp.concatenate([wide(middle)[:, HALF:], wide(middle)[:, :HALF]], axis=1)
    handed = iota((REGIONS, 128), 1) >= HALF
    both = narrow(jnp.where(handed, wide(high), turned))
    rest = narrow(jnp.where(handed, wide(low), 0.0))
    pack((narrow(flow0[...]), near0[...], far, both, rest), sent, WITH_FLOWS)


def season_blocks(region, season, both, rest, got):
    shape = (REGIONS, REGIONS)
    row = iota(shape, 0)
    offset = season + region - (row >> 3)
    order = as_bf(8 * (row & 7) + (offset & 7) == iota(shape, 1))
    parts = dot(order, narrow(both))
    middle = jnp.concatenate([parts[:, HALF:], parts[:, :HALF]], axis=1)
    value = parts + middle + dot(order, narrow(rest))
    for s in range(SEASONS):
        got[s] = value[8 * s : 8 * s + 8]


def line_step(flows, near, far, cap, tau):
    moved = jnp.clip(flows + tau * (far - near), -cap, cap)
    return moved, extrapolate(moved, flows)


def tree(values):
    while len(values) > 1:
        values = [values[i] + values[i + 1] for i in range(0, len(values), 2)]
    return values[0]


def local_step(season, consts, state, price_v, got, turn, tau, sigma):
    avail, asset_bus, run_cost, build_cost, efficiency, power, energy, link = consts
    disp, build, disch, level, scarce, sdual = state
    before_at = (season + SEASONS - 1) & (SEASONS - 1)
    after_at = (season + 1) & (SEASONS - 1)
    parts = tree([got[s, 0:4] for s in range(SEASONS)])
    moved = jnp.concatenate([parts[:, HALF:], parts[:, :HALF]], axis=1)
    left = iota((1, 128), 1) < HALF
    sums = jnp.concatenate(
        [jnp.where(left, moved[n : n + 1], parts[n + 1 : n + 2]) for n in (0, 2)], axis=0
    )
    grad_build = sums * (1.0 / (HOUR * SEASONS))
    build_new = jnp.maximum(build - tau * (build_cost[...] - grad_build), 0.0)
    turn[0:8, :] = got[before_at]
    turn[8:16, :] = got[after_at]
    turn[16:18, :] = wide(extrapolate(build_new, build))
    turn[18:20, :] = run_cost[...]
    turn[20:22, :] = wide(asset_bus[...])
    turn[22:23, 0:BUS] = efficiency[...]
    turn[23:24, 0:BUS] = power[...]
    turn[24:25, 0:BUS] = energy[...]
    turn[25:26, 0:BUS] = wide(link[...])
    turned = columns(turn)
    build_x = long_column(turned, 16)
    cost = long_column(turned, 18)
    asset_t = onehot_rows(long_column(turned, 20), BUS)
    asset_row = row256(asset_bus)
    asset_onehot = as_bf(iota((BUS, SLOT), 0) == asset_row)
    decay = turned[:BUS, 22:23]
    power_c = turned[:BUS, 23:24]
    energy_c = turned[:BUS, 24:25]
    link_c = turned[:BUS, 25:26]
    before_level, before_dual = turned[HALF:, 4:5], turned[HALF:, 5:6]
    before_first, before_link = turned[HALF:, 6:7], turned[HALF:, 7:8]
    after_first, after_link = turned[HALF:, 14:15], turned[HALF:, 15:16]
    price_b = narrow(price_v)
    dual_f = wide(narrow(sdual))
    grad_dispatch = dot(asset_t, price_b) - wide(narrow(scarce))
    grad_charge = wide(price_b) + dual_f
    first = dual_f[:, 0:1]
    after_last = (1.0 - link_c) * first + after_link * after_first
    following = jnp.concatenate([dual_f[:, 1:], after_last], axis=1)
    grad_soc = dual_f - decay * following
    before_grad = before_dual - decay * ((1.0 - before_link) * before_first + link_c * first)
    disp_new = jnp.maximum(disp - tau * (cost - grad_dispatch), 0.0)
    disch_new = jnp.clip(disch + tau * grad_charge, -power_c, power_c)
    level_new = jnp.clip(level + tau * grad_soc, 0.0, energy_c)
    before_new = jnp.clip(before_level + tau * before_grad, 0.0, energy_c)
    disp_x = extrapolate(disp_new, disp)
    charge_f = wide(extrapolate(disch_new, disch))
    soc_f = wide(extrapolate(level_new, level))
    before_x = wide(extrapolate(before_new, before_level))
    balance = dot(asset_onehot, disp_x) + charge_f
    avail_rows = wide(avail[...]) * build_x - wide(disp_x)
    carried = jnp.where(link_c == 1.0, before_x, soc_f[:, HOUR - 1 : HOUR])
    previous = jnp.concatenate([carried, soc_f[:, : HOUR - 1]], axis=1)
    soc_rows = soc_f - decay * previous + charge_f
    scarce_new = jnp.maximum(scarce - sigma * avail_rows, 0.0)
    sdual_new = sdual - sigma * soc_rows
    halves = (
        mean(disp_new, disp),
        mean(build_new, build),
        mean(disch_new, disch),
        mean(level_new, level),
        mean(scarce_new, scarce),
        mean(sdual_new, sdual),
    )
    return balance, halves, link_c


def first_step(
    region, season, avail, asset_bus, run_cost, build_cost, efficiency, power, energy, link,
    disp, build, disch, level, scarce, sdual, price, lines_got, arrive, came_cap,
    demand, flow0, near0, cap, leave,
    disp1, build1, disch1, level1, scarce1, sdual1, price1, flow1, came1, far1, rows, sent,
    turn, got,
):
    f0 = flow0[...]
    p0 = price[...]
    leave_t = leave[...]
    arrive_t = arrive[...]
    came0, came_near, far, both, rest = unpack(lines_got, WITH_FLOWS)
    season_blocks(region[0], season[0], both, rest, got)
    came_far = dot(arrive_t, narrow(p0))
    came_moved, came_x = line_step(came0, came_near, came_far, came_cap[...], step_size)
    came1[...] = mean(came_moved, came0)
    moved, flow_x = line_step(f0, wide(near0[...]), far, cap[...], step_size)
    f1 = mean(moved, f0)
    flow1[...] = f1
    consts = (avail, asset_bus, run_cost, build_cost, efficiency, power, energy, link)
    state = (disp[...], build[...], disch[...], level[...], scarce[...], sdual[...])
    local, halves, link_c = local_step(
        season[0], consts, state, p0, got, turn, step_size, step_size
    )
    for ref, value in zip((disp1, build1, disch1, level1, scarce1, sdual1), halves):
        ref[...] = value
    whole = local + dot_t(arrive_t, came_x) - dot_t(leave_t, flow_x)
    p1 = mean(p0 + step_size * (demand[...] - whole), p0)
    price1[...] = p1
    sums = jnp.sum(wide(avail[...]) * wide(narrow(halves[4])), axis=1, keepdims=True)
    rows[...] = season_block(sums, halves[3], wide(narrow(halves[5])), link_c)
    primal = (
        square(halves[0], state[0])
        + square(halves[1], state[1]) * (1.0 / SEASONS)
        + square(halves[2], state[2])
        + square(halves[3], state[3])
        + square(f1, f0)
    )
    dual = square(halves[4], state[4]) + square(halves[5], state[5]) + square(p1, p0)
    lane = iota((REGIONS, 128), 1)
    held = jnp.zeros((REGIONS, 128), F32)
    for at, value in ((0, primal), (3, dual)):
        for step, piece in enumerate(pieces(value)):
            held = jnp.where(lane == at + step, wide(piece), held)
    held = narrow(held)
    price_b = narrow(p1)
    near = narrow(dot(leave_t, price_b))
    far = narrow(dot(arrive_t, price_b))
    far1[...] = far
    pack((near, far, held, jnp.zeros_like(held)), sent, WITH_MOVES)


def moves_out(got, rows, sent):
    rows_each = sum(WITH_MOVES)
    shape = (8, REGIONS * rows_each)
    at = iota(shape, 1)
    q = lax.shift_right_logical(at * (262144 // rows_each + 1), 18)
    mask = as_bf(at - rows_each * q == 2 * LINK_CAP)
    moves = dot(mask, got[...])
    spot = (iota((8, 128), 0) == 0) & (iota((8, 128), 1) < HALF)
    held = jnp.where(spot, moves, rows[...])
    for s in range(SEASONS):
        sent[s] = held


def second_step(
    season, avail, asset_bus, run_cost, build_cost, efficiency, power, energy, link,
    disp, build, disch, level, scarce, sdual, price, got, lines_got, arrive, came_cap,
    came_far, came, demand, flow, cap, leave,
    disp2, build2, flow2, disch2, level2, price2, scarce2, sdual2, turn,
):
    moves = tree([got[s, 0:1] for s in range(SEASONS)])
    primal = moves[:, 0:1] + moves[:, 1:2] + moves[:, 2:3]
    dual = moves[:, 3:4] + moves[:, 4:5] + moves[:, 5:6]
    weight = jnp.sqrt(jnp.sqrt((dual + 1e-06) / (primal + 1e-06)))
    tau = step_size / weight
    sigma = step_size * weight
    consts = (avail, asset_bus, run_cost, build_cost, efficiency, power, energy, link)
    state = (disp[...], build[...], disch[...], level[...], scarce[...], sdual[...])
    came_near, far, _, _ = unpack(lines_got, WITH_MOVES)
    _, came_x = line_step(came[...], came_near, wide(came_far[...]), came_cap[...], tau)
    f1 = flow[...]
    p1 = price[...]
    leave_t = leave[...]
    near = dot(leave_t, narrow(p1))
    moved, flow_x = line_step(f1, near, far, cap[...], tau)
    flow2[...] = mean(moved, f1)
    local, halves, _ = local_step(season[0], consts, state, p1, got, turn, tau, sigma)
    whole = local + dot_t(arrive[...], came_x) - dot_t(leave_t, flow_x)
    price2[...] = mean(p1 + sigma * (demand[...] - whole), p1)
    for ref, value in zip((disp2, build2, disch2, level2, scarce2, sdual2), halves):
        ref[...] = value


def call(body, outs, *operands, scalars=0, scratch=()):
    in_specs = [pl.BlockSpec(memory_space=pltpu.SMEM)] * scalars
    in_specs += [pl.BlockSpec(memory_space=pltpu.VMEM)] * (len(operands) - scalars)
    return pl.pallas_call(
        body,
        out_shape=[jax.ShapeDtypeStruct(shape, kind) for shape, kind in outs],
        in_specs=in_specs,
        out_specs=[pl.BlockSpec(memory_space=pltpu.VMEM)] * len(outs),
        scratch_shapes=[pltpu.VMEM(shape, F32) for shape in scratch],
        compiler_params=pltpu.CompilerParams(vmem_limit_bytes=32 * 1024 * 1024),
    )(*operands)


def mixed_exchange(value):
    members = [
        [SEASONS * r + (g + r) % SEASONS for r in range(REGIONS)] for g in range(SEASONS)
    ]
    got = lax.all_to_all(
        value.reshape(REGIONS, 1, 128),
        ("region", "season"),
        0,
        0,
        axis_index_groups=members,
        tiled=True,
    )
    return got.reshape(value.shape)


def region_exchange(value, rows, per_pair):
    cut = value.reshape(REGIONS, per_pair, rows, HOUR)
    got = lax.all_to_all(cut, "region", split_axis=0, concat_axis=0, tiled=True)
    return got.reshape(value.shape)


def season_exchange(value):
    return lax.all_to_all(value, "season", split_axis=0, concat_axis=0, tiled=True)


def on_device(
    demand,
    avail,
    asset_bus,
    run_cost,
    build_cost,
    line_from,
    line_to,
    link_count,
    line_limit,
    efficiency,
    power_limit,
    energy_limit,
    season_link,
    dispatch,
    capacity,
    flow,
    charge,
    soc,
    price,
    scarcity,
    soc_dual,
):
    season = lax.axis_index("season").astype(I32).reshape(1)
    region = lax.axis_index("region").astype(I32).reshape(1)
    pair = lambda v: v.reshape(2, 128)
    short = lambda v: v.reshape(1, BUS)
    link = short(season_link)
    lines = ((SLOT, HOUR), F32)
    lines_b = ((SLOT, HOUR), BF16)
    buses = ((BUS, HOUR), F32)
    picks = ((SLOT, BUS), BF16)
    rows_of = lambda kinds: ((REGIONS * sum(kinds), HOUR), BF16)
    seasons = ((SEASONS, 8, 128), F32)
    pack_row = ((8, 128), F32)
    consts = (
        avail,
        pair(asset_bus),
        pair(run_cost),
        pair(build_cost),
        short(efficiency),
        short(power_limit),
        short(energy_limit),
        link,
    )
    limit = pair(line_limit)
    turn = (128, 128)
    (sent1,) = call(
        ends_out,
        [((REGIONS, 128), F32)],
        pair(line_to),
        limit,
        link_count,
        avail,
        scarcity,
        soc,
        soc_dual,
        link,
        scratch=[turn],
    )
    got1 = mixed_exchange(sent1)
    flow0, near0, cap, leave = call(
        lines_near,
        [lines, lines_b, lines, picks],
        flow,
        price,
        pair(line_from),
        limit,
        link_count,
        scratch=[turn],
    )
    sent2, arrive, came_cap = call(
        ends_in, [rows_of(WITH_FLOWS), picks, lines], got1, price, flow0, near0
    )
    got2 = region_exchange(sent2, 2, 7)
    (
        disp1,
        build1,
        disch1,
        level1,
        scarce1,
        sdual1,
        price1,
        flow1,
        came1,
        came_far1,
        rows2,
        sent3,
    ) = call(
        first_step,
        [
            lines,
            ((2, 128), F32),
            buses,
            buses,
            lines,
            buses,
            buses,
            lines,
            lines,
            lines_b,
            pack_row,
            rows_of(WITH_MOVES),
        ],
        region,
        season,
        *consts,
        dispatch,
        pair(capacity),
        charge,
        soc,
        scarcity,
        soc_dual,
        price,
        got2,
        arrive,
        came_cap,
        demand,
        flow0,
        near0,
        cap,
        leave,
        scalars=2,
        scratch=[turn, (SEASONS, 8, 128)],
    )
    got3 = region_exchange(sent3, 2, 5)
    (rows3,) = call(moves_out, [seasons], got3, rows2)
    season2 = season_exchange(rows3)
    disp2, build2, flow2, disch2, level2, price2, scarce2, sdual2 = call(
        second_step,
        [lines, ((2, 128), F32), lines, buses, buses, buses, lines, buses],
        season,
        *consts,
        disp1,
        build1,
        disch1,
        level1,
        scarce1,
        sdual1,
        price1,
        season2,
        got3,
        arrive,
        came_cap,
        came_far1,
        came1,
        demand,
        flow1,
        cap,
        leave,
        scalars=1,
        scratch=[turn],
    )
    return (disp2, build2.reshape(capacity.shape), flow2, disch2, level2, price2, scarce2, sdual2)


def solution(mesh):
    both = P("region", "season")
    rows = P("region")
    in_specs = (
        both,
        both,
        rows,
        rows,
        rows,
        rows,
        rows,
        P("region", None),
        rows,
        rows,
        rows,
        rows,
        both,
        both,
        rows,
        both,
        both,
        both,
        both,
        both,
        both,
    )
    out_specs = (both, rows, both, both, both, both, both, both)
    return jax.shard_map(
        on_device, mesh=mesh, in_specs=in_specs, out_specs=out_specs, check_vma=False
    )
```

```python
import jax
import jax.numpy as jnp
from jax import lax
from jax.experimental import pallas as pl
from jax.experimental.pallas import tpu as pltpu
from jax.sharding import PartitionSpec as P

LINK_CAP = 4
GROUP = 16
step_size = 0.2
F32 = jnp.float32
BF16 = jnp.bfloat16
I32 = jnp.int32
REGIONS, SEASONS = 64, 8
BUS, SLOT, HOUR = 64, 256, 128
LINES = GROUP * LINK_CAP
ROWS_EACH = 2 * LINK_CAP + 2
PACKED = GROUP * ROWS_EACH
UNPACKED = 2 * LINES + GROUP


def iota(shape, axis):
    return lax.broadcasted_iota(I32, shape, axis)


def dot(a, b):
    return jnp.dot(a, b, preferred_element_type=F32)


def dot_t(a, b):
    return lax.dot_general(a, b, (((0,), (0,)), ((), ())), preferred_element_type=F32)


def as_bf(mask):
    return jnp.where(mask, 1.0, 0.0).astype(BF16)


def narrow(value):
    return value.astype(BF16)


def wide(value):
    return value.astype(F32)


def extrapolate(newer, older):
    return narrow(2.0 * newer - older)


def mean(newer, older):
    return 0.5 * (newer + older)


def total(value):
    return jnp.sum(jnp.sum(value, axis=1, keepdims=True), axis=0, keepdims=True)


def square(newer, older):
    moved = newer - older
    return total(moved * moved)


def row256(ref):
    return jnp.concatenate([ref[0:1, :], ref[1:2, :]], axis=1)


def pack_target(packed):
    q = (packed * (262144 // ROWS_EACH + 1)) >> 18
    j = packed - ROWS_EACH * q
    first = LINK_CAP * q + j
    second = LINES + first - LINK_CAP
    third = jnp.where(j == 2 * LINK_CAP, 2 * LINES + q, -1)
    return jnp.where(j < LINK_CAP, first, jnp.where(j < 2 * LINK_CAP, second, third))


def pack(first, second, third, out_ref):
    shape = (PACKED, UNPACKED)
    place = as_bf(pack_target(iota(shape, 0)) == iota(shape, 1))
    for g in range(REGIONS // GROUP):
        rows = jnp.concatenate(
            [
                first[g * LINES : (g + 1) * LINES],
                second[g * LINES : (g + 1) * LINES],
                third[g * GROUP : (g + 1) * GROUP],
            ],
            axis=0,
        )
        out_ref[g * PACKED : (g + 1) * PACKED, :] = narrow(dot(place, rows))


def unpack(ref):
    shape = (UNPACKED, PACKED)
    place = as_bf(pack_target(iota(shape, 1)) == iota(shape, 0))
    parts = [
        dot(place, ref[g * PACKED : (g + 1) * PACKED, :]) for g in range(REGIONS // GROUP)
    ]
    first = jnp.concatenate([p[:LINES] for p in parts], axis=0)
    second = jnp.concatenate([p[LINES : 2 * LINES] for p in parts], axis=0)
    third = jnp.concatenate([p[2 * LINES :] for p in parts], axis=0)
    return first, second, third


def columns(ref):
    return jnp.transpose(ref[...])


def long_column(turned, at):
    return jnp.concatenate([turned[:, at : at + 1], turned[:, at + 1 : at + 2]], axis=0)


def onehot_rows(column, count):
    return as_bf(column == wide(iota((SLOT, count), 1)))


def lines_out(
    flow, price, line_from, line_to, line_limit, link_count,
    sent, flow0, near0, cap, leave, turn,
):
    lane = iota((1, SLOT), 1)
    spread = as_bf(iota((REGIONS, SLOT), 0) == lax.shift_right_logical(iota((REGIONS, SLOT), 1), 2))
    counts = jnp.broadcast_to(narrow(wide(link_count[...])), (8, REGIONS))
    counts = dot(counts, spread)[0:1]
    live = jnp.where(wide(lane & (LINK_CAP - 1)) < counts, 1.0, 0.0)
    limit = row256(line_limit) * live
    turn[0:2, :] = wide(line_from[...])
    turn[2:3, :] = live[:, :128]
    turn[3:4, :] = live[:, 128:]
    turn[4:5, :] = limit[:, :128]
    turn[5:6, :] = limit[:, 128:]
    turned = columns(turn)
    leave_t = onehot_rows(long_column(turned, 0), BUS)
    f0 = flow[...] * long_column(turned, 2)
    near = narrow(dot(leave_t, narrow(price[...])))
    flow0[...] = f0
    near0[...] = near
    cap[...] = jnp.broadcast_to(long_column(turned, 4), (SLOT, HOUR))
    leave[...] = leave_t
    high = wide(narrow(limit))
    low = limit - high
    held = jnp.zeros((REGIONS, 128), F32)
    slot_kind = iota((SLOT, 128), 0) & (LINK_CAP - 1)
    for at, value in enumerate((wide(row256(line_to)), high, low)):
        spots = as_bf(iota((SLOT, 128), 1) == slot_kind + LINK_CAP * at)
        held = held + dot(spread * narrow(value), spots)
    pack(narrow(f0), near, narrow(held), sent)


def season_block(sums, level, dual_f, link_column):
    lane = iota((128, 128), 1)
    tail = jnp.concatenate([level[:, HOUR - 1 : HOUR], dual_f[:, HOUR - 1 : HOUR]], axis=0)
    head = jnp.concatenate([dual_f[:, 0:1], link_column], axis=0)
    held = jnp.where(
        lane == 0,
        sums[:128],
        jnp.where(lane == 1, sums[128:], jnp.where(lane == 2, tail, jnp.where(lane == 3, head, 0.0))),
    )
    return jnp.transpose(held)[0:8]


def season_out(season, avail, scarcity, soc, soc_dual, link, sent, turn):
    turn[0:1, 0:BUS] = wide(link[...])
    turned = columns(turn)
    sums = jnp.sum(wide(avail[...]) * wide(narrow(scarcity[...])), axis=1, keepdims=True)
    rows = season_block(sums, soc[...], wide(narrow(soc_dual[...])), turned[:BUS, 0:1])
    row = iota((8, 128), 0)
    sent[0:8] = jnp.where(row < 2, rows, 0.0)
    for half in range(2):
        own = season[0] - 4 * half
        halo = jnp.where((row & 1) == 0, rows[2:3], rows[3:4])
        sent[8 + 8 * half : 16 + 8 * half] = jnp.where((row >> 1) == own, halo, 0.0)


def ends_in(got, price, sent, arrive, cap):
    _, _, held = unpack(got)
    shape = (SLOT, REGIONS)
    spread = as_bf(iota(shape, 1) == iota(shape, 0) >> 2)
    lines = dot(spread, narrow(held))
    lane = iota((SLOT, 128), 1)
    kind = iota((SLOT, 128), 0) & (LINK_CAP - 1)
    ends = jnp.sum(jnp.where(lane == kind, lines, 0.0), axis=1, keepdims=True)
    limits = (lane == kind + LINK_CAP) | (lane == kind + 2 * LINK_CAP)
    limit = jnp.sum(jnp.where(limits, lines, 0.0), axis=1, keepdims=True)
    arrive_t = onehot_rows(ends, BUS)
    sent[...] = narrow(dot(arrive_t, narrow(price[...])))
    arrive[...] = arrive_t
    cap[...] = jnp.broadcast_to(limit, (SLOT, HOUR))


def line_step(flows, near, far, cap, tau):
    moved = jnp.clip(flows + tau * (far - near), -cap, cap)
    return moved, extrapolate(moved, flows)


def halo_of(got, season):
    rows = got[8:10]
    for s in range(1, SEASONS):
        rows = jnp.where(season == s, got[8 + 2 * s : 10 + 2 * s], rows)
    return rows


def tree(values):
    while len(values) > 1:
        values = [values[i] + values[i + 1] for i in range(0, len(values), 2)]
    return values[0]


def local_step(sums, before, after, consts, state, price_v, turn, tau, sigma):
    avail, asset_bus, run_cost, build_cost, efficiency, power, energy, link = consts
    disp, build, disch, level, scarce, sdual = state
    grad_build = sums * (1.0 / (HOUR * SEASONS))
    build_new = jnp.maximum(build - tau * (build_cost[...] - grad_build), 0.0)
    turn[2:4, :] = before
    turn[10:12, :] = after
    turn[16:18, :] = wide(extrapolate(build_new, build))
    turn[18:20, :] = run_cost[...]
    turn[20:22, :] = wide(asset_bus[...])
    turn[22:23, 0:BUS] = efficiency[...]
    turn[23:24, 0:BUS] = power[...]
    turn[24:25, 0:BUS] = energy[...]
    turn[25:26, 0:BUS] = wide(link[...])
    turned = columns(turn)
    build_x = long_column(turned, 16)
    cost = long_column(turned, 18)
    asset_t = onehot_rows(long_column(turned, 20), BUS)
    asset_row = row256(asset_bus)
    asset_onehot = as_bf(iota((BUS, SLOT), 0) == asset_row)
    decay = turned[:BUS, 22:23]
    power_c = turned[:BUS, 23:24]
    energy_c = turned[:BUS, 24:25]
    link_c = turned[:BUS, 25:26]
    before_level, before_dual = turned[:BUS, 2:3], turned[BUS:, 2:3]
    before_first, before_link = turned[:BUS, 3:4], turned[BUS:, 3:4]
    after_first, after_link = turned[:BUS, 11:12], turned[BUS:, 11:12]
    price_b = narrow(price_v)
    dual_f = wide(narrow(sdual))
    grad_dispatch = dot(asset_t, price_b) - wide(narrow(scarce))
    grad_charge = wide(price_b) + dual_f
    first = dual_f[:, 0:1]
    after_last = (1.0 - link_c) * first + after_link * after_first
    following = jnp.concatenate([dual_f[:, 1:], after_last], axis=1)
    grad_soc = dual_f - decay * following
    before_grad = before_dual - decay * ((1.0 - before_link) * before_first + link_c * first)
    disp_new = jnp.maximum(disp - tau * (cost - grad_dispatch), 0.0)
    disch_new = jnp.clip(disch + tau * grad_charge, -power_c, power_c)
    level_new = jnp.clip(level + tau * grad_soc, 0.0, energy_c)
    before_new = jnp.clip(before_level + tau * before_grad, 0.0, energy_c)
    disp_x = extrapolate(disp_new, disp)
    charge_f = wide(extrapolate(disch_new, disch))
    soc_f = wide(extrapolate(level_new, level))
    before_x = wide(extrapolate(before_new, before_level))
    balance = dot(asset_onehot, disp_x) + charge_f
    avail_rows = wide(avail[...]) * build_x - wide(disp_x)
    carried = jnp.where(link_c == 1.0, before_x, soc_f[:, HOUR - 1 : HOUR])
    previous = jnp.concatenate([carried, soc_f[:, : HOUR - 1]], axis=1)
    soc_rows = soc_f - decay * previous + charge_f
    scarce_new = jnp.maximum(scarce - sigma * avail_rows, 0.0)
    sdual_new = sdual - sigma * soc_rows
    halves = (
        mean(disp_new, disp),
        mean(build_new, build),
        mean(disch_new, disch),
        mean(level_new, level),
        mean(scarce_new, scarce),
        mean(sdual_new, sdual),
    )
    return balance, halves, link_c


def first_local(
    season, avail, asset_bus, run_cost, build_cost, efficiency, power, energy, link,
    disp, build, disch, level, scarce, sdual, price, got, lines_got, arrive, cap, far,
    disp1, build1, disch1, level1, scarce1, sdual1, came1, balance, rows, moves, turn,
):
    consts = (avail, asset_bus, run_cost, build_cost, efficiency, power, energy, link)
    state = (disp[...], build[...], disch[...], level[...], scarce[...], sdual[...])
    came0, near, _ = unpack(lines_got)
    moved, came_x = line_step(came0, near, wide(far[...]), cap[...], step_size)
    came1[...] = mean(moved, came0)
    before = halo_of(got, (season[0] + SEASONS - 1) & (SEASONS - 1))
    after = halo_of(got, (season[0] + 1) & (SEASONS - 1))
    local, halves, link_c = local_step(
        got[0:2], before, after, consts, state, price[...], turn, step_size, step_size
    )
    balance[...] = local + dot_t(arrive[...], came_x)
    for ref, value in zip((disp1, build1, disch1, level1, scarce1, sdual1), halves):
        ref[...] = value
    sums = jnp.sum(wide(avail[...]) * wide(narrow(halves[4])), axis=1, keepdims=True)
    rows[...] = season_block(sums, halves[3], wide(narrow(halves[5])), link_c)
    primal = (
        square(halves[0], state[0])
        + square(halves[1], state[1]) * (1.0 / SEASONS)
        + square(halves[2], state[2])
        + square(halves[3], state[3])
    )
    dual = square(halves[4], state[4]) + square(halves[5], state[5])
    lane = iota((8, 128), 1)
    moves[...] = jnp.where(lane == 0, primal, dual)


def price_step(
    flow0, near0, cap, leave, arrive, got, demand, price, balance, moves,
    price1, flow1, far0, sent,
):
    f0 = flow0[...]
    leave_t = leave[...]
    moved, flow_x = line_step(f0, wide(near0[...]), wide(got[...]), cap[...], step_size)
    f1 = mean(moved, f0)
    flow1[...] = f1
    p0 = price[...]
    whole = balance[...] - dot_t(leave_t, flow_x)
    p1 = mean(p0 + step_size * (demand[...] - whole), p0)
    price1[...] = p1
    primal = moves[0:1, 0:1] + square(f1, f0)
    dual = moves[0:1, 1:2] + square(p1, p0)
    lane = iota((GROUP, 128), 1)
    held = jnp.zeros((GROUP, 128), F32)
    for at, value in ((0, primal), (3, dual)):
        for step in range(3):
            piece = wide(narrow(value))
            held = jnp.where(lane == at + step, piece, held)
            value = value - piece
    held = narrow(held)
    price_b = narrow(p1)
    near = narrow(dot(leave_t, price_b))
    far = narrow(dot(arrive[...], price_b))
    far0[...] = far
    pack(near, far, jnp.concatenate([held] * (REGIONS // GROUP), axis=0), sent)


def moves_out(got, rows, sent):
    at = iota((8, REGIONS * ROWS_EACH), 1)
    q = (at * (262144 // ROWS_EACH + 1)) >> 18
    mask = as_bf(at - ROWS_EACH * q == 2 * LINK_CAP)
    moves = dot(mask, got[...])
    held = jnp.where(iota((8, 128), 0) == 4, moves, rows[...])
    for s in range(SEASONS):
        sent[s] = held


def second_step(
    season, avail, asset_bus, run_cost, build_cost, efficiency, power, energy, link,
    disp, build, disch, level, scarce, sdual, price, got, lines_got, arrive, came_cap,
    came_far, came, demand, flow, cap, leave,
    disp2, build2, flow2, disch2, level2, price2, scarce2, sdual2, turn,
):
    moves = tree([got[s, 4:5] for s in range(SEASONS)])
    primal = moves[:, 0:1] + moves[:, 1:2] + moves[:, 2:3]
    dual = moves[:, 3:4] + moves[:, 4:5] + moves[:, 5:6]
    weight = jnp.sqrt(jnp.sqrt((dual + 1e-06) / (primal + 1e-06)))
    tau = step_size / weight
    sigma = step_size * weight
    consts = (avail, asset_bus, run_cost, build_cost, efficiency, power, energy, link)
    state = (disp[...], build[...], disch[...], level[...], scarce[...], sdual[...])
    came_near, far, _ = unpack(lines_got)
    _, came_x = line_step(came[...], came_near, wide(came_far[...]), came_cap[...], tau)
    f1 = flow[...]
    p1 = price[...]
    leave_t = leave[...]
    near = dot(leave_t, narrow(p1))
    moved, flow_x = line_step(f1, near, far, cap[...], tau)
    flow2[...] = mean(moved, f1)
    sums = tree([got[s, 0:2] for s in range(SEASONS)])
    before = got[(season[0] + SEASONS - 1) & (SEASONS - 1), 2:4]
    after = got[(season[0] + 1) & (SEASONS - 1), 2:4]
    local, halves, _ = local_step(
        sums, before, after, consts, state, p1, turn, tau, sigma
    )
    whole = local + dot_t(arrive[...], came_x) - dot_t(leave_t, flow_x)
    price2[...] = mean(p1 + sigma * (demand[...] - whole), p1)
    for ref, value in zip((disp2, build2, disch2, level2, scarce2, sdual2), halves):
        ref[...] = value


def call(body, outs, *operands, scalar=False, turn=False):
    in_specs = [pl.BlockSpec(memory_space=pltpu.VMEM)] * len(operands)
    if scalar:
        in_specs[0] = pl.BlockSpec(memory_space=pltpu.SMEM)
    return pl.pallas_call(
        body,
        out_shape=[jax.ShapeDtypeStruct(shape, kind) for shape, kind in outs],
        in_specs=in_specs,
        out_specs=[pl.BlockSpec(memory_space=pltpu.VMEM)] * len(outs),
        scratch_shapes=[pltpu.VMEM((128, 128), F32)] if turn else [],
        compiler_params=pltpu.CompilerParams(vmem_limit_bytes=32 * 1024 * 1024),
    )(*operands)


def region_exchange(value, rows, per_pair):
    cut = value.reshape(REGIONS, per_pair, rows, HOUR)
    got = lax.all_to_all(cut, "region", split_axis=0, concat_axis=0, tiled=True)
    return got.reshape(value.shape)


def season_exchange(value):
    return lax.all_to_all(value, "season", split_axis=0, concat_axis=0, tiled=True)


def on_device(
    demand,
    avail,
    asset_bus,
    run_cost,
    build_cost,
    line_from,
    line_to,
    link_count,
    line_limit,
    efficiency,
    power_limit,
    energy_limit,
    season_link,
    dispatch,
    capacity,
    flow,
    charge,
    soc,
    price,
    scarcity,
    soc_dual,
):
    season = lax.axis_index("season").astype(I32).reshape(1)
    pair = lambda v: v.reshape(2, 128)
    short = lambda v: v.reshape(1, BUS)
    link = short(season_link)
    lines = ((SLOT, HOUR), F32)
    lines_b = ((SLOT, HOUR), BF16)
    buses = ((BUS, HOUR), F32)
    picks = ((SLOT, BUS), BF16)
    packed = ((REGIONS * ROWS_EACH, HOUR), BF16)
    seasons = ((SEASONS, 8, 128), F32)
    consts = (
        avail,
        pair(asset_bus),
        pair(run_cost),
        pair(build_cost),
        short(efficiency),
        short(power_limit),
        short(energy_limit),
        link,
    )
    sent1, flow0, near0, cap, leave = call(
        lines_out,
        [packed, lines, lines_b, lines, picks],
        flow,
        price,
        pair(line_from),
        pair(line_to),
        pair(line_limit),
        link_count,
        turn=True,
    )
    got1 = region_exchange(sent1, 2, 5)
    (rows1,) = call(
        season_out,
        [((24, 128), F32)],
        season,
        avail,
        scarcity,
        soc,
        soc_dual,
        link,
        scalar=True,
        turn=True,
    )
    season1 = lax.psum(rows1, "season")
    got1, season1 = lax.optimization_barrier((got1, season1))
    sent2, arrive, came_cap = call(ends_in, [lines_b, picks, lines], got1, price)
    got2 = region_exchange(sent2, LINK_CAP, 1)
    disp1, build1, disch1, level1, scarce1, sdual1, came1, balance, rows2, moves = call(
        first_local,
        [lines, ((2, 128), F32), buses, buses, lines, buses, lines, buses, ((8, 128), F32), ((8, 128), F32)],
        season,
        *consts,
        dispatch,
        pair(capacity),
        charge,
        soc,
        scarcity,
        soc_dual,
        price,
        season1,
        got1,
        arrive,
        came_cap,
        sent2,
        scalar=True,
        turn=True,
    )
    price1, flow1, came_far1, sent3 = call(
        price_step,
        [buses, lines, lines_b, packed],
        flow0,
        near0,
        cap,
        leave,
        arrive,
        got2,
        demand,
        price,
        balance,
        moves,
    )
    got3 = region_exchange(sent3, 2, 5)
    (rows3,) = call(moves_out, [seasons], got3, rows2)
    season2 = season_exchange(rows3)
    disp2, build2, flow2, disch2, level2, price2, scarce2, sdual2 = call(
        second_step,
        [lines, ((2, 128), F32), lines, buses, buses, buses, lines, buses],
        season,
        *consts,
        disp1,
        build1,
        disch1,
        level1,
        scarce1,
        sdual1,
        price1,
        season2,
        got3,
        arrive,
        came_cap,
        came_far1,
        came1,
        demand,
        flow1,
        cap,
        leave,
        scalar=True,
        turn=True,
    )
    return (disp2, build2.reshape(capacity.shape), flow2, disch2, level2, price2, scarce2, sdual2)


def solution(mesh):
    both = P("region", "season")
    rows = P("region")
    in_specs = (
        both,
        both,
        rows,
        rows,
        rows,
        rows,
        rows,
        P("region", None),
        rows,
        rows,
        rows,
        rows,
        both,
        both,
        rows,
        both,
        both,
        both,
        both,
        both,
        both,
    )
    out_specs = (both, rows, both, both, both, both, both, both)
    return jax.shard_map(
        on_device, mesh=mesh, in_specs=in_specs, out_specs=out_specs, check_vma=False
    )
```

```python
import jax
import jax.numpy as jnp
from jax import lax
from jax.experimental import pallas as pl
from jax.experimental.pallas import tpu as pltpu
from jax.sharding import PartitionSpec as P

LINK_CAP = 4
GROUP = 16
step_size = 0.2
F32 = jnp.float32
BF16 = jnp.bfloat16
I32 = jnp.int32
REGIONS, SEASONS = 64, 8
BUS, SLOT, HOUR = 64, 256, 128
LINES = GROUP * LINK_CAP
ROWS_EACH = 2 * LINK_CAP + 2
PACKED = GROUP * ROWS_EACH
UNPACKED = 2 * LINES + GROUP


def iota(shape, axis):
    return lax.broadcasted_iota(I32, shape, axis)


def dot(a, b):
    return jnp.dot(a, b, preferred_element_type=F32)


def dot_t(a, b):
    return lax.dot_general(a, b, (((0,), (0,)), ((), ())), preferred_element_type=F32)


def as_bf(mask):
    return jnp.where(mask, 1.0, 0.0).astype(BF16)


def narrow(value):
    return value.astype(BF16)


def wide(value):
    return value.astype(F32)


def extrapolate(newer, older):
    return narrow(2.0 * newer - older)


def mean(newer, older):
    return 0.5 * (newer + older)


def total(value):
    return jnp.sum(jnp.sum(value, axis=1, keepdims=True), axis=0, keepdims=True)


def square(newer, older):
    moved = newer - older
    return total(moved * moved)


def row256(ref):
    return jnp.concatenate([ref[0:1, :], ref[1:2, :]], axis=1)


def pack_target(packed):
    q = (packed * (262144 // ROWS_EACH + 1)) >> 18
    j = packed - ROWS_EACH * q
    first = LINK_CAP * q + j
    second = LINES + first - LINK_CAP
    third = jnp.where(j == 2 * LINK_CAP, 2 * LINES + q, -1)
    return jnp.where(j < LINK_CAP, first, jnp.where(j < 2 * LINK_CAP, second, third))


def pack(first, second, third, out_ref):
    shape = (PACKED, UNPACKED)
    place = as_bf(pack_target(iota(shape, 0)) == iota(shape, 1))
    for g in range(REGIONS // GROUP):
        rows = jnp.concatenate(
            [
                first[g * LINES : (g + 1) * LINES],
                second[g * LINES : (g + 1) * LINES],
                third[g * GROUP : (g + 1) * GROUP],
            ],
            axis=0,
        )
        out_ref[g * PACKED : (g + 1) * PACKED, :] = narrow(dot(place, rows))


def unpack(ref):
    shape = (UNPACKED, PACKED)
    place = as_bf(pack_target(iota(shape, 1)) == iota(shape, 0))
    parts = [
        dot(place, ref[g * PACKED : (g + 1) * PACKED, :]) for g in range(REGIONS // GROUP)
    ]
    first = jnp.concatenate([p[:LINES] for p in parts], axis=0)
    second = jnp.concatenate([p[LINES : 2 * LINES] for p in parts], axis=0)
    third = jnp.concatenate([p[2 * LINES :] for p in parts], axis=0)
    return first, second, third


def columns(ref):
    return jnp.transpose(ref[...])


def long_column(turned, at):
    return jnp.concatenate([turned[:, at : at + 1], turned[:, at + 1 : at + 2]], axis=0)


def onehot_rows(column, count):
    return as_bf(column == wide(iota((SLOT, count), 1)))


def lines_out(
    flow, price, line_from, line_to, line_limit, link_count,
    sent, flow0, near0, cap, leave, turn,
):
    lane = iota((1, SLOT), 1)
    spread = as_bf(iota((REGIONS, SLOT), 0) == lax.shift_right_logical(iota((REGIONS, SLOT), 1), 2))
    counts = jnp.broadcast_to(narrow(wide(link_count[...])), (8, REGIONS))
    counts = dot(counts, spread)[0:1]
    live = jnp.where(wide(lane & (LINK_CAP - 1)) < counts, 1.0, 0.0)
    limit = row256(line_limit) * live
    turn[0:2, :] = wide(line_from[...])
    turn[2:3, :] = live[:, :128]
    turn[3:4, :] = live[:, 128:]
    turn[4:5, :] = limit[:, :128]
    turn[5:6, :] = limit[:, 128:]
    turned = columns(turn)
    leave_t = onehot_rows(long_column(turned, 0), BUS)
    f0 = flow[...] * long_column(turned, 2)
    near = narrow(dot(leave_t, narrow(price[...])))
    flow0[...] = f0
    near0[...] = near
    cap[...] = jnp.broadcast_to(long_column(turned, 4), (SLOT, HOUR))
    leave[...] = leave_t
    high = wide(narrow(limit))
    low = limit - high
    held = jnp.zeros((REGIONS, 128), F32)
    slot_kind = iota((SLOT, 128), 0) & (LINK_CAP - 1)
    for at, value in enumerate((wide(row256(line_to)), high, low)):
        spots = as_bf(iota((SLOT, 128), 1) == slot_kind + LINK_CAP * at)
        held = held + dot(spread * narrow(value), spots)
    pack(narrow(f0), near, narrow(held), sent)


def season_block(sums, level, dual_f, link_column):
    lane = iota((128, 128), 1)
    tail = jnp.concatenate([level[:, HOUR - 1 : HOUR], dual_f[:, HOUR - 1 : HOUR]], axis=0)
    head = jnp.concatenate([dual_f[:, 0:1], link_column], axis=0)
    held = jnp.where(
        lane == 0,
        sums[:128],
        jnp.where(lane == 1, sums[128:], jnp.where(lane == 2, tail, jnp.where(lane == 3, head, 0.0))),
    )
    return jnp.transpose(held)[0:8]


def season_out(avail, scarcity, soc, soc_dual, link, sent, halo, turn):
    turn[0:1, 0:BUS] = wide(link[...])
    turned = columns(turn)
    sums = jnp.sum(wide(avail[...]) * wide(narrow(scarcity[...])), axis=1, keepdims=True)
    rows = season_block(sums, soc[...], wide(narrow(soc_dual[...])), turned[:BUS, 0:1])
    sent[...] = rows[0:2]
    halo[...] = rows[2:4]


def ends_in(got, price, sent, arrive, cap):
    _, _, held = unpack(got)
    shape = (SLOT, REGIONS)
    spread = as_bf(iota(shape, 1) == iota(shape, 0) >> 2)
    lines = dot(spread, narrow(held))
    lane = iota((SLOT, 128), 1)
    kind = iota((SLOT, 128), 0) & (LINK_CAP - 1)
    ends = jnp.sum(jnp.where(lane == kind, lines, 0.0), axis=1, keepdims=True)
    limits = (lane == kind + LINK_CAP) | (lane == kind + 2 * LINK_CAP)
    limit = jnp.sum(jnp.where(limits, lines, 0.0), axis=1, keepdims=True)
    arrive_t = onehot_rows(ends, BUS)
    sent[...] = narrow(dot(arrive_t, narrow(price[...])))
    arrive[...] = arrive_t
    cap[...] = jnp.broadcast_to(limit, (SLOT, HOUR))


def line_step(flows, near, far, cap, tau):
    moved = jnp.clip(flows + tau * (far - near), -cap, cap)
    return moved, extrapolate(moved, flows)


def tree(values):
    while len(values) > 1:
        values = [values[i] + values[i + 1] for i in range(0, len(values), 2)]
    return values[0]


def local_step(sums, before, after, consts, state, price_v, turn, tau, sigma):
    avail, asset_bus, run_cost, build_cost, efficiency, power, energy, link = consts
    disp, build, disch, level, scarce, sdual = state
    grad_build = sums * (1.0 / (HOUR * SEASONS))
    build_new = jnp.maximum(build - tau * (build_cost[...] - grad_build), 0.0)
    turn[2:4, :] = before
    turn[10:12, :] = after
    turn[16:18, :] = wide(extrapolate(build_new, build))
    turn[18:20, :] = run_cost[...]
    turn[20:22, :] = wide(asset_bus[...])
    turn[22:23, 0:BUS] = efficiency[...]
    turn[23:24, 0:BUS] = power[...]
    turn[24:25, 0:BUS] = energy[...]
    turn[25:26, 0:BUS] = wide(link[...])
    turned = columns(turn)
    build_x = long_column(turned, 16)
    cost = long_column(turned, 18)
    asset_t = onehot_rows(long_column(turned, 20), BUS)
    asset_row = row256(asset_bus)
    asset_onehot = as_bf(iota((BUS, SLOT), 0) == asset_row)
    decay = turned[:BUS, 22:23]
    power_c = turned[:BUS, 23:24]
    energy_c = turned[:BUS, 24:25]
    link_c = turned[:BUS, 25:26]
    before_level, before_dual = turned[:BUS, 2:3], turned[BUS:, 2:3]
    before_first, before_link = turned[:BUS, 3:4], turned[BUS:, 3:4]
    after_first, after_link = turned[:BUS, 11:12], turned[BUS:, 11:12]
    price_b = narrow(price_v)
    dual_f = wide(narrow(sdual))
    grad_dispatch = dot(asset_t, price_b) - wide(narrow(scarce))
    grad_charge = wide(price_b) + dual_f
    first = dual_f[:, 0:1]
    after_last = (1.0 - link_c) * first + after_link * after_first
    following = jnp.concatenate([dual_f[:, 1:], after_last], axis=1)
    grad_soc = dual_f - decay * following
    before_grad = before_dual - decay * ((1.0 - before_link) * before_first + link_c * first)
    disp_new = jnp.maximum(disp - tau * (cost - grad_dispatch), 0.0)
    disch_new = jnp.clip(disch + tau * grad_charge, -power_c, power_c)
    level_new = jnp.clip(level + tau * grad_soc, 0.0, energy_c)
    before_new = jnp.clip(before_level + tau * before_grad, 0.0, energy_c)
    disp_x = extrapolate(disp_new, disp)
    charge_f = wide(extrapolate(disch_new, disch))
    soc_f = wide(extrapolate(level_new, level))
    before_x = wide(extrapolate(before_new, before_level))
    balance = dot(asset_onehot, disp_x) + charge_f
    avail_rows = wide(avail[...]) * build_x - wide(disp_x)
    carried = jnp.where(link_c == 1.0, before_x, soc_f[:, HOUR - 1 : HOUR])
    previous = jnp.concatenate([carried, soc_f[:, : HOUR - 1]], axis=1)
    soc_rows = soc_f - decay * previous + charge_f
    scarce_new = jnp.maximum(scarce - sigma * avail_rows, 0.0)
    sdual_new = sdual - sigma * soc_rows
    halves = (
        mean(disp_new, disp),
        mean(build_new, build),
        mean(disch_new, disch),
        mean(level_new, level),
        mean(scarce_new, scarce),
        mean(sdual_new, sdual),
    )
    return balance, halves, link_c


def first_local(
    avail, asset_bus, run_cost, build_cost, efficiency, power, energy, link,
    disp, build, disch, level, scarce, sdual, price, sums, before, after,
    lines_got, arrive, cap, far,
    disp1, build1, disch1, level1, scarce1, sdual1, came1, balance, rows, moves, turn,
):
    consts = (avail, asset_bus, run_cost, build_cost, efficiency, power, energy, link)
    state = (disp[...], build[...], disch[...], level[...], scarce[...], sdual[...])
    came0, near, _ = unpack(lines_got)
    moved, came_x = line_step(came0, near, wide(far[...]), cap[...], step_size)
    came1[...] = mean(moved, came0)
    local, halves, link_c = local_step(
        sums[...], before[...], after[...], consts, state, price[...], turn, step_size, step_size
    )
    balance[...] = local + dot_t(arrive[...], came_x)
    for ref, value in zip((disp1, build1, disch1, level1, scarce1, sdual1), halves):
        ref[...] = value
    sums = jnp.sum(wide(avail[...]) * wide(narrow(halves[4])), axis=1, keepdims=True)
    rows[...] = season_block(sums, halves[3], wide(narrow(halves[5])), link_c)
    primal = (
        square(halves[0], state[0])
        + square(halves[1], state[1]) * (1.0 / SEASONS)
        + square(halves[2], state[2])
        + square(halves[3], state[3])
    )
    dual = square(halves[4], state[4]) + square(halves[5], state[5])
    lane = iota((8, 128), 1)
    moves[...] = jnp.where(lane == 0, primal, dual)


def price_step(
    flow0, near0, cap, leave, arrive, got, demand, price, balance, moves,
    price1, flow1, far0, sent,
):
    f0 = flow0[...]
    leave_t = leave[...]
    moved, flow_x = line_step(f0, wide(near0[...]), wide(got[...]), cap[...], step_size)
    f1 = mean(moved, f0)
    flow1[...] = f1
    p0 = price[...]
    whole = balance[...] - dot_t(leave_t, flow_x)
    p1 = mean(p0 + step_size * (demand[...] - whole), p0)
    price1[...] = p1
    primal = moves[0:1, 0:1] + square(f1, f0)
    dual = moves[0:1, 1:2] + square(p1, p0)
    lane = iota((GROUP, 128), 1)
    held = jnp.zeros((GROUP, 128), F32)
    for at, value in ((0, primal), (3, dual)):
        for step in range(3):
            piece = wide(narrow(value))
            held = jnp.where(lane == at + step, piece, held)
            value = value - piece
    held = narrow(held)
    price_b = narrow(p1)
    near = narrow(dot(leave_t, price_b))
    far = narrow(dot(arrive[...], price_b))
    far0[...] = far
    pack(near, far, jnp.concatenate([held] * (REGIONS // GROUP), axis=0), sent)


def moves_out(got, rows, sent):
    at = iota((8, REGIONS * ROWS_EACH), 1)
    q = (at * (262144 // ROWS_EACH + 1)) >> 18
    mask = as_bf(at - ROWS_EACH * q == 2 * LINK_CAP)
    moves = dot(mask, got[...])
    held = jnp.where(iota((8, 128), 0) == 4, moves, rows[...])
    for s in range(SEASONS):
        sent[s] = held


def second_step(
    season, avail, asset_bus, run_cost, build_cost, efficiency, power, energy, link,
    disp, build, disch, level, scarce, sdual, price, got, lines_got, arrive, came_cap,
    came_far, came, demand, flow, cap, leave,
    disp2, build2, flow2, disch2, level2, price2, scarce2, sdual2, turn,
):
    moves = tree([got[s, 4:5] for s in range(SEASONS)])
    primal = moves[:, 0:1] + moves[:, 1:2] + moves[:, 2:3]
    dual = moves[:, 3:4] + moves[:, 4:5] + moves[:, 5:6]
    weight = jnp.sqrt(jnp.sqrt((dual + 1e-06) / (primal + 1e-06)))
    tau = step_size / weight
    sigma = step_size * weight
    consts = (avail, asset_bus, run_cost, build_cost, efficiency, power, energy, link)
    state = (disp[...], build[...], disch[...], level[...], scarce[...], sdual[...])
    came_near, far, _ = unpack(lines_got)
    _, came_x = line_step(came[...], came_near, wide(came_far[...]), came_cap[...], tau)
    f1 = flow[...]
    p1 = price[...]
    leave_t = leave[...]
    near = dot(leave_t, narrow(p1))
    moved, flow_x = line_step(f1, near, far, cap[...], tau)
    flow2[...] = mean(moved, f1)
    sums = tree([got[s, 0:2] for s in range(SEASONS)])
    before = got[(season[0] + SEASONS - 1) & (SEASONS - 1), 2:4]
    after = got[(season[0] + 1) & (SEASONS - 1), 2:4]
    local, halves, _ = local_step(
        sums, before, after, consts, state, p1, turn, tau, sigma
    )
    whole = local + dot_t(arrive[...], came_x) - dot_t(leave_t, flow_x)
    price2[...] = mean(p1 + sigma * (demand[...] - whole), p1)
    for ref, value in zip((disp2, build2, disch2, level2, scarce2, sdual2), halves):
        ref[...] = value


def call(body, outs, *operands, scalar=False, turn=False):
    in_specs = [pl.BlockSpec(memory_space=pltpu.VMEM)] * len(operands)
    if scalar:
        in_specs[0] = pl.BlockSpec(memory_space=pltpu.SMEM)
    return pl.pallas_call(
        body,
        out_shape=[jax.ShapeDtypeStruct(shape, kind) for shape, kind in outs],
        in_specs=in_specs,
        out_specs=[pl.BlockSpec(memory_space=pltpu.VMEM)] * len(outs),
        scratch_shapes=[pltpu.VMEM((128, 128), F32)] if turn else [],
        compiler_params=pltpu.CompilerParams(vmem_limit_bytes=32 * 1024 * 1024),
    )(*operands)


def region_exchange(value, rows, per_pair):
    cut = value.reshape(REGIONS, per_pair, rows, HOUR)
    got = lax.all_to_all(cut, "region", split_axis=0, concat_axis=0, tiled=True)
    return got.reshape(value.shape)


def season_pass(value, steps):
    pairs = [(s, (s + steps) % SEASONS) for s in range(SEASONS)]
    return lax.ppermute(value, "season", pairs)


def season_exchange(value):
    return lax.all_to_all(value, "season", split_axis=0, concat_axis=0, tiled=True)


def on_device(
    demand,
    avail,
    asset_bus,
    run_cost,
    build_cost,
    line_from,
    line_to,
    link_count,
    line_limit,
    efficiency,
    power_limit,
    energy_limit,
    season_link,
    dispatch,
    capacity,
    flow,
    charge,
    soc,
    price,
    scarcity,
    soc_dual,
):
    season = lax.axis_index("season").astype(I32).reshape(1)
    pair = lambda v: v.reshape(2, 128)
    short = lambda v: v.reshape(1, BUS)
    link = short(season_link)
    lines = ((SLOT, HOUR), F32)
    lines_b = ((SLOT, HOUR), BF16)
    buses = ((BUS, HOUR), F32)
    picks = ((SLOT, BUS), BF16)
    packed = ((REGIONS * ROWS_EACH, HOUR), BF16)
    seasons = ((SEASONS, 8, 128), F32)
    consts = (
        avail,
        pair(asset_bus),
        pair(run_cost),
        pair(build_cost),
        short(efficiency),
        short(power_limit),
        short(energy_limit),
        link,
    )
    sent1, flow0, near0, cap, leave = call(
        lines_out,
        [packed, lines, lines_b, lines, picks],
        flow,
        price,
        pair(line_from),
        pair(line_to),
        pair(line_limit),
        link_count,
        turn=True,
    )
    got1 = region_exchange(sent1, 2, 5)
    sums0, halo0 = call(
        season_out,
        [((2, 128), F32), ((2, 128), F32)],
        avail,
        scarcity,
        soc,
        soc_dual,
        link,
        turn=True,
    )
    sums1 = lax.psum(sums0, "season")
    before1 = season_pass(halo0, 1)
    after1 = season_pass(halo0, SEASONS - 1)
    got1, sums1 = lax.optimization_barrier((got1, sums1))
    sent2, arrive, came_cap = call(ends_in, [lines_b, picks, lines], got1, price)
    got2 = region_exchange(sent2, LINK_CAP, 1)
    disp1, build1, disch1, level1, scarce1, sdual1, came1, balance, rows2, moves = call(
        first_local,
        [lines, ((2, 128), F32), buses, buses, lines, buses, lines, buses, ((8, 128), F32), ((8, 128), F32)],
        *consts,
        dispatch,
        pair(capacity),
        charge,
        soc,
        scarcity,
        soc_dual,
        price,
        sums1,
        before1,
        after1,
        got1,
        arrive,
        came_cap,
        sent2,
        turn=True,
    )
    price1, flow1, came_far1, sent3 = call(
        price_step,
        [buses, lines, lines_b, packed],
        flow0,
        near0,
        cap,
        leave,
        arrive,
        got2,
        demand,
        price,
        balance,
        moves,
    )
    got3 = region_exchange(sent3, 2, 5)
    (rows3,) = call(moves_out, [seasons], got3, rows2)
    season2 = season_exchange(rows3)
    disp2, build2, flow2, disch2, level2, price2, scarce2, sdual2 = call(
        second_step,
        [lines, ((2, 128), F32), lines, buses, buses, buses, lines, buses],
        season,
        *consts,
        disp1,
        build1,
        disch1,
        level1,
        scarce1,
        sdual1,
        price1,
        season2,
        got3,
        arrive,
        came_cap,
        came_far1,
        came1,
        demand,
        flow1,
        cap,
        leave,
        scalar=True,
        turn=True,
    )
    return (disp2, build2.reshape(capacity.shape), flow2, disch2, level2, price2, scarce2, sdual2)


def solution(mesh):
    both = P("region", "season")
    rows = P("region")
    in_specs = (
        both,
        both,
        rows,
        rows,
        rows,
        rows,
        rows,
        P("region", None),
        rows,
        rows,
        rows,
        rows,
        both,
        both,
        rows,
        both,
        both,
        both,
        both,
        both,
        both,
    )
    out_specs = (both, rows, both, both, both, both, both, both)
    return jax.shard_map(
        on_device, mesh=mesh, in_specs=in_specs, out_specs=out_specs, check_vma=False
    )
```

```python
import jax
import jax.numpy as jnp
from jax import lax
from jax.experimental import pallas as pl
from jax.experimental.pallas import tpu as pltpu
from jax.sharding import PartitionSpec as P

LINK_CAP = 4
GROUP = 16
step_size = 0.2
F32 = jnp.float32
BF16 = jnp.bfloat16
I32 = jnp.int32
REGIONS, SEASONS = 64, 8
BUS, SLOT, HOUR = 64, 256, 128
LINES = GROUP * LINK_CAP
ROWS_EACH = 2 * LINK_CAP + 2
PACKED = GROUP * ROWS_EACH
UNPACKED = 2 * LINES + GROUP


def iota(shape, axis):
    return lax.broadcasted_iota(I32, shape, axis)


def dot(a, b):
    return jnp.dot(a, b, preferred_element_type=F32)


def dot_t(a, b):
    return lax.dot_general(a, b, (((0,), (0,)), ((), ())), preferred_element_type=F32)


def as_bf(mask):
    return jnp.where(mask, 1.0, 0.0).astype(BF16)


def narrow(value):
    return value.astype(BF16)


def wide(value):
    return value.astype(F32)


def extrapolate(newer, older):
    return narrow(2.0 * newer - older)


def mean(newer, older):
    return 0.5 * (newer + older)


def total(value):
    return jnp.sum(jnp.sum(value, axis=1, keepdims=True), axis=0, keepdims=True)


def square(newer, older):
    moved = newer - older
    return total(moved * moved)


def row256(ref):
    return jnp.concatenate([ref[0:1, :], ref[1:2, :]], axis=1)


def pack_target(packed):
    q = (packed * (262144 // ROWS_EACH + 1)) >> 18
    j = packed - ROWS_EACH * q
    first = LINK_CAP * q + j
    second = LINES + first - LINK_CAP
    third = jnp.where(j == 2 * LINK_CAP, 2 * LINES + q, -1)
    return jnp.where(j < LINK_CAP, first, jnp.where(j < 2 * LINK_CAP, second, third))


def pack(first, second, third, out_ref):
    shape = (PACKED, UNPACKED)
    place = as_bf(pack_target(iota(shape, 0)) == iota(shape, 1))
    for g in range(REGIONS // GROUP):
        rows = jnp.concatenate(
            [
                first[g * LINES : (g + 1) * LINES],
                second[g * LINES : (g + 1) * LINES],
                third[g * GROUP : (g + 1) * GROUP],
            ],
            axis=0,
        )
        out_ref[g * PACKED : (g + 1) * PACKED, :] = narrow(dot(place, rows))


def unpack(ref):
    shape = (UNPACKED, PACKED)
    place = as_bf(pack_target(iota(shape, 1)) == iota(shape, 0))
    parts = [
        dot(place, ref[g * PACKED : (g + 1) * PACKED, :]) for g in range(REGIONS // GROUP)
    ]
    first = jnp.concatenate([p[:LINES] for p in parts], axis=0)
    second = jnp.concatenate([p[LINES : 2 * LINES] for p in parts], axis=0)
    third = jnp.concatenate([p[2 * LINES :] for p in parts], axis=0)
    return first, second, third


def fetch(sources, held, sems):
    copies = [
        pltpu.make_async_copy(source, target, sems.at[at])
        for at, (source, target) in enumerate(zip(sources, held))
    ]
    for copy in copies:
        copy.start()
    for copy in copies:
        copy.wait()


def columns(ref):
    return jnp.transpose(ref[...])


def long_column(turned, at):
    return jnp.concatenate([turned[:, at : at + 1], turned[:, at + 1 : at + 2]], axis=0)


def onehot_rows(column, count):
    return as_bf(column == wide(iota((SLOT, count), 1)))


def lines_out(*refs):
    sent, flow0, near0, cap, leave, turn = refs[6:12]
    flow, price, line_from, line_to, line_limit, link_count, sems = refs[12:]
    fetch(refs[:6], refs[12:18], sems)
    lane = iota((1, SLOT), 1)
    spread = as_bf(iota((REGIONS, SLOT), 0) == lax.shift_right_logical(iota((REGIONS, SLOT), 1), 2))
    counts = jnp.broadcast_to(narrow(wide(link_count[...])), (8, REGIONS))
    counts = dot(counts, spread)[0:1]
    live = jnp.where(wide(lane & (LINK_CAP - 1)) < counts, 1.0, 0.0)
    limit = row256(line_limit) * live
    turn[0:2, :] = wide(line_from[...])
    turn[2:3, :] = live[:, :128]
    turn[3:4, :] = live[:, 128:]
    turn[4:5, :] = limit[:, :128]
    turn[5:6, :] = limit[:, 128:]
    turned = columns(turn)
    leave_t = onehot_rows(long_column(turned, 0), BUS)
    f0 = flow[...] * long_column(turned, 2)
    near = narrow(dot(leave_t, narrow(price[...])))
    flow0[...] = f0
    near0[...] = near
    cap[...] = jnp.broadcast_to(long_column(turned, 4), (SLOT, HOUR))
    leave[...] = leave_t
    high = wide(narrow(limit))
    low = limit - high
    held = jnp.zeros((REGIONS, 128), F32)
    slot_kind = iota((SLOT, 128), 0) & (LINK_CAP - 1)
    for at, value in enumerate((wide(row256(line_to)), high, low)):
        spots = as_bf(iota((SLOT, 128), 1) == slot_kind + LINK_CAP * at)
        held = held + dot(spread * narrow(value), spots)
    pack(narrow(f0), near, narrow(held), sent)


def season_block(sums, level, dual_f, link_column):
    lane = iota((128, 128), 1)
    tail = jnp.concatenate([level[:, HOUR - 1 : HOUR], dual_f[:, HOUR - 1 : HOUR]], axis=0)
    head = jnp.concatenate([dual_f[:, 0:1], link_column], axis=0)
    held = jnp.where(
        lane == 0,
        sums[:128],
        jnp.where(lane == 1, sums[128:], jnp.where(lane == 2, tail, jnp.where(lane == 3, head, 0.0))),
    )
    return jnp.transpose(held)[0:8]


def season_out(*refs):
    sent, turn, avail, scarcity, soc, soc_dual, link, sems = refs[5:]
    fetch(refs[:5], refs[7:12], sems)
    turn[0:1, 0:BUS] = wide(link[...])
    turned = columns(turn)
    sums = jnp.sum(wide(avail[...]) * wide(narrow(scarcity[...])), axis=1, keepdims=True)
    rows = season_block(sums, soc[...], wide(narrow(soc_dual[...])), turned[:BUS, 0:1])
    for s in range(SEASONS):
        sent[s] = rows


def ends_in(got, price, sent, arrive, cap):
    _, _, held = unpack(got)
    shape = (SLOT, REGIONS)
    spread = as_bf(iota(shape, 1) == iota(shape, 0) >> 2)
    lines = dot(spread, narrow(held))
    lane = iota((SLOT, 128), 1)
    kind = iota((SLOT, 128), 0) & (LINK_CAP - 1)
    ends = jnp.sum(jnp.where(lane == kind, lines, 0.0), axis=1, keepdims=True)
    limits = (lane == kind + LINK_CAP) | (lane == kind + 2 * LINK_CAP)
    limit = jnp.sum(jnp.where(limits, lines, 0.0), axis=1, keepdims=True)
    arrive_t = onehot_rows(ends, BUS)
    sent[...] = narrow(dot(arrive_t, narrow(price[...])))
    arrive[...] = arrive_t
    cap[...] = jnp.broadcast_to(limit, (SLOT, HOUR))


def line_step(flows, near, far, cap, tau):
    moved = jnp.clip(flows + tau * (far - near), -cap, cap)
    return moved, extrapolate(moved, flows)


def tree(values):
    while len(values) > 1:
        values = [values[i] + values[i + 1] for i in range(0, len(values), 2)]
    return values[0]


def season_parts(got, season):
    sums = tree([got[s, 0:2] for s in range(SEASONS)])
    before = got[(season + SEASONS - 1) & (SEASONS - 1), 2:4]
    after = got[(season + 1) & (SEASONS - 1), 2:4]
    return sums, before, after


def local_step(sums, before, after, consts, state, price_v, turn, tau, sigma):
    avail, asset_bus, run_cost, build_cost, efficiency, power, energy, link = consts
    disp, build, disch, level, scarce, sdual = state
    grad_build = sums * (1.0 / (HOUR * SEASONS))
    build_new = jnp.maximum(build - tau * (build_cost[...] - grad_build), 0.0)
    turn[2:4, :] = before
    turn[10:12, :] = after
    turn[16:18, :] = wide(extrapolate(build_new, build))
    turn[18:20, :] = run_cost[...]
    turn[20:22, :] = wide(asset_bus[...])
    turn[22:23, 0:BUS] = efficiency[...]
    turn[23:24, 0:BUS] = power[...]
    turn[24:25, 0:BUS] = energy[...]
    turn[25:26, 0:BUS] = wide(link[...])
    turned = columns(turn)
    build_x = long_column(turned, 16)
    cost = long_column(turned, 18)
    asset_t = onehot_rows(long_column(turned, 20), BUS)
    asset_row = row256(asset_bus)
    asset_onehot = as_bf(iota((BUS, SLOT), 0) == asset_row)
    decay = turned[:BUS, 22:23]
    power_c = turned[:BUS, 23:24]
    energy_c = turned[:BUS, 24:25]
    link_c = turned[:BUS, 25:26]
    before_level, before_dual = turned[:BUS, 2:3], turned[BUS:, 2:3]
    before_first, before_link = turned[:BUS, 3:4], turned[BUS:, 3:4]
    after_first, after_link = turned[:BUS, 11:12], turned[BUS:, 11:12]
    price_b = narrow(price_v)
    dual_f = wide(narrow(sdual))
    grad_dispatch = dot(asset_t, price_b) - wide(narrow(scarce))
    grad_charge = wide(price_b) + dual_f
    first = dual_f[:, 0:1]
    after_last = (1.0 - link_c) * first + after_link * after_first
    following = jnp.concatenate([dual_f[:, 1:], after_last], axis=1)
    grad_soc = dual_f - decay * following
    before_grad = before_dual - decay * ((1.0 - before_link) * before_first + link_c * first)
    disp_new = jnp.maximum(disp - tau * (cost - grad_dispatch), 0.0)
    disch_new = jnp.clip(disch + tau * grad_charge, -power_c, power_c)
    level_new = jnp.clip(level + tau * grad_soc, 0.0, energy_c)
    before_new = jnp.clip(before_level + tau * before_grad, 0.0, energy_c)
    disp_x = extrapolate(disp_new, disp)
    charge_f = wide(extrapolate(disch_new, disch))
    soc_f = wide(extrapolate(level_new, level))
    before_x = wide(extrapolate(before_new, before_level))
    balance = dot(asset_onehot, disp_x) + charge_f
    avail_rows = wide(avail[...]) * build_x - wide(disp_x)
    carried = jnp.where(link_c == 1.0, before_x, soc_f[:, HOUR - 1 : HOUR])
    previous = jnp.concatenate([carried, soc_f[:, : HOUR - 1]], axis=1)
    soc_rows = soc_f - decay * previous + charge_f
    scarce_new = jnp.maximum(scarce - sigma * avail_rows, 0.0)
    sdual_new = sdual - sigma * soc_rows
    halves = (
        mean(disp_new, disp),
        mean(build_new, build),
        mean(disch_new, disch),
        mean(level_new, level),
        mean(scarce_new, scarce),
        mean(sdual_new, sdual),
    )
    return balance, halves, link_c


def first_local(
    season, avail, asset_bus, run_cost, build_cost, efficiency, power, energy, link,
    disp, build, disch, level, scarce, sdual, price, got, lines_got, arrive, cap, far,
    disp1, build1, disch1, level1, scarce1, sdual1, came1, balance, rows, moves, turn,
):
    consts = (avail, asset_bus, run_cost, build_cost, efficiency, power, energy, link)
    state = (disp[...], build[...], disch[...], level[...], scarce[...], sdual[...])
    came0, near, _ = unpack(lines_got)
    moved, came_x = line_step(came0, near, wide(far[...]), cap[...], step_size)
    came1[...] = mean(moved, came0)
    sums, before, after = season_parts(got, season[0])
    local, halves, link_c = local_step(
        sums, before, after, consts, state, price[...], turn, step_size, step_size
    )
    balance[...] = local + dot_t(arrive[...], came_x)
    for ref, value in zip((disp1, build1, disch1, level1, scarce1, sdual1), halves):
        ref[...] = value
    sums = jnp.sum(wide(avail[...]) * wide(narrow(halves[4])), axis=1, keepdims=True)
    rows[...] = season_block(sums, halves[3], wide(narrow(halves[5])), link_c)
    primal = (
        square(halves[0], state[0])
        + square(halves[1], state[1]) * (1.0 / SEASONS)
        + square(halves[2], state[2])
        + square(halves[3], state[3])
    )
    dual = square(halves[4], state[4]) + square(halves[5], state[5])
    lane = iota((8, 128), 1)
    moves[...] = jnp.where(lane == 0, primal, dual)


def price_step(
    flow0, near0, cap, leave, arrive, got, demand, price, balance, moves,
    price1, flow1, far0, sent,
):
    f0 = flow0[...]
    leave_t = leave[...]
    moved, flow_x = line_step(f0, wide(near0[...]), wide(got[...]), cap[...], step_size)
    f1 = mean(moved, f0)
    flow1[...] = f1
    p0 = price[...]
    whole = balance[...] - dot_t(leave_t, flow_x)
    p1 = mean(p0 + step_size * (demand[...] - whole), p0)
    price1[...] = p1
    primal = moves[0:1, 0:1] + square(f1, f0)
    dual = moves[0:1, 1:2] + square(p1, p0)
    lane = iota((GROUP, 128), 1)
    held = jnp.zeros((GROUP, 128), F32)
    for at, value in ((0, primal), (3, dual)):
        for step in range(3):
            piece = wide(narrow(value))
            held = jnp.where(lane == at + step, piece, held)
            value = value - piece
    held = narrow(held)
    price_b = narrow(p1)
    near = narrow(dot(leave_t, price_b))
    far = narrow(dot(arrive[...], price_b))
    far0[...] = far
    pack(near, far, jnp.concatenate([held] * (REGIONS // GROUP), axis=0), sent)


def moves_out(got, rows, sent):
    at = iota((8, REGIONS * ROWS_EACH), 1)
    q = (at * (262144 // ROWS_EACH + 1)) >> 18
    mask = as_bf(at - ROWS_EACH * q == 2 * LINK_CAP)
    moves = dot(mask, got[...])
    held = jnp.where(iota((8, 128), 0) == 4, moves, rows[...])
    for s in range(SEASONS):
        sent[s] = held


def second_step(
    season, avail, asset_bus, run_cost, build_cost, efficiency, power, energy, link,
    disp, build, disch, level, scarce, sdual, price, got, lines_got, arrive, came_cap,
    came_far, came, demand, flow, cap, leave,
    disp2, build2, flow2, disch2, level2, price2, scarce2, sdual2, turn,
):
    moves = tree([got[s, 4:5] for s in range(SEASONS)])
    primal = moves[:, 0:1] + moves[:, 1:2] + moves[:, 2:3]
    dual = moves[:, 3:4] + moves[:, 4:5] + moves[:, 5:6]
    weight = jnp.sqrt(jnp.sqrt((dual + 1e-06) / (primal + 1e-06)))
    tau = step_size / weight
    sigma = step_size * weight
    consts = (avail, asset_bus, run_cost, build_cost, efficiency, power, energy, link)
    state = (disp[...], build[...], disch[...], level[...], scarce[...], sdual[...])
    came_near, far, _ = unpack(lines_got)
    _, came_x = line_step(came[...], came_near, wide(came_far[...]), came_cap[...], tau)
    f1 = flow[...]
    p1 = price[...]
    leave_t = leave[...]
    near = dot(leave_t, narrow(p1))
    moved, flow_x = line_step(f1, near, far, cap[...], tau)
    flow2[...] = mean(moved, f1)
    sums, before, after = season_parts(got, season[0])
    local, halves, _ = local_step(
        sums, before, after, consts, state, p1, turn, tau, sigma
    )
    whole = local + dot_t(arrive[...], came_x) - dot_t(leave_t, flow_x)
    price2[...] = mean(p1 + sigma * (demand[...] - whole), p1)
    for ref, value in zip((disp2, build2, disch2, level2, scarce2, sdual2), halves):
        ref[...] = value


def call(body, outs, *operands, scalar=False, turn=False, fetched=False):
    space = pltpu.HBM if fetched else pltpu.VMEM
    in_specs = [pl.BlockSpec(memory_space=space)] * len(operands)
    scratch = [pltpu.VMEM((128, 128), F32)] if turn else []
    if fetched:
        operands = [pltpu.with_memory_space_constraint(v, pltpu.HBM) for v in operands]
        scratch += [pltpu.VMEM(v.shape, v.dtype) for v in operands]
        scratch += [pltpu.SemaphoreType.DMA((len(operands),))]
    if scalar:
        in_specs[0] = pl.BlockSpec(memory_space=pltpu.SMEM)
    return pl.pallas_call(
        body,
        out_shape=[jax.ShapeDtypeStruct(shape, kind) for shape, kind in outs],
        in_specs=in_specs,
        out_specs=[pl.BlockSpec(memory_space=pltpu.VMEM)] * len(outs),
        scratch_shapes=scratch,
        compiler_params=pltpu.CompilerParams(vmem_limit_bytes=32 * 1024 * 1024),
    )(*operands)


def region_exchange(value, rows, per_pair):
    cut = value.reshape(REGIONS, per_pair, rows, HOUR)
    got = lax.all_to_all(cut, "region", split_axis=0, concat_axis=0, tiled=True)
    return got.reshape(value.shape)


def season_exchange(value):
    return lax.all_to_all(value, "season", split_axis=0, concat_axis=0, tiled=True)


def on_device(
    demand,
    avail,
    asset_bus,
    run_cost,
    build_cost,
    line_from,
    line_to,
    link_count,
    line_limit,
    efficiency,
    power_limit,
    energy_limit,
    season_link,
    dispatch,
    capacity,
    flow,
    charge,
    soc,
    price,
    scarcity,
    soc_dual,
):
    season = lax.axis_index("season").astype(I32).reshape(1)
    pair = lambda v: v.reshape(2, 128)
    short = lambda v: v.reshape(1, BUS)
    link = short(season_link)
    lines = ((SLOT, HOUR), F32)
    lines_b = ((SLOT, HOUR), BF16)
    buses = ((BUS, HOUR), F32)
    picks = ((SLOT, BUS), BF16)
    packed = ((REGIONS * ROWS_EACH, HOUR), BF16)
    seasons = ((SEASONS, 8, 128), F32)
    consts = (
        avail,
        pair(asset_bus),
        pair(run_cost),
        pair(build_cost),
        short(efficiency),
        short(power_limit),
        short(energy_limit),
        link,
    )
    sent1, flow0, near0, cap, leave = call(
        lines_out,
        [packed, lines, lines_b, lines, picks],
        flow,
        price,
        pair(line_from),
        pair(line_to),
        pair(line_limit),
        link_count,
        turn=True,
        fetched=True,
    )
    got1 = region_exchange(sent1, 2, 5)
    (rows1,) = call(season_out, [seasons], avail, scarcity, soc, soc_dual, link, turn=True, fetched=True)
    season1 = season_exchange(rows1)
    sent2, arrive, came_cap = call(ends_in, [lines_b, picks, lines], got1, price)
    got2 = region_exchange(sent2, LINK_CAP, 1)
    disp1, build1, disch1, level1, scarce1, sdual1, came1, balance, rows2, moves = call(
        first_local,
        [lines, ((2, 128), F32), buses, buses, lines, buses, lines, buses, ((8, 128), F32), ((8, 128), F32)],
        season,
        *consts,
        dispatch,
        pair(capacity),
        charge,
        soc,
        scarcity,
        soc_dual,
        price,
        season1,
        got1,
        arrive,
        came_cap,
        sent2,
        scalar=True,
        turn=True,
    )
    price1, flow1, came_far1, sent3 = call(
        price_step,
        [buses, lines, lines_b, packed],
        flow0,
        near0,
        cap,
        leave,
        arrive,
        got2,
        demand,
        price,
        balance,
        moves,
    )
    got3 = region_exchange(sent3, 2, 5)
    (rows3,) = call(moves_out, [seasons], got3, rows2)
    season2 = season_exchange(rows3)
    disp2, build2, flow2, disch2, level2, price2, scarce2, sdual2 = call(
        second_step,
        [lines, ((2, 128), F32), lines, buses, buses, buses, lines, buses],
        season,
        *consts,
        disp1,
        build1,
        disch1,
        level1,
        scarce1,
        sdual1,
        price1,
        season2,
        got3,
        arrive,
        came_cap,
        came_far1,
        came1,
        demand,
        flow1,
        cap,
        leave,
        scalar=True,
        turn=True,
    )
    return (disp2, build2.reshape(capacity.shape), flow2, disch2, level2, price2, scarce2, sdual2)


def solution(mesh):
    both = P("region", "season")
    rows = P("region")
    in_specs = (
        both,
        both,
        rows,
        rows,
        rows,
        rows,
        rows,
        P("region", None),
        rows,
        rows,
        rows,
        rows,
        both,
        both,
        rows,
        both,
        both,
        both,
        both,
        both,
        both,
    )
    out_specs = (both, rows, both, both, both, both, both, both)
    return jax.shard_map(
        on_device, mesh=mesh, in_specs=in_specs, out_specs=out_specs, check_vma=False
    )
```

```python
import jax
import jax.numpy as jnp
from jax import lax
from jax.experimental import pallas as pl
from jax.experimental.pallas import tpu as pltpu
from jax.sharding import PartitionSpec as P

LINK_CAP = 4
GROUP = 16
step_size = 0.2
F32 = jnp.float32
BF16 = jnp.bfloat16
I32 = jnp.int32
REGIONS, SEASONS = 64, 8
BUS, SLOT, HOUR = 64, 256, 128
LINES = GROUP * LINK_CAP
ROWS_EACH = 2 * LINK_CAP + 2
PACKED = GROUP * ROWS_EACH
UNPACKED = 2 * LINES + GROUP


def iota(shape, axis):
    return lax.broadcasted_iota(I32, shape, axis)


def dot(a, b):
    return jnp.dot(a, b, preferred_element_type=F32)


def dot_t(a, b):
    return lax.dot_general(a, b, (((0,), (0,)), ((), ())), preferred_element_type=F32)


def as_bf(mask):
    return jnp.where(mask, 1.0, 0.0).astype(BF16)


def narrow(value):
    return value.astype(BF16)


def wide(value):
    return value.astype(F32)


def extrapolate(newer, older):
    return narrow(2.0 * newer - older)


def mean(newer, older):
    return 0.5 * (newer + older)


def total(value):
    return jnp.sum(jnp.sum(value, axis=1, keepdims=True), axis=0, keepdims=True)


def square(newer, older):
    moved = newer - older
    return total(moved * moved)


def row256(ref):
    return jnp.concatenate([ref[0:1, :], ref[1:2, :]], axis=1)


def pack_target(packed):
    q = (packed * (262144 // ROWS_EACH + 1)) >> 18
    j = packed - ROWS_EACH * q
    first = LINK_CAP * q + j
    second = LINES + first - LINK_CAP
    third = jnp.where(j == 2 * LINK_CAP, 2 * LINES + q, -1)
    return jnp.where(j < LINK_CAP, first, jnp.where(j < 2 * LINK_CAP, second, third))


def pack(first, second, third, out_ref):
    shape = (PACKED, UNPACKED)
    place = as_bf(pack_target(iota(shape, 0)) == iota(shape, 1))
    for g in range(REGIONS // GROUP):
        rows = jnp.concatenate(
            [
                first[g * LINES : (g + 1) * LINES],
                second[g * LINES : (g + 1) * LINES],
                third[g * GROUP : (g + 1) * GROUP],
            ],
            axis=0,
        )
        out_ref[g * PACKED : (g + 1) * PACKED, :] = narrow(dot(place, rows))


def unpack(ref):
    shape = (UNPACKED, PACKED)
    place = as_bf(pack_target(iota(shape, 1)) == iota(shape, 0))
    parts = [
        dot(place, ref[g * PACKED : (g + 1) * PACKED, :]) for g in range(REGIONS // GROUP)
    ]
    first = jnp.concatenate([p[:LINES] for p in parts], axis=0)
    second = jnp.concatenate([p[LINES : 2 * LINES] for p in parts], axis=0)
    third = jnp.concatenate([p[2 * LINES :] for p in parts], axis=0)
    return first, second, third


def start_copies(sources, held, sems):
    copies = [
        pltpu.make_async_copy(source, target, sems.at[at])
        for at, (source, target) in enumerate(zip(sources, held))
    ]
    for copy in copies:
        copy.start()
    return [copy.wait for copy in copies]


def fetch(sources, held, sems):
    for wait in start_copies(sources, held, sems):
        wait()


def columns(ref):
    return jnp.transpose(ref[...])


def long_column(turned, at):
    return jnp.concatenate([turned[:, at : at + 1], turned[:, at + 1 : at + 2]], axis=0)


def onehot_rows(column, count):
    return as_bf(column == wide(iota((SLOT, count), 1)))


def lines_out(*refs):
    sent, flow0, near0, cap, leave, turn = refs[6:12]
    flow, price, line_from, line_to, line_limit, link_count, sems = refs[12:]
    waits = start_copies(refs[:6], refs[12:18], sems)
    for wait in waits[2:]:
        wait()
    lane = iota((1, SLOT), 1)
    spread = as_bf(iota((REGIONS, SLOT), 0) == lax.shift_right_logical(iota((REGIONS, SLOT), 1), 2))
    counts = jnp.broadcast_to(narrow(wide(link_count[...])), (8, REGIONS))
    counts = dot(counts, spread)[0:1]
    live = jnp.where(wide(lane & (LINK_CAP - 1)) < counts, 1.0, 0.0)
    limit = row256(line_limit) * live
    turn[0:2, :] = wide(line_from[...])
    turn[2:3, :] = live[:, :128]
    turn[3:4, :] = live[:, 128:]
    turn[4:5, :] = limit[:, :128]
    turn[5:6, :] = limit[:, 128:]
    turned = columns(turn)
    leave_t = onehot_rows(long_column(turned, 0), BUS)
    cap[...] = jnp.broadcast_to(long_column(turned, 4), (SLOT, HOUR))
    leave[...] = leave_t
    high = wide(narrow(limit))
    low = limit - high
    held = jnp.zeros((REGIONS, 128), F32)
    slot_kind = iota((SLOT, 128), 0) & (LINK_CAP - 1)
    for at, value in enumerate((wide(row256(line_to)), high, low)):
        spots = as_bf(iota((SLOT, 128), 1) == slot_kind + LINK_CAP * at)
        held = held + dot(spread * narrow(value), spots)
    waits[1]()
    near = narrow(dot(leave_t, narrow(price[...])))
    near0[...] = near
    waits[0]()
    f0 = flow[...] * long_column(turned, 2)
    flow0[...] = f0
    pack(narrow(f0), near, narrow(held), sent)


def season_block(sums, level, dual_f, link_column):
    lane = iota((128, 128), 1)
    tail = jnp.concatenate([level[:, HOUR - 1 : HOUR], dual_f[:, HOUR - 1 : HOUR]], axis=0)
    head = jnp.concatenate([dual_f[:, 0:1], link_column], axis=0)
    held = jnp.where(
        lane == 0,
        sums[:128],
        jnp.where(lane == 1, sums[128:], jnp.where(lane == 2, tail, jnp.where(lane == 3, head, 0.0))),
    )
    return jnp.transpose(held)[0:8]


def season_out(*refs):
    sent, turn, avail, scarcity, soc, soc_dual, link, sems = refs[5:]
    fetch(refs[:5], refs[7:12], sems)
    turn[0:1, 0:BUS] = wide(link[...])
    turned = columns(turn)
    sums = jnp.sum(wide(avail[...]) * wide(narrow(scarcity[...])), axis=1, keepdims=True)
    rows = season_block(sums, soc[...], wide(narrow(soc_dual[...])), turned[:BUS, 0:1])
    for s in range(SEASONS):
        sent[s] = rows


def ends_in(got, price, sent, arrive, cap):
    _, _, held = unpack(got)
    shape = (SLOT, REGIONS)
    spread = as_bf(iota(shape, 1) == iota(shape, 0) >> 2)
    lines = dot(spread, narrow(held))
    lane = iota((SLOT, 128), 1)
    kind = iota((SLOT, 128), 0) & (LINK_CAP - 1)
    ends = jnp.sum(jnp.where(lane == kind, lines, 0.0), axis=1, keepdims=True)
    limits = (lane == kind + LINK_CAP) | (lane == kind + 2 * LINK_CAP)
    limit = jnp.sum(jnp.where(limits, lines, 0.0), axis=1, keepdims=True)
    arrive_t = onehot_rows(ends, BUS)
    sent[...] = narrow(dot(arrive_t, narrow(price[...])))
    arrive[...] = arrive_t
    cap[...] = jnp.broadcast_to(limit, (SLOT, HOUR))


def line_step(flows, near, far, cap, tau):
    moved = jnp.clip(flows + tau * (far - near), -cap, cap)
    return moved, extrapolate(moved, flows)


def tree(values):
    while len(values) > 1:
        values = [values[i] + values[i + 1] for i in range(0, len(values), 2)]
    return values[0]


def season_parts(got, season):
    sums = tree([got[s, 0:2] for s in range(SEASONS)])
    before = got[(season + SEASONS - 1) & (SEASONS - 1), 2:4]
    after = got[(season + 1) & (SEASONS - 1), 2:4]
    return sums, before, after


def local_step(sums, before, after, consts, state, price_v, turn, tau, sigma):
    avail, asset_bus, run_cost, build_cost, efficiency, power, energy, link = consts
    disp, build, disch, level, scarce, sdual = state
    grad_build = sums * (1.0 / (HOUR * SEASONS))
    build_new = jnp.maximum(build - tau * (build_cost[...] - grad_build), 0.0)
    turn[2:4, :] = before
    turn[10:12, :] = after
    turn[16:18, :] = wide(extrapolate(build_new, build))
    turn[18:20, :] = run_cost[...]
    turn[20:22, :] = wide(asset_bus[...])
    turn[22:23, 0:BUS] = efficiency[...]
    turn[23:24, 0:BUS] = power[...]
    turn[24:25, 0:BUS] = energy[...]
    turn[25:26, 0:BUS] = wide(link[...])
    turned = columns(turn)
    build_x = long_column(turned, 16)
    cost = long_column(turned, 18)
    asset_t = onehot_rows(long_column(turned, 20), BUS)
    asset_row = row256(asset_bus)
    asset_onehot = as_bf(iota((BUS, SLOT), 0) == asset_row)
    decay = turned[:BUS, 22:23]
    power_c = turned[:BUS, 23:24]
    energy_c = turned[:BUS, 24:25]
    link_c = turned[:BUS, 25:26]
    before_level, before_dual = turned[:BUS, 2:3], turned[BUS:, 2:3]
    before_first, before_link = turned[:BUS, 3:4], turned[BUS:, 3:4]
    after_first, after_link = turned[:BUS, 11:12], turned[BUS:, 11:12]
    price_b = narrow(price_v)
    dual_f = wide(narrow(sdual))
    grad_dispatch = dot(asset_t, price_b) - wide(narrow(scarce))
    grad_charge = wide(price_b) + dual_f
    first = dual_f[:, 0:1]
    after_last = (1.0 - link_c) * first + after_link * after_first
    following = jnp.concatenate([dual_f[:, 1:], after_last], axis=1)
    grad_soc = dual_f - decay * following
    before_grad = before_dual - decay * ((1.0 - before_link) * before_first + link_c * first)
    disp_new = jnp.maximum(disp - tau * (cost - grad_dispatch), 0.0)
    disch_new = jnp.clip(disch + tau * grad_charge, -power_c, power_c)
    level_new = jnp.clip(level + tau * grad_soc, 0.0, energy_c)
    before_new = jnp.clip(before_level + tau * before_grad, 0.0, energy_c)
    disp_x = extrapolate(disp_new, disp)
    charge_f = wide(extrapolate(disch_new, disch))
    soc_f = wide(extrapolate(level_new, level))
    before_x = wide(extrapolate(before_new, before_level))
    balance = dot(asset_onehot, disp_x) + charge_f
    avail_rows = wide(avail[...]) * build_x - wide(disp_x)
    carried = jnp.where(link_c == 1.0, before_x, soc_f[:, HOUR - 1 : HOUR])
    previous = jnp.concatenate([carried, soc_f[:, : HOUR - 1]], axis=1)
    soc_rows = soc_f - decay * previous + charge_f
    scarce_new = jnp.maximum(scarce - sigma * avail_rows, 0.0)
    sdual_new = sdual - sigma * soc_rows
    halves = (
        mean(disp_new, disp),
        mean(build_new, build),
        mean(disch_new, disch),
        mean(level_new, level),
        mean(scarce_new, scarce),
        mean(sdual_new, sdual),
    )
    return balance, halves, link_c


def first_step(
    season, avail, asset_bus, run_cost, build_cost, efficiency, power, energy, link,
    disp, build, disch, level, scarce, sdual, price, seasons_got, lines_got, arrive, came_cap,
    came_far, got, demand, flow0, near0, cap, leave,
    disp1, build1, disch1, level1, scarce1, sdual1, price1, flow1, came1, far1, rows, sent, turn,
):
    f0 = flow0[...]
    p0 = price[...]
    leave_t = leave[...]
    arrive_t = arrive[...]
    came0, came_near, _ = unpack(lines_got)
    came_moved, came_x = line_step(came0, came_near, wide(came_far[...]), came_cap[...], step_size)
    came1[...] = mean(came_moved, came0)
    moved, flow_x = line_step(f0, wide(near0[...]), wide(got[...]), cap[...], step_size)
    f1 = mean(moved, f0)
    flow1[...] = f1
    consts = (avail, asset_bus, run_cost, build_cost, efficiency, power, energy, link)
    state = (disp[...], build[...], disch[...], level[...], scarce[...], sdual[...])
    sums, before, after = season_parts(seasons_got, season[0])
    local, halves, link_c = local_step(
        sums, before, after, consts, state, p0, turn, step_size, step_size
    )
    for ref, value in zip((disp1, build1, disch1, level1, scarce1, sdual1), halves):
        ref[...] = value
    whole = local + dot_t(arrive_t, came_x) - dot_t(leave_t, flow_x)
    p1 = mean(p0 + step_size * (demand[...] - whole), p0)
    price1[...] = p1
    price_b = narrow(p1)
    near = narrow(dot(leave_t, price_b))
    far = narrow(dot(arrive_t, price_b))
    far1[...] = far
    sums = jnp.sum(wide(avail[...]) * wide(narrow(halves[4])), axis=1, keepdims=True)
    rows[...] = season_block(sums, halves[3], wide(narrow(halves[5])), link_c)
    primal = (
        square(halves[0], state[0])
        + square(halves[1], state[1]) * (1.0 / SEASONS)
        + square(halves[2], state[2])
        + square(halves[3], state[3])
        + square(f1, f0)
    )
    dual = square(halves[4], state[4]) + square(halves[5], state[5]) + square(p1, p0)
    lane = iota((GROUP, 128), 1)
    held = jnp.zeros((GROUP, 128), F32)
    for at, value in ((0, primal), (3, dual)):
        for step in range(3):
            piece = wide(narrow(value))
            held = jnp.where(lane == at + step, piece, held)
            value = value - piece
    held = narrow(held)
    pack(near, far, jnp.concatenate([held] * (REGIONS // GROUP), axis=0), sent)


def moves_out(got, rows, sent):
    at = iota((8, REGIONS * ROWS_EACH), 1)
    q = (at * (262144 // ROWS_EACH + 1)) >> 18
    mask = as_bf(at - ROWS_EACH * q == 2 * LINK_CAP)
    moves = dot(mask, got[...])
    held = jnp.where(iota((8, 128), 0) == 4, moves, rows[...])
    for s in range(SEASONS):
        sent[s] = held


def second_step(
    season, avail, asset_bus, run_cost, build_cost, efficiency, power, energy, link,
    disp, build, disch, level, scarce, sdual, price, got, lines_got, arrive, came_cap,
    came_far, came, demand, flow, cap, leave,
    disp2, build2, flow2, disch2, level2, price2, scarce2, sdual2, turn,
):
    moves = tree([got[s, 4:5] for s in range(SEASONS)])
    primal = moves[:, 0:1] + moves[:, 1:2] + moves[:, 2:3]
    dual = moves[:, 3:4] + moves[:, 4:5] + moves[:, 5:6]
    weight = jnp.sqrt(jnp.sqrt((dual + 1e-06) / (primal + 1e-06)))
    tau = step_size / weight
    sigma = step_size * weight
    consts = (avail, asset_bus, run_cost, build_cost, efficiency, power, energy, link)
    state = (disp[...], build[...], disch[...], level[...], scarce[...], sdual[...])
    came_near, far, _ = unpack(lines_got)
    _, came_x = line_step(came[...], came_near, wide(came_far[...]), came_cap[...], tau)
    f1 = flow[...]
    p1 = price[...]
    leave_t = leave[...]
    near = dot(leave_t, narrow(p1))
    moved, flow_x = line_step(f1, near, far, cap[...], tau)
    flow2[...] = mean(moved, f1)
    sums, before, after = season_parts(got, season[0])
    local, halves, _ = local_step(
        sums, before, after, consts, state, p1, turn, tau, sigma
    )
    whole = local + dot_t(arrive[...], came_x) - dot_t(leave_t, flow_x)
    price2[...] = mean(p1 + sigma * (demand[...] - whole), p1)
    for ref, value in zip((disp2, build2, disch2, level2, scarce2, sdual2), halves):
        ref[...] = value


def call(body, outs, *operands, scalar=False, turn=False, fetched=False):
    space = pltpu.HBM if fetched else pltpu.VMEM
    in_specs = [pl.BlockSpec(memory_space=space)] * len(operands)
    scratch = [pltpu.VMEM((128, 128), F32)] if turn else []
    if fetched:
        operands = [pltpu.with_memory_space_constraint(v, pltpu.HBM) for v in operands]
        scratch += [pltpu.VMEM(v.shape, v.dtype) for v in operands]
        scratch += [pltpu.SemaphoreType.DMA((len(operands),))]
    if scalar:
        in_specs[0] = pl.BlockSpec(memory_space=pltpu.SMEM)
    return pl.pallas_call(
        body,
        out_shape=[jax.ShapeDtypeStruct(shape, kind) for shape, kind in outs],
        in_specs=in_specs,
        out_specs=[pl.BlockSpec(memory_space=pltpu.VMEM)] * len(outs),
        scratch_shapes=scratch,
        compiler_params=pltpu.CompilerParams(vmem_limit_bytes=32 * 1024 * 1024),
    )(*operands)


def region_exchange(value, rows, per_pair):
    cut = value.reshape(REGIONS, per_pair, rows, HOUR)
    got = lax.all_to_all(cut, "region", split_axis=0, concat_axis=0, tiled=True)
    return got.reshape(value.shape)


def season_exchange(value):
    return lax.all_to_all(value, "season", split_axis=0, concat_axis=0, tiled=True)


def on_device(
    demand,
    avail,
    asset_bus,
    run_cost,
    build_cost,
    line_from,
    line_to,
    link_count,
    line_limit,
    efficiency,
    power_limit,
    energy_limit,
    season_link,
    dispatch,
    capacity,
    flow,
    charge,
    soc,
    price,
    scarcity,
    soc_dual,
):
    season = lax.axis_index("season").astype(I32).reshape(1)
    pair = lambda v: v.reshape(2, 128)
    short = lambda v: v.reshape(1, BUS)
    link = short(season_link)
    lines = ((SLOT, HOUR), F32)
    lines_b = ((SLOT, HOUR), BF16)
    buses = ((BUS, HOUR), F32)
    picks = ((SLOT, BUS), BF16)
    packed = ((REGIONS * ROWS_EACH, HOUR), BF16)
    seasons = ((SEASONS, 8, 128), F32)
    consts = (
        avail,
        pair(asset_bus),
        pair(run_cost),
        pair(build_cost),
        short(efficiency),
        short(power_limit),
        short(energy_limit),
        link,
    )
    sent1, flow0, near0, cap, leave = call(
        lines_out,
        [packed, lines, lines_b, lines, picks],
        flow,
        price,
        pair(line_from),
        pair(line_to),
        pair(line_limit),
        link_count,
        turn=True,
        fetched=True,
    )
    got1 = region_exchange(sent1, 2, 5)
    (rows1,) = call(season_out, [seasons], avail, scarcity, soc, soc_dual, link, turn=True, fetched=True)
    season1 = season_exchange(rows1)
    sent2, arrive, came_cap = call(ends_in, [lines_b, picks, lines], got1, price)
    got2 = region_exchange(sent2, LINK_CAP, 1)
    (
        disp1,
        build1,
        disch1,
        level1,
        scarce1,
        sdual1,
        price1,
        flow1,
        came1,
        came_far1,
        rows2,
        sent3,
    ) = call(
        first_step,
        [
            lines,
            ((2, 128), F32),
            buses,
            buses,
            lines,
            buses,
            buses,
            lines,
            lines,
            lines_b,
            ((8, 128), F32),
            packed,
        ],
        season,
        *consts,
        dispatch,
        pair(capacity),
        charge,
        soc,
        scarcity,
        soc_dual,
        price,
        season1,
        got1,
        arrive,
        came_cap,
        sent2,
        got2,
        demand,
        flow0,
        near0,
        cap,
        leave,
        scalar=True,
        turn=True,
    )
    got3 = region_exchange(sent3, 2, 5)
    (rows3,) = call(moves_out, [seasons], got3, rows2)
    season2 = season_exchange(rows3)
    disp2, build2, flow2, disch2, level2, price2, scarce2, sdual2 = call(
        second_step,
        [lines, ((2, 128), F32), lines, buses, buses, buses, lines, buses],
        season,
        *consts,
        disp1,
        build1,
        disch1,
        level1,
        scarce1,
        sdual1,
        price1,
        season2,
        got3,
        arrive,
        came_cap,
        came_far1,
        came1,
        demand,
        flow1,
        cap,
        leave,
        scalar=True,
        turn=True,
    )
    return (disp2, build2.reshape(capacity.shape), flow2, disch2, level2, price2, scarce2, sdual2)


def solution(mesh):
    both = P("region", "season")
    rows = P("region")
    in_specs = (
        both,
        both,
        rows,
        rows,
        rows,
        rows,
        rows,
        P("region", None),
        rows,
        rows,
        rows,
        rows,
        both,
        both,
        rows,
        both,
        both,
        both,
        both,
        both,
        both,
    )
    out_specs = (both, rows, both, both, both, both, both, both)
    return jax.shard_map(
        on_device, mesh=mesh, in_specs=in_specs, out_specs=out_specs, check_vma=False
    )
```

```python
import jax
import jax.numpy as jnp
from jax import lax
from jax.experimental import pallas as pl
from jax.experimental.pallas import tpu as pltpu
from jax.sharding import PartitionSpec as P

LINK_CAP = 4
GROUP = 16
step_size = 0.2
F32 = jnp.float32
BF16 = jnp.bfloat16
I32 = jnp.int32
REGIONS, SEASONS = 64, 8
BUS, SLOT, HOUR = 64, 256, 128
LINES = GROUP * LINK_CAP
ROWS_EACH = 2 * LINK_CAP + 2
PACKED = GROUP * ROWS_EACH
UNPACKED = 2 * LINES + GROUP


def iota(shape, axis):
    return lax.broadcasted_iota(I32, shape, axis)


def dot(a, b):
    return jnp.dot(a, b, preferred_element_type=F32)


def dot_t(a, b):
    return lax.dot_general(a, b, (((0,), (0,)), ((), ())), preferred_element_type=F32)


def as_bf(mask):
    return jnp.where(mask, 1.0, 0.0).astype(BF16)


def narrow(value):
    return value.astype(BF16)


def wide(value):
    return value.astype(F32)


def extrapolate(newer, older):
    return narrow(2.0 * newer - older)


def mean(newer, older):
    return 0.5 * (newer + older)


def total(value):
    return jnp.sum(jnp.sum(value, axis=1, keepdims=True), axis=0, keepdims=True)


def square(newer, older):
    moved = newer - older
    return total(moved * moved)


def row256(ref):
    return jnp.concatenate([ref[0:1, :], ref[1:2, :]], axis=1)


def pack_target(packed):
    q = (packed * (262144 // ROWS_EACH + 1)) >> 18
    j = packed - ROWS_EACH * q
    first = LINK_CAP * q + j
    second = LINES + first - LINK_CAP
    third = jnp.where(j == 2 * LINK_CAP, 2 * LINES + q, -1)
    return jnp.where(j < LINK_CAP, first, jnp.where(j < 2 * LINK_CAP, second, third))


def pack(first, second, third, out_ref, packed_group=None):
    shape = (PACKED, UNPACKED)
    place = as_bf(pack_target(iota(shape, 0)) == iota(shape, 1))
    for g in range(REGIONS // GROUP):
        rows = jnp.concatenate(
            [
                first[g * LINES : (g + 1) * LINES],
                second[g * LINES : (g + 1) * LINES],
                third[g * GROUP : (g + 1) * GROUP],
            ],
            axis=0,
        )
        out_ref[g * PACKED : (g + 1) * PACKED, :] = narrow(dot(place, rows))
        if packed_group is not None:
            packed_group(g)


def unpack(ref):
    shape = (UNPACKED, PACKED)
    place = as_bf(pack_target(iota(shape, 1)) == iota(shape, 0))
    parts = [
        dot(place, ref[g * PACKED : (g + 1) * PACKED, :]) for g in range(REGIONS // GROUP)
    ]
    first = jnp.concatenate([p[:LINES] for p in parts], axis=0)
    second = jnp.concatenate([p[LINES : 2 * LINES] for p in parts], axis=0)
    third = jnp.concatenate([p[2 * LINES :] for p in parts], axis=0)
    return first, second, third


def fetch(sources, held, sems):
    copies = [
        pltpu.make_async_copy(source, target, sems.at[at])
        for at, (source, target) in enumerate(zip(sources, held))
    ]
    for copy in copies:
        copy.start()
    for copy in copies:
        copy.wait()


def columns(ref):
    return jnp.transpose(ref[...])


def long_column(turned, at):
    return jnp.concatenate([turned[:, at : at + 1], turned[:, at + 1 : at + 2]], axis=0)


def onehot_rows(column, count):
    return as_bf(column == wide(iota((SLOT, count), 1)))


def lines_out(*refs):
    sent, flow0, near0, cap, leave, turn = refs[6:12]
    flow, price, line_from, line_to, line_limit, link_count, sems, held_out, out_sems = refs[12:]
    fetch(refs[:6], refs[12:18], sems)
    lane = iota((1, SLOT), 1)
    spread = as_bf(iota((REGIONS, SLOT), 0) == lax.shift_right_logical(iota((REGIONS, SLOT), 1), 2))
    counts = jnp.broadcast_to(narrow(wide(link_count[...])), (8, REGIONS))
    counts = dot(counts, spread)[0:1]
    live = jnp.where(wide(lane & (LINK_CAP - 1)) < counts, 1.0, 0.0)
    limit = row256(line_limit) * live
    turn[0:2, :] = wide(line_from[...])
    turn[2:3, :] = live[:, :128]
    turn[3:4, :] = live[:, 128:]
    turn[4:5, :] = limit[:, :128]
    turn[5:6, :] = limit[:, 128:]
    turned = columns(turn)
    leave_t = onehot_rows(long_column(turned, 0), BUS)
    f0 = flow[...] * long_column(turned, 2)
    near = narrow(dot(leave_t, narrow(price[...])))
    flow0[...] = f0
    near0[...] = near
    cap[...] = jnp.broadcast_to(long_column(turned, 4), (SLOT, HOUR))
    leave[...] = leave_t
    high = wide(narrow(limit))
    low = limit - high
    held = jnp.zeros((REGIONS, 128), F32)
    slot_kind = iota((SLOT, 128), 0) & (LINK_CAP - 1)
    for at, value in enumerate((wide(row256(line_to)), high, low)):
        spots = as_bf(iota((SLOT, 128), 1) == slot_kind + LINK_CAP * at)
        held = held + dot(spread * narrow(value), spots)
    copies = []

    def send(g):
        rows = pl.ds(g * PACKED, PACKED)
        copy = pltpu.make_async_copy(held_out.at[rows], sent.at[rows], out_sems.at[g])
        copy.start()
        copies.append(copy)

    pack(narrow(f0), near, narrow(held), held_out, send)
    for copy in copies:
        copy.wait()


def season_block(sums, level, dual_f, link_column):
    lane = iota((128, 128), 1)
    tail = jnp.concatenate([level[:, HOUR - 1 : HOUR], dual_f[:, HOUR - 1 : HOUR]], axis=0)
    head = jnp.concatenate([dual_f[:, 0:1], link_column], axis=0)
    held = jnp.where(
        lane == 0,
        sums[:128],
        jnp.where(lane == 1, sums[128:], jnp.where(lane == 2, tail, jnp.where(lane == 3, head, 0.0))),
    )
    return jnp.transpose(held)[0:8]


def season_out(*refs):
    sent, turn, avail, scarcity, soc, soc_dual, link, sems = refs[5:]
    fetch(refs[:5], refs[7:12], sems)
    turn[0:1, 0:BUS] = wide(link[...])
    turned = columns(turn)
    sums = jnp.sum(wide(avail[...]) * wide(narrow(scarcity[...])), axis=1, keepdims=True)
    rows = season_block(sums, soc[...], wide(narrow(soc_dual[...])), turned[:BUS, 0:1])
    for s in range(SEASONS):
        sent[s] = rows


def ends_in(got, price, sent, far, arrive, cap):
    _, _, held = unpack(got)
    shape = (SLOT, REGIONS)
    spread = as_bf(iota(shape, 1) == iota(shape, 0) >> 2)
    lines = dot(spread, narrow(held))
    lane = iota((SLOT, 128), 1)
    kind = iota((SLOT, 128), 0) & (LINK_CAP - 1)
    ends = jnp.sum(jnp.where(lane == kind, lines, 0.0), axis=1, keepdims=True)
    limits = (lane == kind + LINK_CAP) | (lane == kind + 2 * LINK_CAP)
    limit = jnp.sum(jnp.where(limits, lines, 0.0), axis=1, keepdims=True)
    arrive_t = onehot_rows(ends, BUS)
    values = narrow(dot(arrive_t, narrow(price[...])))
    sent[...] = values
    far[...] = values
    arrive[...] = arrive_t
    cap[...] = jnp.broadcast_to(limit, (SLOT, HOUR))


def line_step(flows, near, far, cap, tau):
    moved = jnp.clip(flows + tau * (far - near), -cap, cap)
    return moved, extrapolate(moved, flows)


def tree(values):
    while len(values) > 1:
        values = [values[i] + values[i + 1] for i in range(0, len(values), 2)]
    return values[0]


def season_parts(got, season):
    sums = tree([got[s, 0:2] for s in range(SEASONS)])
    before = got[(season + SEASONS - 1) & (SEASONS - 1), 2:4]
    after = got[(season + 1) & (SEASONS - 1), 2:4]
    return sums, before, after


def local_step(sums, before, after, consts, state, price_v, turn, tau, sigma):
    avail, asset_bus, run_cost, build_cost, efficiency, power, energy, link = consts
    disp, build, disch, level, scarce, sdual = state
    grad_build = sums * (1.0 / (HOUR * SEASONS))
    build_new = jnp.maximum(build - tau * (build_cost[...] - grad_build), 0.0)
    turn[2:4, :] = before
    turn[10:12, :] = after
    turn[16:18, :] = wide(extrapolate(build_new, build))
    turn[18:20, :] = run_cost[...]
    turn[20:22, :] = wide(asset_bus[...])
    turn[22:23, 0:BUS] = efficiency[...]
    turn[23:24, 0:BUS] = power[...]
    turn[24:25, 0:BUS] = energy[...]
    turn[25:26, 0:BUS] = wide(link[...])
    turned = columns(turn)
    build_x = long_column(turned, 16)
    cost = long_column(turned, 18)
    asset_t = onehot_rows(long_column(turned, 20), BUS)
    asset_row = row256(asset_bus)
    asset_onehot = as_bf(iota((BUS, SLOT), 0) == asset_row)
    decay = turned[:BUS, 22:23]
    power_c = turned[:BUS, 23:24]
    energy_c = turned[:BUS, 24:25]
    link_c = turned[:BUS, 25:26]
    before_level, before_dual = turned[:BUS, 2:3], turned[BUS:, 2:3]
    before_first, before_link = turned[:BUS, 3:4], turned[BUS:, 3:4]
    after_first, after_link = turned[:BUS, 11:12], turned[BUS:, 11:12]
    price_b = narrow(price_v)
    dual_f = wide(narrow(sdual))
    grad_dispatch = dot(asset_t, price_b) - wide(narrow(scarce))
    grad_charge = wide(price_b) + dual_f
    first = dual_f[:, 0:1]
    after_last = (1.0 - link_c) * first + after_link * after_first
    following = jnp.concatenate([dual_f[:, 1:], after_last], axis=1)
    grad_soc = dual_f - decay * following
    before_grad = before_dual - decay * ((1.0 - before_link) * before_first + link_c * first)
    disp_new = jnp.maximum(disp - tau * (cost - grad_dispatch), 0.0)
    disch_new = jnp.clip(disch + tau * grad_charge, -power_c, power_c)
    level_new = jnp.clip(level + tau * grad_soc, 0.0, energy_c)
    before_new = jnp.clip(before_level + tau * before_grad, 0.0, energy_c)
    disp_x = extrapolate(disp_new, disp)
    charge_f = wide(extrapolate(disch_new, disch))
    soc_f = wide(extrapolate(level_new, level))
    before_x = wide(extrapolate(before_new, before_level))
    balance = dot(asset_onehot, disp_x) + charge_f
    avail_rows = wide(avail[...]) * build_x - wide(disp_x)
    carried = jnp.where(link_c == 1.0, before_x, soc_f[:, HOUR - 1 : HOUR])
    previous = jnp.concatenate([carried, soc_f[:, : HOUR - 1]], axis=1)
    soc_rows = soc_f - decay * previous + charge_f
    scarce_new = jnp.maximum(scarce - sigma * avail_rows, 0.0)
    sdual_new = sdual - sigma * soc_rows
    halves = (
        mean(disp_new, disp),
        mean(build_new, build),
        mean(disch_new, disch),
        mean(level_new, level),
        mean(scarce_new, scarce),
        mean(sdual_new, sdual),
    )
    return balance, halves, link_c


def first_local(
    season, avail, asset_bus, run_cost, build_cost, efficiency, power, energy, link,
    disp, build, disch, level, scarce, sdual, price, got, lines_got, arrive, cap, far,
    disp1, build1, disch1, level1, scarce1, sdual1, came1, balance, rows, moves, turn,
):
    consts = (avail, asset_bus, run_cost, build_cost, efficiency, power, energy, link)
    state = (disp[...], build[...], disch[...], level[...], scarce[...], sdual[...])
    came0, near, _ = unpack(lines_got)
    moved, came_x = line_step(came0, near, wide(far[...]), cap[...], step_size)
    came1[...] = mean(moved, came0)
    sums, before, after = season_parts(got, season[0])
    local, halves, link_c = local_step(
        sums, before, after, consts, state, price[...], turn, step_size, step_size
    )
    balance[...] = local + dot_t(arrive[...], came_x)
    for ref, value in zip((disp1, build1, disch1, level1, scarce1, sdual1), halves):
        ref[...] = value
    sums = jnp.sum(wide(avail[...]) * wide(narrow(halves[4])), axis=1, keepdims=True)
    rows[...] = season_block(sums, halves[3], wide(narrow(halves[5])), link_c)
    primal = (
        square(halves[0], state[0])
        + square(halves[1], state[1]) * (1.0 / SEASONS)
        + square(halves[2], state[2])
        + square(halves[3], state[3])
    )
    dual = square(halves[4], state[4]) + square(halves[5], state[5])
    lane = iota((8, 128), 1)
    moves[...] = jnp.where(lane == 0, primal, dual)


def price_step(
    flow0, near0, cap, leave, arrive, got, demand, price, balance, moves,
    price1, flow1, far0, sent,
):
    f0 = flow0[...]
    leave_t = leave[...]
    moved, flow_x = line_step(f0, wide(near0[...]), wide(got[...]), cap[...], step_size)
    f1 = mean(moved, f0)
    flow1[...] = f1
    p0 = price[...]
    whole = balance[...] - dot_t(leave_t, flow_x)
    p1 = mean(p0 + step_size * (demand[...] - whole), p0)
    price1[...] = p1
    primal = moves[0:1, 0:1] + square(f1, f0)
    dual = moves[0:1, 1:2] + square(p1, p0)
    lane = iota((GROUP, 128), 1)
    held = jnp.zeros((GROUP, 128), F32)
    for at, value in ((0, primal), (3, dual)):
        for step in range(3):
            piece = wide(narrow(value))
            held = jnp.where(lane == at + step, piece, held)
            value = value - piece
    held = narrow(held)
    price_b = narrow(p1)
    near = narrow(dot(leave_t, price_b))
    far = narrow(dot(arrive[...], price_b))
    far0[...] = far
    pack(near, far, jnp.concatenate([held] * (REGIONS // GROUP), axis=0), sent)


def moves_out(got, rows, sent):
    at = iota((8, REGIONS * ROWS_EACH), 1)
    q = (at * (262144 // ROWS_EACH + 1)) >> 18
    mask = as_bf(at - ROWS_EACH * q == 2 * LINK_CAP)
    moves = dot(mask, got[...])
    held = jnp.where(iota((8, 128), 0) == 4, moves, rows[...])
    for s in range(SEASONS):
        sent[s] = held


def second_step(
    season, avail, asset_bus, run_cost, build_cost, efficiency, power, energy, link,
    disp, build, disch, level, scarce, sdual, price, got, lines_got, arrive, came_cap,
    came_far, came, demand, flow, cap, leave,
    *refs,
):
    outs, turn, held, sems = refs[:8], refs[8], refs[9:17], refs[17]
    copies = []

    def give(at, value):
        held[at][...] = value
        copy = pltpu.make_async_copy(held[at], outs[at], sems.at[at])
        copy.start()
        copies.append(copy)

    moves = tree([got[s, 4:5] for s in range(SEASONS)])
    primal = moves[:, 0:1] + moves[:, 1:2] + moves[:, 2:3]
    dual = moves[:, 3:4] + moves[:, 4:5] + moves[:, 5:6]
    weight = jnp.sqrt(jnp.sqrt((dual + 1e-06) / (primal + 1e-06)))
    tau = step_size / weight
    sigma = step_size * weight
    consts = (avail, asset_bus, run_cost, build_cost, efficiency, power, energy, link)
    state = (disp[...], build[...], disch[...], level[...], scarce[...], sdual[...])
    came_near, far, _ = unpack(lines_got)
    _, came_x = line_step(came[...], came_near, wide(came_far[...]), came_cap[...], tau)
    f1 = flow[...]
    p1 = price[...]
    leave_t = leave[...]
    near = dot(leave_t, narrow(p1))
    moved, flow_x = line_step(f1, near, far, cap[...], tau)
    give(2, mean(moved, f1))
    sums, before, after = season_parts(got, season[0])
    local, halves, _ = local_step(
        sums, before, after, consts, state, p1, turn, tau, sigma
    )
    whole = local + dot_t(arrive[...], came_x) - dot_t(leave_t, flow_x)
    for at, value in zip((0, 1, 3, 4, 6, 7), halves):
        give(at, value)
    give(5, mean(p1 + sigma * (demand[...] - whole), p1))
    for copy in copies:
        copy.wait()


def call(body, outs, *operands, scalar=False, turn=False, fetched=False, streamed=0):
    space = pltpu.HBM if fetched else pltpu.VMEM
    in_specs = [pl.BlockSpec(memory_space=space)] * len(operands)
    out_specs = [pl.BlockSpec(memory_space=pltpu.HBM)] * streamed
    out_specs += [pl.BlockSpec(memory_space=pltpu.VMEM)] * (len(outs) - streamed)
    scratch = [pltpu.VMEM((128, 128), F32)] if turn else []
    if fetched:
        operands = [pltpu.with_memory_space_constraint(v, pltpu.HBM) for v in operands]
        scratch += [pltpu.VMEM(v.shape, v.dtype) for v in operands]
        scratch += [pltpu.SemaphoreType.DMA((len(operands),))]
    if streamed:
        scratch += [pltpu.VMEM(shape, kind) for shape, kind in outs[:streamed]]
        scratch += [pltpu.SemaphoreType.DMA((8,))]
    if scalar:
        in_specs[0] = pl.BlockSpec(memory_space=pltpu.SMEM)
    return pl.pallas_call(
        body,
        out_shape=[jax.ShapeDtypeStruct(shape, kind) for shape, kind in outs],
        in_specs=in_specs,
        out_specs=out_specs,
        scratch_shapes=scratch,
        compiler_params=pltpu.CompilerParams(vmem_limit_bytes=32 * 1024 * 1024),
    )(*operands)


def region_exchange(value, rows, per_pair):
    cut = value.reshape(REGIONS, per_pair, rows, HOUR)
    got = lax.all_to_all(cut, "region", split_axis=0, concat_axis=0, tiled=True)
    return got.reshape(value.shape)


def season_exchange(value):
    return lax.all_to_all(value, "season", split_axis=0, concat_axis=0, tiled=True)


def on_device(
    demand,
    avail,
    asset_bus,
    run_cost,
    build_cost,
    line_from,
    line_to,
    link_count,
    line_limit,
    efficiency,
    power_limit,
    energy_limit,
    season_link,
    dispatch,
    capacity,
    flow,
    charge,
    soc,
    price,
    scarcity,
    soc_dual,
):
    season = lax.axis_index("season").astype(I32).reshape(1)
    pair = lambda v: v.reshape(2, 128)
    short = lambda v: v.reshape(1, BUS)
    link = short(season_link)
    lines = ((SLOT, HOUR), F32)
    lines_b = ((SLOT, HOUR), BF16)
    buses = ((BUS, HOUR), F32)
    picks = ((SLOT, BUS), BF16)
    packed = ((REGIONS * ROWS_EACH, HOUR), BF16)
    seasons = ((SEASONS, 8, 128), F32)
    consts = (
        avail,
        pair(asset_bus),
        pair(run_cost),
        pair(build_cost),
        short(efficiency),
        short(power_limit),
        short(energy_limit),
        link,
    )
    sent1, flow0, near0, cap, leave = call(
        lines_out,
        [packed, lines, lines_b, lines, picks],
        flow,
        price,
        pair(line_from),
        pair(line_to),
        pair(line_limit),
        link_count,
        turn=True,
        fetched=True,
        streamed=1,
    )
    got1 = region_exchange(sent1, 2, 5)
    (rows1,) = call(season_out, [seasons], avail, scarcity, soc, soc_dual, link, turn=True, fetched=True)
    season1 = season_exchange(rows1)
    sent2, came_far0, arrive, came_cap = call(
        ends_in, [lines_b, lines_b, picks, lines], got1, price
    )
    got2 = region_exchange(sent2, LINK_CAP, 1)
    disp1, build1, disch1, level1, scarce1, sdual1, came1, balance, rows2, moves = call(
        first_local,
        [lines, ((2, 128), F32), buses, buses, lines, buses, lines, buses, ((8, 128), F32), ((8, 128), F32)],
        season,
        *consts,
        dispatch,
        pair(capacity),
        charge,
        soc,
        scarcity,
        soc_dual,
        price,
        season1,
        got1,
        arrive,
        came_cap,
        came_far0,
        scalar=True,
        turn=True,
    )
    price1, flow1, came_far1, sent3 = call(
        price_step,
        [buses, lines, lines_b, packed],
        flow0,
        near0,
        cap,
        leave,
        arrive,
        got2,
        demand,
        price,
        balance,
        moves,
    )
    got3 = region_exchange(sent3, 2, 5)
    (rows3,) = call(moves_out, [seasons], got3, rows2)
    season2 = season_exchange(rows3)
    disp2, build2, flow2, disch2, level2, price2, scarce2, sdual2 = call(
        second_step,
        [lines, ((2, 128), F32), lines, buses, buses, buses, lines, buses],
        season,
        *consts,
        disp1,
        build1,
        disch1,
        level1,
        scarce1,
        sdual1,
        price1,
        season2,
        got3,
        arrive,
        came_cap,
        came_far1,
        came1,
        demand,
        flow1,
        cap,
        leave,
        scalar=True,
        turn=True,
        streamed=8,
    )
    return (disp2, build2.reshape(capacity.shape), flow2, disch2, level2, price2, scarce2, sdual2)


def solution(mesh):
    both = P("region", "season")
    rows = P("region")
    in_specs = (
        both,
        both,
        rows,
        rows,
        rows,
        rows,
        rows,
        P("region", None),
        rows,
        rows,
        rows,
        rows,
        both,
        both,
        rows,
        both,
        both,
        both,
        both,
        both,
        both,
    )
    out_specs = (both, rows, both, both, both, both, both, both)
    return jax.shard_map(
        on_device, mesh=mesh, in_specs=in_specs, out_specs=out_specs, check_vma=False
    )
```

```python
import jax
import jax.numpy as jnp
from jax import lax
from jax.experimental import pallas as pl
from jax.experimental.pallas import tpu as pltpu
from jax.sharding import PartitionSpec as P

LINK_CAP = 4
GROUP = 16
step_size = 0.2
F32 = jnp.float32
BF16 = jnp.bfloat16
I32 = jnp.int32
REGIONS, SEASONS = 64, 8
BUS, SLOT, HOUR = 64, 256, 128
FIRST = 40
LINES = GROUP * LINK_CAP
ROWS_EACH = 2 * LINK_CAP + 2
PACKED = GROUP * ROWS_EACH
UNPACKED = 2 * LINES + GROUP


def iota(shape, axis):
    return lax.broadcasted_iota(I32, shape, axis)


def dot(a, b):
    return jnp.dot(a, b, preferred_element_type=F32)


def dot_t(a, b):
    return lax.dot_general(a, b, (((0,), (0,)), ((), ())), preferred_element_type=F32)


def as_bf(mask):
    return jnp.where(mask, 1.0, 0.0).astype(BF16)


def narrow(value):
    return value.astype(BF16)


def wide(value):
    return value.astype(F32)


def extrapolate(newer, older):
    return narrow(2.0 * newer - older)


def mean(newer, older):
    return 0.5 * (newer + older)


def total(value):
    return jnp.sum(jnp.sum(value, axis=1, keepdims=True), axis=0, keepdims=True)


def square(newer, older):
    moved = newer - older
    return total(moved * moved)


def row256(ref):
    return jnp.concatenate([ref[0:1, :], ref[1:2, :]], axis=1)


def pack_target(packed):
    q = (packed * (262144 // ROWS_EACH + 1)) >> 18
    j = packed - ROWS_EACH * q
    first = LINK_CAP * q + j
    second = LINES + first - LINK_CAP
    third = jnp.where(j == 2 * LINK_CAP, 2 * LINES + q, -1)
    return jnp.where(j < LINK_CAP, first, jnp.where(j < 2 * LINK_CAP, second, third))


def rolled(value, by):
    return jnp.concatenate([value[by:], value[:by]], axis=0)


def pack(first, second, third, out_ref):
    first = rolled(first, FIRST * LINK_CAP)
    second = rolled(second, FIRST * LINK_CAP)
    shape = (PACKED, UNPACKED)
    place = as_bf(pack_target(iota(shape, 0)) == iota(shape, 1))
    for g in range(REGIONS // GROUP):
        rows = jnp.concatenate(
            [
                first[g * LINES : (g + 1) * LINES],
                second[g * LINES : (g + 1) * LINES],
                third[g * GROUP : (g + 1) * GROUP],
            ],
            axis=0,
        )
        out_ref[g * PACKED : (g + 1) * PACKED, :] = narrow(dot(place, rows))


def unpack(ref):
    shape = (UNPACKED, PACKED)
    place = as_bf(pack_target(iota(shape, 1)) == iota(shape, 0))
    parts = [
        dot(place, ref[g * PACKED : (g + 1) * PACKED, :]) for g in range(REGIONS // GROUP)
    ]
    first = jnp.concatenate([p[:LINES] for p in parts], axis=0)
    second = jnp.concatenate([p[LINES : 2 * LINES] for p in parts], axis=0)
    third = jnp.concatenate([p[2 * LINES :] for p in parts], axis=0)
    back = REGIONS - FIRST
    return rolled(first, back * LINK_CAP), rolled(second, back * LINK_CAP), rolled(third, back)


def fetch(sources, held, sems):
    copies = [
        pltpu.make_async_copy(source, target, sems.at[at])
        for at, (source, target) in enumerate(zip(sources, held))
    ]
    for copy in copies:
        copy.start()
    for copy in copies:
        copy.wait()


def columns(ref):
    return jnp.transpose(ref[...])


def long_column(turned, at):
    return jnp.concatenate([turned[:, at : at + 1], turned[:, at + 1 : at + 2]], axis=0)


def onehot_rows(column, count):
    return as_bf(column == wide(iota((SLOT, count), 1)))


def lines_out(*refs):
    sent, flow0, near0, cap, leave, turn = refs[6:12]
    flow, price, line_from, line_to, line_limit, link_count, sems = refs[12:]
    fetch(refs[:6], refs[12:18], sems)
    lane = iota((1, SLOT), 1)
    spread = as_bf(iota((REGIONS, SLOT), 0) == lax.shift_right_logical(iota((REGIONS, SLOT), 1), 2))
    counts = jnp.broadcast_to(narrow(wide(link_count[...])), (8, REGIONS))
    counts = dot(counts, spread)[0:1]
    live = jnp.where(wide(lane & (LINK_CAP - 1)) < counts, 1.0, 0.0)
    limit = row256(line_limit) * live
    turn[0:2, :] = wide(line_from[...])
    turn[2:3, :] = live[:, :128]
    turn[3:4, :] = live[:, 128:]
    turn[4:5, :] = limit[:, :128]
    turn[5:6, :] = limit[:, 128:]
    turned = columns(turn)
    leave_t = onehot_rows(long_column(turned, 0), BUS)
    f0 = flow[...] * long_column(turned, 2)
    near = narrow(dot(leave_t, narrow(price[...])))
    flow0[...] = f0
    near0[...] = near
    cap[...] = jnp.broadcast_to(long_column(turned, 4), (SLOT, HOUR))
    leave[...] = leave_t
    high = wide(narrow(limit))
    low = limit - high
    held = jnp.zeros((REGIONS, 128), F32)
    slot_kind = iota((SLOT, 128), 0) & (LINK_CAP - 1)
    for at, value in enumerate((wide(row256(line_to)), high, low)):
        spots = as_bf(iota((SLOT, 128), 1) == slot_kind + LINK_CAP * at)
        held = held + dot(spread * narrow(value), spots)
    pack(narrow(f0), near, narrow(rolled(held, FIRST)), sent)


def season_block(sums, level, dual_f, link_column):
    lane = iota((128, 128), 1)
    tail = jnp.concatenate([level[:, HOUR - 1 : HOUR], dual_f[:, HOUR - 1 : HOUR]], axis=0)
    head = jnp.concatenate([dual_f[:, 0:1], link_column], axis=0)
    held = jnp.where(
        lane == 0,
        sums[:128],
        jnp.where(lane == 1, sums[128:], jnp.where(lane == 2, tail, jnp.where(lane == 3, head, 0.0))),
    )
    return jnp.transpose(held)[0:8]


def season_out(*refs):
    sent, turn, avail, scarcity, soc, soc_dual, link, sems = refs[5:]
    fetch(refs[:5], refs[7:12], sems)
    turn[0:1, 0:BUS] = wide(link[...])
    turned = columns(turn)
    sums = jnp.sum(wide(avail[...]) * wide(narrow(scarcity[...])), axis=1, keepdims=True)
    rows = season_block(sums, soc[...], wide(narrow(soc_dual[...])), turned[:BUS, 0:1])
    for s in range(SEASONS):
        sent[s] = rows


def ends_in(got, price, sent, far, arrive, cap):
    _, _, held = unpack(got)
    shape = (SLOT, REGIONS)
    spread = as_bf(iota(shape, 1) == iota(shape, 0) >> 2)
    lines = dot(spread, narrow(held))
    lane = iota((SLOT, 128), 1)
    kind = iota((SLOT, 128), 0) & (LINK_CAP - 1)
    ends = jnp.sum(jnp.where(lane == kind, lines, 0.0), axis=1, keepdims=True)
    limits = (lane == kind + LINK_CAP) | (lane == kind + 2 * LINK_CAP)
    limit = jnp.sum(jnp.where(limits, lines, 0.0), axis=1, keepdims=True)
    arrive_t = onehot_rows(ends, BUS)
    values = narrow(dot(arrive_t, narrow(price[...])))
    far[...] = values
    sent[...] = rolled(values, FIRST * LINK_CAP)
    arrive[...] = arrive_t
    cap[...] = jnp.broadcast_to(limit, (SLOT, HOUR))


def line_step(flows, near, far, cap, tau):
    moved = jnp.clip(flows + tau * (far - near), -cap, cap)
    return moved, extrapolate(moved, flows)


def tree(values):
    while len(values) > 1:
        values = [values[i] + values[i + 1] for i in range(0, len(values), 2)]
    return values[0]


def season_parts(got, season):
    sums = tree([got[s, 0:2] for s in range(SEASONS)])
    before = got[(season + SEASONS - 1) & (SEASONS - 1), 2:4]
    after = got[(season + 1) & (SEASONS - 1), 2:4]
    return sums, before, after


def local_step(sums, before, after, consts, state, price_v, turn, tau, sigma):
    avail, asset_bus, run_cost, build_cost, efficiency, power, energy, link = consts
    disp, build, disch, level, scarce, sdual = state
    grad_build = sums * (1.0 / (HOUR * SEASONS))
    build_new = jnp.maximum(build - tau * (build_cost[...] - grad_build), 0.0)
    turn[2:4, :] = before
    turn[10:12, :] = after
    turn[16:18, :] = wide(extrapolate(build_new, build))
    turn[18:20, :] = run_cost[...]
    turn[20:22, :] = wide(asset_bus[...])
    turn[22:23, 0:BUS] = efficiency[...]
    turn[23:24, 0:BUS] = power[...]
    turn[24:25, 0:BUS] = energy[...]
    turn[25:26, 0:BUS] = wide(link[...])
    turned = columns(turn)
    build_x = long_column(turned, 16)
    cost = long_column(turned, 18)
    asset_t = onehot_rows(long_column(turned, 20), BUS)
    asset_row = row256(asset_bus)
    asset_onehot = as_bf(iota((BUS, SLOT), 0) == asset_row)
    decay = turned[:BUS, 22:23]
    power_c = turned[:BUS, 23:24]
    energy_c = turned[:BUS, 24:25]
    link_c = turned[:BUS, 25:26]
    before_level, before_dual = turned[:BUS, 2:3], turned[BUS:, 2:3]
    before_first, before_link = turned[:BUS, 3:4], turned[BUS:, 3:4]
    after_first, after_link = turned[:BUS, 11:12], turned[BUS:, 11:12]
    price_b = narrow(price_v)
    dual_f = wide(narrow(sdual))
    grad_dispatch = dot(asset_t, price_b) - wide(narrow(scarce))
    grad_charge = wide(price_b) + dual_f
    first = dual_f[:, 0:1]
    after_last = (1.0 - link_c) * first + after_link * after_first
    following = jnp.concatenate([dual_f[:, 1:], after_last], axis=1)
    grad_soc = dual_f - decay * following
    before_grad = before_dual - decay * ((1.0 - before_link) * before_first + link_c * first)
    disp_new = jnp.maximum(disp - tau * (cost - grad_dispatch), 0.0)
    disch_new = jnp.clip(disch + tau * grad_charge, -power_c, power_c)
    level_new = jnp.clip(level + tau * grad_soc, 0.0, energy_c)
    before_new = jnp.clip(before_level + tau * before_grad, 0.0, energy_c)
    disp_x = extrapolate(disp_new, disp)
    charge_f = wide(extrapolate(disch_new, disch))
    soc_f = wide(extrapolate(level_new, level))
    before_x = wide(extrapolate(before_new, before_level))
    balance = dot(asset_onehot, disp_x) + charge_f
    avail_rows = wide(avail[...]) * build_x - wide(disp_x)
    carried = jnp.where(link_c == 1.0, before_x, soc_f[:, HOUR - 1 : HOUR])
    previous = jnp.concatenate([carried, soc_f[:, : HOUR - 1]], axis=1)
    soc_rows = soc_f - decay * previous + charge_f
    scarce_new = jnp.maximum(scarce - sigma * avail_rows, 0.0)
    sdual_new = sdual - sigma * soc_rows
    halves = (
        mean(disp_new, disp),
        mean(build_new, build),
        mean(disch_new, disch),
        mean(level_new, level),
        mean(scarce_new, scarce),
        mean(sdual_new, sdual),
    )
    return balance, halves, link_c


def first_local(
    season, avail, asset_bus, run_cost, build_cost, efficiency, power, energy, link,
    disp, build, disch, level, scarce, sdual, price, got, lines_got, arrive, cap, far,
    disp1, build1, disch1, level1, scarce1, sdual1, came1, balance, rows, moves, turn,
):
    consts = (avail, asset_bus, run_cost, build_cost, efficiency, power, energy, link)
    state = (disp[...], build[...], disch[...], level[...], scarce[...], sdual[...])
    came0, near, _ = unpack(lines_got)
    moved, came_x = line_step(came0, near, wide(far[...]), cap[...], step_size)
    came1[...] = mean(moved, came0)
    sums, before, after = season_parts(got, season[0])
    local, halves, link_c = local_step(
        sums, before, after, consts, state, price[...], turn, step_size, step_size
    )
    balance[...] = local + dot_t(arrive[...], came_x)
    for ref, value in zip((disp1, build1, disch1, level1, scarce1, sdual1), halves):
        ref[...] = value
    sums = jnp.sum(wide(avail[...]) * wide(narrow(halves[4])), axis=1, keepdims=True)
    rows[...] = season_block(sums, halves[3], wide(narrow(halves[5])), link_c)
    primal = (
        square(halves[0], state[0])
        + square(halves[1], state[1]) * (1.0 / SEASONS)
        + square(halves[2], state[2])
        + square(halves[3], state[3])
    )
    dual = square(halves[4], state[4]) + square(halves[5], state[5])
    lane = iota((8, 128), 1)
    moves[...] = jnp.where(lane == 0, primal, dual)


def price_step(
    flow0, near0, cap, leave, arrive, got, demand, price, balance, moves,
    price1, flow1, far0, sent,
):
    f0 = flow0[...]
    leave_t = leave[...]
    far = wide(rolled(got[...], (REGIONS - FIRST) * LINK_CAP))
    moved, flow_x = line_step(f0, wide(near0[...]), far, cap[...], step_size)
    f1 = mean(moved, f0)
    flow1[...] = f1
    p0 = price[...]
    whole = balance[...] - dot_t(leave_t, flow_x)
    p1 = mean(p0 + step_size * (demand[...] - whole), p0)
    price1[...] = p1
    primal = moves[0:1, 0:1] + square(f1, f0)
    dual = moves[0:1, 1:2] + square(p1, p0)
    lane = iota((GROUP, 128), 1)
    held = jnp.zeros((GROUP, 128), F32)
    for at, value in ((0, primal), (3, dual)):
        for step in range(3):
            piece = wide(narrow(value))
            held = jnp.where(lane == at + step, piece, held)
            value = value - piece
    held = narrow(held)
    price_b = narrow(p1)
    near = narrow(dot(leave_t, price_b))
    far = narrow(dot(arrive[...], price_b))
    far0[...] = far
    pack(near, far, jnp.concatenate([held] * (REGIONS // GROUP), axis=0), sent)


def moves_out(got, rows, sent):
    at = iota((8, REGIONS * ROWS_EACH), 1)
    q = (at * (262144 // ROWS_EACH + 1)) >> 18
    mask = as_bf(at - ROWS_EACH * q == 2 * LINK_CAP)
    moves = dot(mask, got[...])
    held = jnp.where(iota((8, 128), 0) == 4, moves, rows[...])
    for s in range(SEASONS):
        sent[s] = held


def second_step(
    season, avail, asset_bus, run_cost, build_cost, efficiency, power, energy, link,
    disp, build, disch, level, scarce, sdual, price, got, lines_got, arrive, came_cap,
    came_far, came, demand, flow, cap, leave,
    disp2, build2, flow2, disch2, level2, price2, scarce2, sdual2, turn,
):
    moves = tree([got[s, 4:5] for s in range(SEASONS)])
    primal = moves[:, 0:1] + moves[:, 1:2] + moves[:, 2:3]
    dual = moves[:, 3:4] + moves[:, 4:5] + moves[:, 5:6]
    weight = jnp.sqrt(jnp.sqrt((dual + 1e-06) / (primal + 1e-06)))
    tau = step_size / weight
    sigma = step_size * weight
    consts = (avail, asset_bus, run_cost, build_cost, efficiency, power, energy, link)
    state = (disp[...], build[...], disch[...], level[...], scarce[...], sdual[...])
    came_near, far, _ = unpack(lines_got)
    _, came_x = line_step(came[...], came_near, wide(came_far[...]), came_cap[...], tau)
    f1 = flow[...]
    p1 = price[...]
    leave_t = leave[...]
    near = dot(leave_t, narrow(p1))
    moved, flow_x = line_step(f1, near, far, cap[...], tau)
    flow2[...] = mean(moved, f1)
    sums, before, after = season_parts(got, season[0])
    local, halves, _ = local_step(
        sums, before, after, consts, state, p1, turn, tau, sigma
    )
    whole = local + dot_t(arrive[...], came_x) - dot_t(leave_t, flow_x)
    price2[...] = mean(p1 + sigma * (demand[...] - whole), p1)
    for ref, value in zip((disp2, build2, disch2, level2, scarce2, sdual2), halves):
        ref[...] = value


def call(body, outs, *operands, scalar=False, turn=False, fetched=False):
    space = pltpu.HBM if fetched else pltpu.VMEM
    in_specs = [pl.BlockSpec(memory_space=space)] * len(operands)
    scratch = [pltpu.VMEM((128, 128), F32)] if turn else []
    if fetched:
        operands = [pltpu.with_memory_space_constraint(v, pltpu.HBM) for v in operands]
        scratch += [pltpu.VMEM(v.shape, v.dtype) for v in operands]
        scratch += [pltpu.SemaphoreType.DMA((len(operands),))]
    if scalar:
        in_specs[0] = pl.BlockSpec(memory_space=pltpu.SMEM)
    return pl.pallas_call(
        body,
        out_shape=[jax.ShapeDtypeStruct(shape, kind) for shape, kind in outs],
        in_specs=in_specs,
        out_specs=[pl.BlockSpec(memory_space=pltpu.VMEM)] * len(outs),
        scratch_shapes=scratch,
        compiler_params=pltpu.CompilerParams(vmem_limit_bytes=32 * 1024 * 1024),
    )(*operands)


def region_exchange(value, rows, per_pair):
    cut = value.reshape(REGIONS, per_pair, rows, HOUR)
    members = [[(FIRST + place) % REGIONS for place in range(REGIONS)]]
    got = lax.all_to_all(cut, "region", 0, 0, axis_index_groups=members, tiled=True)
    return got.reshape(value.shape)


def season_exchange(value):
    return lax.all_to_all(value, "season", split_axis=0, concat_axis=0, tiled=True)


def on_device(
    demand,
    avail,
    asset_bus,
    run_cost,
    build_cost,
    line_from,
    line_to,
    link_count,
    line_limit,
    efficiency,
    power_limit,
    energy_limit,
    season_link,
    dispatch,
    capacity,
    flow,
    charge,
    soc,
    price,
    scarcity,
    soc_dual,
):
    season = lax.axis_index("season").astype(I32).reshape(1)
    pair = lambda v: v.reshape(2, 128)
    short = lambda v: v.reshape(1, BUS)
    link = short(season_link)
    lines = ((SLOT, HOUR), F32)
    lines_b = ((SLOT, HOUR), BF16)
    buses = ((BUS, HOUR), F32)
    picks = ((SLOT, BUS), BF16)
    packed = ((REGIONS * ROWS_EACH, HOUR), BF16)
    seasons = ((SEASONS, 8, 128), F32)
    consts = (
        avail,
        pair(asset_bus),
        pair(run_cost),
        pair(build_cost),
        short(efficiency),
        short(power_limit),
        short(energy_limit),
        link,
    )
    sent1, flow0, near0, cap, leave = call(
        lines_out,
        [packed, lines, lines_b, lines, picks],
        flow,
        price,
        pair(line_from),
        pair(line_to),
        pair(line_limit),
        link_count,
        turn=True,
        fetched=True,
    )
    got1 = region_exchange(sent1, 2, 5)
    (rows1,) = call(season_out, [seasons], avail, scarcity, soc, soc_dual, link, turn=True, fetched=True)
    season1 = season_exchange(rows1)
    sent2, came_far0, arrive, came_cap = call(
        ends_in, [lines_b, lines_b, picks, lines], got1, price
    )
    got2 = region_exchange(sent2, LINK_CAP, 1)
    disp1, build1, disch1, level1, scarce1, sdual1, came1, balance, rows2, moves = call(
        first_local,
        [lines, ((2, 128), F32), buses, buses, lines, buses, lines, buses, ((8, 128), F32), ((8, 128), F32)],
        season,
        *consts,
        dispatch,
        pair(capacity),
        charge,
        soc,
        scarcity,
        soc_dual,
        price,
        season1,
        got1,
        arrive,
        came_cap,
        came_far0,
        scalar=True,
        turn=True,
    )
    price1, flow1, came_far1, sent3 = call(
        price_step,
        [buses, lines, lines_b, packed],
        flow0,
        near0,
        cap,
        leave,
        arrive,
        got2,
        demand,
        price,
        balance,
        moves,
    )
    got3 = region_exchange(sent3, 2, 5)
    (rows3,) = call(moves_out, [seasons], got3, rows2)
    season2 = season_exchange(rows3)
    disp2, build2, flow2, disch2, level2, price2, scarce2, sdual2 = call(
        second_step,
        [lines, ((2, 128), F32), lines, buses, buses, buses, lines, buses],
        season,
        *consts,
        disp1,
        build1,
        disch1,
        level1,
        scarce1,
        sdual1,
        price1,
        season2,
        got3,
        arrive,
        came_cap,
        came_far1,
        came1,
        demand,
        flow1,
        cap,
        leave,
        scalar=True,
        turn=True,
    )
    return (disp2, build2.reshape(capacity.shape), flow2, disch2, level2, price2, scarce2, sdual2)


def solution(mesh):
    both = P("region", "season")
    rows = P("region")
    in_specs = (
        both,
        both,
        rows,
        rows,
        rows,
        rows,
        rows,
        P("region", None),
        rows,
        rows,
        rows,
        rows,
        both,
        both,
        rows,
        both,
        both,
        both,
        both,
        both,
        both,
    )
    out_specs = (both, rows, both, both, both, both, both, both)
    return jax.shard_map(
        on_device, mesh=mesh, in_specs=in_specs, out_specs=out_specs, check_vma=False
    )
```

```python
import jax
import jax.numpy as jnp
from jax import lax
from jax.experimental import pallas as pl
from jax.experimental.pallas import tpu as pltpu
from jax.sharding import PartitionSpec as P

LINK_CAP = 4
GROUP = 16
step_size = 0.2
F32 = jnp.float32
BF16 = jnp.bfloat16
I32 = jnp.int32
REGIONS, SEASONS = 64, 8
BUS, SLOT, HOUR = 64, 256, 128
FIRST, FIRST_SEASON = 40, 4
LINES = GROUP * LINK_CAP
ROWS_EACH = 2 * LINK_CAP + 2
PACKED = GROUP * ROWS_EACH
UNPACKED = 2 * LINES + GROUP


def iota(shape, axis):
    return lax.broadcasted_iota(I32, shape, axis)


def dot(a, b):
    return jnp.dot(a, b, preferred_element_type=F32)


def dot_t(a, b):
    return lax.dot_general(a, b, (((0,), (0,)), ((), ())), preferred_element_type=F32)


def as_bf(mask):
    return jnp.where(mask, 1.0, 0.0).astype(BF16)


def narrow(value):
    return value.astype(BF16)


def wide(value):
    return value.astype(F32)


def extrapolate(newer, older):
    return narrow(2.0 * newer - older)


def mean(newer, older):
    return 0.5 * (newer + older)


def total(value):
    return jnp.sum(jnp.sum(value, axis=1, keepdims=True), axis=0, keepdims=True)


def square(newer, older):
    moved = newer - older
    return total(moved * moved)


def row256(ref):
    return jnp.concatenate([ref[0:1, :], ref[1:2, :]], axis=1)


def pack_target(packed):
    q = (packed * (262144 // ROWS_EACH + 1)) >> 18
    j = packed - ROWS_EACH * q
    first = LINK_CAP * q + j
    second = LINES + first - LINK_CAP
    third = jnp.where(j == 2 * LINK_CAP, 2 * LINES + q, -1)
    return jnp.where(j < LINK_CAP, first, jnp.where(j < 2 * LINK_CAP, second, third))


def rolled(value, by):
    return jnp.concatenate([value[by:], value[:by]], axis=0)


def pack(first, second, third, out_ref):
    first = rolled(first, FIRST * LINK_CAP)
    second = rolled(second, FIRST * LINK_CAP)
    shape = (PACKED, UNPACKED)
    place = as_bf(pack_target(iota(shape, 0)) == iota(shape, 1))
    for g in range(REGIONS // GROUP):
        rows = jnp.concatenate(
            [
                first[g * LINES : (g + 1) * LINES],
                second[g * LINES : (g + 1) * LINES],
                third[g * GROUP : (g + 1) * GROUP],
            ],
            axis=0,
        )
        out_ref[g * PACKED : (g + 1) * PACKED, :] = narrow(dot(place, rows))


def unpack(ref):
    shape = (UNPACKED, PACKED)
    place = as_bf(pack_target(iota(shape, 1)) == iota(shape, 0))
    parts = [
        dot(place, ref[g * PACKED : (g + 1) * PACKED, :]) for g in range(REGIONS // GROUP)
    ]
    first = jnp.concatenate([p[:LINES] for p in parts], axis=0)
    second = jnp.concatenate([p[LINES : 2 * LINES] for p in parts], axis=0)
    third = jnp.concatenate([p[2 * LINES :] for p in parts], axis=0)
    back = REGIONS - FIRST
    return rolled(first, back * LINK_CAP), rolled(second, back * LINK_CAP), rolled(third, back)


def fetch(sources, held, sems):
    copies = [
        pltpu.make_async_copy(source, target, sems.at[at])
        for at, (source, target) in enumerate(zip(sources, held))
    ]
    for copy in copies:
        copy.start()
    for copy in copies:
        copy.wait()


def columns(ref):
    return jnp.transpose(ref[...])


def long_column(turned, at):
    return jnp.concatenate([turned[:, at : at + 1], turned[:, at + 1 : at + 2]], axis=0)


def onehot_rows(column, count):
    return as_bf(column == wide(iota((SLOT, count), 1)))


def lines_out(*refs):
    sent, flow0, near0, cap, leave, turn = refs[6:12]
    flow, price, line_from, line_to, line_limit, link_count, sems = refs[12:]
    fetch(refs[:6], refs[12:18], sems)
    lane = iota((1, SLOT), 1)
    spread = as_bf(iota((REGIONS, SLOT), 0) == lax.shift_right_logical(iota((REGIONS, SLOT), 1), 2))
    counts = jnp.broadcast_to(narrow(wide(link_count[...])), (8, REGIONS))
    counts = dot(counts, spread)[0:1]
    live = jnp.where(wide(lane & (LINK_CAP - 1)) < counts, 1.0, 0.0)
    limit = row256(line_limit) * live
    turn[0:2, :] = wide(line_from[...])
    turn[2:3, :] = live[:, :128]
    turn[3:4, :] = live[:, 128:]
    turn[4:5, :] = limit[:, :128]
    turn[5:6, :] = limit[:, 128:]
    turned = columns(turn)
    leave_t = onehot_rows(long_column(turned, 0), BUS)
    f0 = flow[...] * long_column(turned, 2)
    near = narrow(dot(leave_t, narrow(price[...])))
    flow0[...] = f0
    near0[...] = near
    cap[...] = jnp.broadcast_to(long_column(turned, 4), (SLOT, HOUR))
    leave[...] = leave_t
    high = wide(narrow(limit))
    low = limit - high
    held = jnp.zeros((REGIONS, 128), F32)
    slot_kind = iota((SLOT, 128), 0) & (LINK_CAP - 1)
    for at, value in enumerate((wide(row256(line_to)), high, low)):
        spots = as_bf(iota((SLOT, 128), 1) == slot_kind + LINK_CAP * at)
        held = held + dot(spread * narrow(value), spots)
    pack(narrow(f0), near, narrow(rolled(held, FIRST)), sent)


def season_block(sums, level, dual_f, link_column):
    lane = iota((128, 128), 1)
    tail = jnp.concatenate([level[:, HOUR - 1 : HOUR], dual_f[:, HOUR - 1 : HOUR]], axis=0)
    head = jnp.concatenate([dual_f[:, 0:1], link_column], axis=0)
    held = jnp.where(
        lane == 0,
        sums[:128],
        jnp.where(lane == 1, sums[128:], jnp.where(lane == 2, tail, jnp.where(lane == 3, head, 0.0))),
    )
    return jnp.transpose(held)[0:8]


def season_out(*refs):
    sent, turn, avail, scarcity, soc, soc_dual, link, sems = refs[5:]
    fetch(refs[:5], refs[7:12], sems)
    turn[0:1, 0:BUS] = wide(link[...])
    turned = columns(turn)
    sums = jnp.sum(wide(avail[...]) * wide(narrow(scarcity[...])), axis=1, keepdims=True)
    rows = season_block(sums, soc[...], wide(narrow(soc_dual[...])), turned[:BUS, 0:1])
    for s in range(SEASONS):
        sent[s] = rows


def ends_in(got, price, sent, far, arrive, cap):
    _, _, held = unpack(got)
    shape = (SLOT, REGIONS)
    spread = as_bf(iota(shape, 1) == iota(shape, 0) >> 2)
    lines = dot(spread, narrow(held))
    lane = iota((SLOT, 128), 1)
    kind = iota((SLOT, 128), 0) & (LINK_CAP - 1)
    ends = jnp.sum(jnp.where(lane == kind, lines, 0.0), axis=1, keepdims=True)
    limits = (lane == kind + LINK_CAP) | (lane == kind + 2 * LINK_CAP)
    limit = jnp.sum(jnp.where(limits, lines, 0.0), axis=1, keepdims=True)
    arrive_t = onehot_rows(ends, BUS)
    values = narrow(dot(arrive_t, narrow(price[...])))
    far[...] = values
    sent[...] = rolled(values, FIRST * LINK_CAP)
    arrive[...] = arrive_t
    cap[...] = jnp.broadcast_to(limit, (SLOT, HOUR))


def line_step(flows, near, far, cap, tau):
    moved = jnp.clip(flows + tau * (far - near), -cap, cap)
    return moved, extrapolate(moved, flows)


def tree(values):
    while len(values) > 1:
        values = [values[i] + values[i + 1] for i in range(0, len(values), 2)]
    return values[0]


def season_parts(got, season):
    sums = tree([got[s, 0:2] for s in range(SEASONS)])
    before = got[((season + SEASONS - 1) & (SEASONS - 1)) ^ FIRST_SEASON, 2:4]
    after = got[((season + 1) & (SEASONS - 1)) ^ FIRST_SEASON, 2:4]
    return sums, before, after


def local_step(sums, before, after, consts, state, price_v, turn, tau, sigma):
    avail, asset_bus, run_cost, build_cost, efficiency, power, energy, link = consts
    disp, build, disch, level, scarce, sdual = state
    grad_build = sums * (1.0 / (HOUR * SEASONS))
    build_new = jnp.maximum(build - tau * (build_cost[...] - grad_build), 0.0)
    turn[2:4, :] = before
    turn[10:12, :] = after
    turn[16:18, :] = wide(extrapolate(build_new, build))
    turn[18:20, :] = run_cost[...]
    turn[20:22, :] = wide(asset_bus[...])
    turn[22:23, 0:BUS] = efficiency[...]
    turn[23:24, 0:BUS] = power[...]
    turn[24:25, 0:BUS] = energy[...]
    turn[25:26, 0:BUS] = wide(link[...])
    turned = columns(turn)
    build_x = long_column(turned, 16)
    cost = long_column(turned, 18)
    asset_t = onehot_rows(long_column(turned, 20), BUS)
    asset_row = row256(asset_bus)
    asset_onehot = as_bf(iota((BUS, SLOT), 0) == asset_row)
    decay = turned[:BUS, 22:23]
    power_c = turned[:BUS, 23:24]
    energy_c = turned[:BUS, 24:25]
    link_c = turned[:BUS, 25:26]
    before_level, before_dual = turned[:BUS, 2:3], turned[BUS:, 2:3]
    before_first, before_link = turned[:BUS, 3:4], turned[BUS:, 3:4]
    after_first, after_link = turned[:BUS, 11:12], turned[BUS:, 11:12]
    price_b = narrow(price_v)
    dual_f = wide(narrow(sdual))
    grad_dispatch = dot(asset_t, price_b) - wide(narrow(scarce))
    grad_charge = wide(price_b) + dual_f
    first = dual_f[:, 0:1]
    after_last = (1.0 - link_c) * first + after_link * after_first
    following = jnp.concatenate([dual_f[:, 1:], after_last], axis=1)
    grad_soc = dual_f - decay * following
    before_grad = before_dual - decay * ((1.0 - before_link) * before_first + link_c * first)
    disp_new = jnp.maximum(disp - tau * (cost - grad_dispatch), 0.0)
    disch_new = jnp.clip(disch + tau * grad_charge, -power_c, power_c)
    level_new = jnp.clip(level + tau * grad_soc, 0.0, energy_c)
    before_new = jnp.clip(before_level + tau * before_grad, 0.0, energy_c)
    disp_x = extrapolate(disp_new, disp)
    charge_f = wide(extrapolate(disch_new, disch))
    soc_f = wide(extrapolate(level_new, level))
    before_x = wide(extrapolate(before_new, before_level))
    balance = dot(asset_onehot, disp_x) + charge_f
    avail_rows = wide(avail[...]) * build_x - wide(disp_x)
    carried = jnp.where(link_c == 1.0, before_x, soc_f[:, HOUR - 1 : HOUR])
    previous = jnp.concatenate([carried, soc_f[:, : HOUR - 1]], axis=1)
    soc_rows = soc_f - decay * previous + charge_f
    scarce_new = jnp.maximum(scarce - sigma * avail_rows, 0.0)
    sdual_new = sdual - sigma * soc_rows
    halves = (
        mean(disp_new, disp),
        mean(build_new, build),
        mean(disch_new, disch),
        mean(level_new, level),
        mean(scarce_new, scarce),
        mean(sdual_new, sdual),
    )
    return balance, halves, link_c


def first_local(
    season, avail, asset_bus, run_cost, build_cost, efficiency, power, energy, link,
    disp, build, disch, level, scarce, sdual, price, got, lines_got, arrive, cap, far,
    disp1, build1, disch1, level1, scarce1, sdual1, came1, balance, rows, moves, turn,
):
    consts = (avail, asset_bus, run_cost, build_cost, efficiency, power, energy, link)
    state = (disp[...], build[...], disch[...], level[...], scarce[...], sdual[...])
    came0, near, _ = unpack(lines_got)
    moved, came_x = line_step(came0, near, wide(far[...]), cap[...], step_size)
    came1[...] = mean(moved, came0)
    sums, before, after = season_parts(got, season[0])
    local, halves, link_c = local_step(
        sums, before, after, consts, state, price[...], turn, step_size, step_size
    )
    balance[...] = local + dot_t(arrive[...], came_x)
    for ref, value in zip((disp1, build1, disch1, level1, scarce1, sdual1), halves):
        ref[...] = value
    sums = jnp.sum(wide(avail[...]) * wide(narrow(halves[4])), axis=1, keepdims=True)
    rows[...] = season_block(sums, halves[3], wide(narrow(halves[5])), link_c)
    primal = (
        square(halves[0], state[0])
        + square(halves[1], state[1]) * (1.0 / SEASONS)
        + square(halves[2], state[2])
        + square(halves[3], state[3])
    )
    dual = square(halves[4], state[4]) + square(halves[5], state[5])
    lane = iota((8, 128), 1)
    moves[...] = jnp.where(lane == 0, primal, dual)


def price_step(
    flow0, near0, cap, leave, arrive, got, demand, price, balance, moves,
    price1, flow1, far0, sent,
):
    f0 = flow0[...]
    leave_t = leave[...]
    far = wide(rolled(got[...], (REGIONS - FIRST) * LINK_CAP))
    moved, flow_x = line_step(f0, wide(near0[...]), far, cap[...], step_size)
    f1 = mean(moved, f0)
    flow1[...] = f1
    p0 = price[...]
    whole = balance[...] - dot_t(leave_t, flow_x)
    p1 = mean(p0 + step_size * (demand[...] - whole), p0)
    price1[...] = p1
    primal = moves[0:1, 0:1] + square(f1, f0)
    dual = moves[0:1, 1:2] + square(p1, p0)
    lane = iota((GROUP, 128), 1)
    held = jnp.zeros((GROUP, 128), F32)
    for at, value in ((0, primal), (3, dual)):
        for step in range(3):
            piece = wide(narrow(value))
            held = jnp.where(lane == at + step, piece, held)
            value = value - piece
    held = narrow(held)
    price_b = narrow(p1)
    near = narrow(dot(leave_t, price_b))
    far = narrow(dot(arrive[...], price_b))
    far0[...] = far
    pack(near, far, jnp.concatenate([held] * (REGIONS // GROUP), axis=0), sent)


def moves_out(got, rows, sent):
    at = iota((8, REGIONS * ROWS_EACH), 1)
    q = (at * (262144 // ROWS_EACH + 1)) >> 18
    mask = as_bf(at - ROWS_EACH * q == 2 * LINK_CAP)
    moves = dot(mask, got[...])
    held = jnp.where(iota((8, 128), 0) == 4, moves, rows[...])
    for s in range(SEASONS):
        sent[s] = held


def second_step(
    season, avail, asset_bus, run_cost, build_cost, efficiency, power, energy, link,
    disp, build, disch, level, scarce, sdual, price, got, lines_got, arrive, came_cap,
    came_far, came, demand, flow, cap, leave,
    disp2, build2, flow2, disch2, level2, price2, scarce2, sdual2, turn,
):
    moves = tree([got[s, 4:5] for s in range(SEASONS)])
    primal = moves[:, 0:1] + moves[:, 1:2] + moves[:, 2:3]
    dual = moves[:, 3:4] + moves[:, 4:5] + moves[:, 5:6]
    weight = jnp.sqrt(jnp.sqrt((dual + 1e-06) / (primal + 1e-06)))
    tau = step_size / weight
    sigma = step_size * weight
    consts = (avail, asset_bus, run_cost, build_cost, efficiency, power, energy, link)
    state = (disp[...], build[...], disch[...], level[...], scarce[...], sdual[...])
    came_near, far, _ = unpack(lines_got)
    _, came_x = line_step(came[...], came_near, wide(came_far[...]), came_cap[...], tau)
    f1 = flow[...]
    p1 = price[...]
    leave_t = leave[...]
    near = dot(leave_t, narrow(p1))
    moved, flow_x = line_step(f1, near, far, cap[...], tau)
    flow2[...] = mean(moved, f1)
    sums, before, after = season_parts(got, season[0])
    local, halves, _ = local_step(
        sums, before, after, consts, state, p1, turn, tau, sigma
    )
    whole = local + dot_t(arrive[...], came_x) - dot_t(leave_t, flow_x)
    price2[...] = mean(p1 + sigma * (demand[...] - whole), p1)
    for ref, value in zip((disp2, build2, disch2, level2, scarce2, sdual2), halves):
        ref[...] = value


def call(body, outs, *operands, scalar=False, turn=False, fetched=False):
    space = pltpu.HBM if fetched else pltpu.VMEM
    in_specs = [pl.BlockSpec(memory_space=space)] * len(operands)
    scratch = [pltpu.VMEM((128, 128), F32)] if turn else []
    if fetched:
        operands = [pltpu.with_memory_space_constraint(v, pltpu.HBM) for v in operands]
        scratch += [pltpu.VMEM(v.shape, v.dtype) for v in operands]
        scratch += [pltpu.SemaphoreType.DMA((len(operands),))]
    if scalar:
        in_specs[0] = pl.BlockSpec(memory_space=pltpu.SMEM)
    return pl.pallas_call(
        body,
        out_shape=[jax.ShapeDtypeStruct(shape, kind) for shape, kind in outs],
        in_specs=in_specs,
        out_specs=[pl.BlockSpec(memory_space=pltpu.VMEM)] * len(outs),
        scratch_shapes=scratch,
        compiler_params=pltpu.CompilerParams(vmem_limit_bytes=32 * 1024 * 1024),
    )(*operands)


def region_exchange(value, rows, per_pair):
    cut = value.reshape(REGIONS, per_pair, rows, HOUR)
    members = [[(FIRST + place) % REGIONS for place in range(REGIONS)]]
    got = lax.all_to_all(cut, "region", 0, 0, axis_index_groups=members, tiled=True)
    return got.reshape(value.shape)


def season_exchange(value):
    members = [[place ^ FIRST_SEASON for place in range(SEASONS)]]
    return lax.all_to_all(value, "season", 0, 0, axis_index_groups=members, tiled=True)


def on_device(
    demand,
    avail,
    asset_bus,
    run_cost,
    build_cost,
    line_from,
    line_to,
    link_count,
    line_limit,
    efficiency,
    power_limit,
    energy_limit,
    season_link,
    dispatch,
    capacity,
    flow,
    charge,
    soc,
    price,
    scarcity,
    soc_dual,
):
    season = lax.axis_index("season").astype(I32).reshape(1)
    pair = lambda v: v.reshape(2, 128)
    short = lambda v: v.reshape(1, BUS)
    link = short(season_link)
    lines = ((SLOT, HOUR), F32)
    lines_b = ((SLOT, HOUR), BF16)
    buses = ((BUS, HOUR), F32)
    picks = ((SLOT, BUS), BF16)
    packed = ((REGIONS * ROWS_EACH, HOUR), BF16)
    seasons = ((SEASONS, 8, 128), F32)
    consts = (
        avail,
        pair(asset_bus),
        pair(run_cost),
        pair(build_cost),
        short(efficiency),
        short(power_limit),
        short(energy_limit),
        link,
    )
    sent1, flow0, near0, cap, leave = call(
        lines_out,
        [packed, lines, lines_b, lines, picks],
        flow,
        price,
        pair(line_from),
        pair(line_to),
        pair(line_limit),
        link_count,
        turn=True,
        fetched=True,
    )
    got1 = region_exchange(sent1, 2, 5)
    (rows1,) = call(season_out, [seasons], avail, scarcity, soc, soc_dual, link, turn=True, fetched=True)
    season1 = season_exchange(rows1)
    sent2, came_far0, arrive, came_cap = call(
        ends_in, [lines_b, lines_b, picks, lines], got1, price
    )
    got2 = region_exchange(sent2, LINK_CAP, 1)
    disp1, build1, disch1, level1, scarce1, sdual1, came1, balance, rows2, moves = call(
        first_local,
        [lines, ((2, 128), F32), buses, buses, lines, buses, lines, buses, ((8, 128), F32), ((8, 128), F32)],
        season,
        *consts,
        dispatch,
        pair(capacity),
        charge,
        soc,
        scarcity,
        soc_dual,
        price,
        season1,
        got1,
        arrive,
        came_cap,
        came_far0,
        scalar=True,
        turn=True,
    )
    price1, flow1, came_far1, sent3 = call(
        price_step,
        [buses, lines, lines_b, packed],
        flow0,
        near0,
        cap,
        leave,
        arrive,
        got2,
        demand,
        price,
        balance,
        moves,
    )
    got3 = region_exchange(sent3, 2, 5)
    (rows3,) = call(moves_out, [seasons], got3, rows2)
    season2 = season_exchange(rows3)
    disp2, build2, flow2, disch2, level2, price2, scarce2, sdual2 = call(
        second_step,
        [lines, ((2, 128), F32), lines, buses, buses, buses, lines, buses],
        season,
        *consts,
        disp1,
        build1,
        disch1,
        level1,
        scarce1,
        sdual1,
        price1,
        season2,
        got3,
        arrive,
        came_cap,
        came_far1,
        came1,
        demand,
        flow1,
        cap,
        leave,
        scalar=True,
        turn=True,
    )
    return (disp2, build2.reshape(capacity.shape), flow2, disch2, level2, price2, scarce2, sdual2)


def solution(mesh):
    both = P("region", "season")
    rows = P("region")
    in_specs = (
        both,
        both,
        rows,
        rows,
        rows,
        rows,
        rows,
        P("region", None),
        rows,
        rows,
        rows,
        rows,
        both,
        both,
        rows,
        both,
        both,
        both,
        both,
        both,
        both,
    )
    out_specs = (both, rows, both, both, both, both, both, both)
    return jax.shard_map(
        on_device, mesh=mesh, in_specs=in_specs, out_specs=out_specs, check_vma=False
    )
```
